32 devices in a mesh: rep: 8 (over z, y), shard: 4 (over x, core).
Axes of the slice: x: 2, y: 2, z: 4, core: 2. Of those that a mesh axis runs over, the one named last changes fastest.
Arguments:
- q_grad: float32 [8, 1152, 1152], P('rep', None, 'shard'), may hold values from -6 to 6
- o_grad: float32 [8, 1152, 1152], P('rep', None, 'shard'), may hold values from -6 to 6
- q_error: float32 [8, 1152, 1152], P('rep', None, 'shard'), may hold values from -4 to 4
- o_error: float32 [8, 1152, 1152], P('rep', None, 'shard'), may hold values from -4 to 4
- q_basis: float32 [1152, 32], P('shard'), may hold values from -6 to 6
- o_basis: float32 [1152, 32], P('shard'), may hold values from -6 to 6
- q_moment: float32 [1152, 1152], P('rep', 'shard'), may hold values from -6 to 6
- o_moment: float32 [1152, 1152], P('rep', 'shard'), may hold values from -6 to 6
- q_weight: float32 [1152, 1152], P('rep', 'shard'), may hold values from -0.1875 to 0.1875
- o_weight: float32 [1152, 1152], P('rep', 'shard'), may hold values from -0.1875 to 0.1875
- norm_grads: float32 [8, 4, 2304], P('rep', 'shard'), may hold values from -5 to 5
- norm_moment: float32 [2304], P(('rep', 'shard')), may hold values from -6 to 6
- norm_weight: float32 [2304], P(('rep', 'shard')), may hold values from 0.5 to 1.5
Outputs:
- q_weight_new: float32 [1152, 1152], P(None, 'shard')
- o_weight_new: float32 [1152, 1152], P(None, 'shard')
- q_moment_new: float32 [1152, 1152], P('rep', 'shard')
- o_moment_new: float32 [1152, 1152], P('rep', 'shard')
- q_error_new: float32 [8, 1152, 1152], P('rep', None, 'shard')
- o_error_new: float32 [8, 1152, 1152], P('rep', None, 'shard')
- norm_weight_new: float32 [2304], replicated
- norm_moment_new: float32 [2304], P(('rep', 'shard'))
The draws below stay inside these ranges and needn't reach their ends.
All inputs are finite; a program needn't handle non-finite values.
Results may differ from the reference program's by a relative error of at most 0.0003.
Values sent between devices are 32-bit elements; how exact they have to be, the bound alone decides.
No kernel may reach another device: no remote copies, remote signals or barrier semaphores. Data moves between devices by JAX's collectives and lax.ppermute only.
A program may use at most 64 MiB of HBM per device.

```python
import jax
import jax.numpy as jnp
from jax import lax

D = 1152
RANK = 32
ROUNDS = 2
FLAT = 2304
N_REP = 8
N_SHARD = 4


def spiked(result, stream_key, source, target, parts, factor):
    def block_of(position):
        return (jnp.arange(result.shape[position]) // (result.shape[position] // parts)).reshape((-1,) + (1,) * (result.ndim - 1 - position))

    first = jax.random.permutation(stream_key, parts)[block_of(target)]
    other_side = (block_of(target) + parts // 2) % parts
    return jnp.where((block_of(source) == first) | (block_of(source) == other_side), factor * result, result)


def block_levels(stream_key, shape, cuts, smallest, high):
    factor_of, own = 1.0, jax.random.fold_in(stream_key, 6)
    for position, shards_of in cuts:
        heights = jnp.exp(jax.random.uniform(jax.random.fold_in(own, position), (shards_of,), jnp.float32, smallest / len(cuts), high / len(cuts)))
        factor_of = factor_of * jnp.repeat(heights, shape[position] // shards_of).reshape([-1 if axis == position else 1 for axis in range(len(shape))])
    return factor_of


def scatter_about(rng, shape, scale, most, split=(), held_as=jnp.bfloat16):
    result = jax.random.normal(rng, shape, jnp.float32) * scale
    if len(split) > 0:
        result = block_levels(rng, shape, split, -0.22, 0.18) * result
    return jnp.clip(result, min=-most, max=most).astype(held_as)


def gaussian_with(key, extent, spread, reach, cuts, heavy, dtype=jnp.bfloat16):
    drawn = spread * jax.random.normal(key, extent, jnp.float32)
    if cuts:
        drawn = drawn * block_levels(key, extent, cuts, -0.22, 0.18)
    return jnp.clip(spiked(drawn, jax.random.fold_in(key, 3), *heavy), -reach, reach).astype(dtype)


def setup_inputs(seed: int = 0) -> dict:
    keys = jax.random.split(jax.random.key(seed), 14)
    q_grad = gaussian_with(keys[0], (N_REP, D, D), 1.0, 6.0, ((0, 8), (2, 4)), (0, 1, 8, 2.0), jnp.float32)
    o_grad = gaussian_with(keys[1], (N_REP, D, D), 1.0, 6.0, ((0, 8), (2, 4)), (0, 1, 8, 2.0), jnp.float32)
    q_error = scatter_about(keys[2], (N_REP, D, D), 0.5, 4.0, ((0, 8), (2, 4)), jnp.float32)
    o_error = scatter_about(keys[3], (N_REP, D, D), 0.5, 4.0, ((0, 8), (2, 4)), jnp.float32)
    q_basis = scatter_about(keys[4], (D, RANK), 1.0, 6.0, ((0, 4),), jnp.float32)
    o_basis = scatter_about(keys[5], (D, RANK), 1.0, 6.0, ((0, 4),), jnp.float32)
    q_moment = scatter_about(keys[6], (D, D), 1.0, 6.0, ((0, 8), (1, 4)), jnp.float32)
    o_moment = scatter_about(keys[7], (D, D), 1.0, 6.0, ((0, 8), (1, 4)), jnp.float32)
    q_weight = scatter_about(keys[8], (D, D), D ** -0.5, 0.1875, ((0, 8), (1, 4)), jnp.float32)
    o_weight = scatter_about(keys[9], (D, D), D ** -0.5, 0.1875, ((0, 8), (1, 4)), jnp.float32)
    norm_grads = gaussian_with(keys[10], (N_REP, N_SHARD, FLAT), 0.25, 5.0, ((0, 8), (1, 4)), (0, 2, 8, 2.0), jnp.float32)
    norm_moment = scatter_about(keys[11], (FLAT,), 1.0, 6.0, ((0, 32),), jnp.float32)
    norm_weight = jnp.clip(1.0 + 0.1 * jax.random.normal(keys[12], (FLAT,), jnp.float32), 0.5, 1.5)
    return dict(q_grad=q_grad, o_grad=o_grad, q_error=q_error, o_error=o_error, q_basis=q_basis, o_basis=o_basis, q_moment=q_moment, o_moment=o_moment, q_weight=q_weight, o_weight=o_weight, norm_grads=norm_grads, norm_moment=norm_moment, norm_weight=norm_weight)


highest = lax.Precision.HIGHEST
decay_rate = 0.9
step_size = 0.1

def unwhiten(lower, factor):
    return jax.scipy.linalg.solve_triangular(lower, factor.T, lower=True).T

def compress(grad, error, basis):
    corrected = grad + error
    total = jnp.sum(corrected, axis=0)
    normal = None
    for sweep in range(ROUNDS):
        left = jnp.dot(total, basis, precision=highest)
        gram = jnp.dot(left.T, left, precision=highest)
        lower = jnp.linalg.cholesky(gram)
        normal = unwhiten(lower, left)
        basis = jnp.dot(total.T, normal, precision=highest)
    decoded = jnp.dot(normal, basis.T, precision=highest)
    return (corrected - decoded[None], decoded)

def reference(q_grad, o_grad, q_error, o_error, q_basis, o_basis, q_moment, o_moment, q_weight, o_weight, norm_grads, norm_moment, norm_weight):
    q_error_new, q_decoded = compress(q_grad, q_error, q_basis)
    o_error_new, o_decoded = compress(o_grad, o_error, o_basis)
    q_moment_new = decay_rate * q_moment + q_decoded
    o_moment_new = decay_rate * o_moment + o_decoded
    q_weight_new = q_weight - step_size * q_moment_new
    o_weight_new = o_weight - step_size * o_moment_new
    norm_sum = jnp.sum(norm_grads, axis=(0, 1))
    norm_moment_new = decay_rate * norm_moment + norm_sum
    norm_weight_new = norm_weight - step_size * norm_moment_new
    return (q_weight_new, o_weight_new, q_moment_new, o_moment_new, q_error_new, o_error_new, norm_weight_new, norm_moment_new)
```

```python
import jax
import jax.numpy as jnp
from jax import lax
from jax.sharding import PartitionSpec as P

ROUNDS = 2
AXES = ("rep", "shard")

highest = lax.Precision.HIGHEST
decay_rate = 0.9
step_size = 0.1


def product(left, right):
    return jnp.dot(left, right, precision=highest)


def halves(count):
    masks = []
    mask = 1
    while mask < count:
        masks.append(mask)
        mask *= 2
    return masks


def swap(block, axis, mask, count):
    pairs = [(i, i ^ mask) for i in range(count)]
    return lax.ppermute(block, axis, pairs)


def sum_over(block, axis, count):
    for mask in halves(count):
        block = block + swap(block, axis, mask, count)
    return block


def sum_over_all(part, n_rep, n_shard):
    place = lax.axis_index("shard")
    bits = [(mask, (place & mask) != 0) for mask in halves(n_shard)]
    for mask, high in bits:
        half = part.shape[0] // 2
        low_rows, high_rows = part[:half], part[half:]
        keep = jnp.where(high, high_rows, low_rows)
        give = jnp.where(high, low_rows, high_rows)
        part = keep + swap(give, "shard", mask, n_shard)
    part = sum_over(part, "rep", n_rep)
    for mask, high in reversed(bits):
        other = swap(part, "shard", mask, n_shard)
        part = jnp.concatenate([jnp.where(high, other, part), jnp.where(high, part, other)], axis=0)
    return part


def per_device(n_rep, n_shard, q_grad, o_grad, q_error, o_error, q_basis, o_basis, q_moment, o_moment, q_weight, o_weight, norm_grads, norm_moment, norm_weight):
    rank = q_basis.shape[1]
    size = q_grad.shape[1]
    row_count = q_moment.shape[0]
    flat = norm_grads.shape[-1]
    share = norm_moment.shape[0]
    device = lax.axis_index("rep") * n_shard + lax.axis_index("shard")

    base = jnp.stack([q_weight - (step_size * decay_rate) * q_moment, o_weight - (step_size * decay_rate) * o_moment])
    bases = lax.all_gather(base, "rep", axis=0, tiled=False)

    corr_q = q_grad[0] + q_error[0]
    corr_o = o_grad[0] + o_error[0]

    grads = norm_grads.reshape(flat)
    placed = lax.dynamic_update_slice(-step_size * grads, lax.dynamic_slice(-step_size * grads, (device * share,), (share,)) + (norm_weight - (step_size * decay_rate) * norm_moment), (device * share,))
    lanes = 128
    extra = jnp.concatenate([grads.reshape(-1, lanes), placed.reshape(-1, lanes)], axis=0)
    extra_rows = extra.shape[0]
    extra = jnp.pad(extra, ((0, 2 * rank - extra_rows), (0, 0)))

    basis_q, basis_o = q_basis.T, o_basis.T
    for sweep in range(ROUNDS):
        part_q = lax.dot_general(basis_q, corr_q, (((1,), (1,)), ((), ())), precision=highest)
        part_o = lax.dot_general(basis_o, corr_o, (((1,), (1,)), ((), ())), precision=highest)
        part = jnp.concatenate([part_q, part_o], axis=0)
        if sweep == ROUNDS - 1:
            part = jnp.concatenate([part, extra], axis=1)
        left = sum_over_all(part, n_rep, n_shard)
        if sweep == ROUNDS - 1:
            extra_sum = left[:extra_rows, size:]
            left = left[:, :size]
        left_q, left_o = left[:rank], left[rank:]
        right = jnp.concatenate([product(left_q, corr_q), product(left_o, corr_o)], axis=0)
        right = sum_over(right, "rep", n_rep)
        both = left.reshape(2, rank, size)
        gram = jnp.einsum("pij,pkj->pik", both, both, precision=highest)
        lower = jnp.linalg.cholesky(gram)
        identity = jnp.broadcast_to(jnp.eye(rank, dtype=jnp.float32), (2, rank, rank))
        inverse = jax.scipy.linalg.solve_triangular(lower, identity, lower=True)
        basis_q = product(inverse[0], right[:rank])
        basis_o = product(inverse[1], right[rank:])
        if sweep == ROUNDS - 1:
            normal_q = product(inverse[0], left_q)
            normal_o = product(inverse[1], left_o)
    decoded_q = lax.dot_general(normal_q, basis_q, (((0,), (0,)), ((), ())), precision=highest)
    decoded_o = lax.dot_general(normal_o, basis_o, (((0,), (0,)), ((), ())), precision=highest)
    q_error_new = (corr_q - decoded_q)[None]
    o_error_new = (corr_o - decoded_o)[None]
    start = lax.axis_index("rep") * row_count
    slice_q = lax.dynamic_slice_in_dim(decoded_q, start, row_count, 0)
    slice_o = lax.dynamic_slice_in_dim(decoded_o, start, row_count, 0)
    q_moment_new = decay_rate * q_moment + slice_q
    o_moment_new = decay_rate * o_moment + slice_o
    q_weight_new = bases[:, 0].reshape(size, -1) - step_size * decoded_q
    o_weight_new = bases[:, 1].reshape(size, -1) - step_size * decoded_o
    half = extra_rows // 2
    norm_sum = extra_sum[:half].reshape(flat)
    norm_weight_new = extra_sum[half:].reshape(flat)
    norm_moment_new = decay_rate * norm_moment + lax.dynamic_slice(norm_sum, (device * share,), (share,))
    return (
        q_weight_new,
        o_weight_new,
        q_moment_new,
        o_moment_new,
        q_error_new,
        o_error_new,
        norm_weight_new,
        norm_moment_new,
    )


def solution(mesh):
    n_rep, n_shard = mesh.shape["rep"], mesh.shape["shard"]

    def whole(*arrays):
        return per_device(n_rep, n_shard, *arrays)

    return jax.shard_map(
        whole,
        mesh=mesh,
        in_specs=(
            P("rep", None, "shard"),
            P("rep", None, "shard"),
            P("rep", None, "shard"),
            P("rep", None, "shard"),
            P("shard", None),
            P("shard", None),
            P("rep", "shard"),
            P("rep", "shard"),
            P("rep", "shard"),
            P("rep", "shard"),
            P("rep", "shard", None),
            P(("rep", "shard")),
            P(("rep", "shard")),
        ),
        out_specs=(
            P(None, "shard"),
            P(None, "shard"),
            P("rep", "shard"),
            P("rep", "shard"),
            P("rep", None, "shard"),
            P("rep", None, "shard"),
            P(),
            P(("rep", "shard")),
        ),
        check_vma=False,
    )
```

```python
import functools

import jax
import jax.numpy as jnp
from jax import lax
from jax.experimental import pallas as pl
from jax.experimental.pallas import tpu as pltpu
from jax.sharding import PartitionSpec as P

ROUNDS = 2
GROUP = 8

highest = lax.Precision.HIGHEST
decay_rate = 0.9
step_size = 0.1
NT = (((1,), (1,)), ((), ()))
TN = (((0,), (0,)), ((), ()))


def product(left, right):
    return jnp.dot(left, right, precision=highest)


def halves(count):
    masks = []
    mask = 1
    while mask < count:
        masks.append(mask)
        mask *= 2
    return masks


def swap(block, axis, mask, count):
    pairs = [(i, i ^ mask) for i in range(count)]
    return lax.ppermute(block, axis, pairs)


def sum_over(block, count, gather, stage):
    for mask in halves(count):
        block = gather.before(block, stage, mask)
        block = block + swap(block, "rep", mask, count)
        block = gather.after(block, stage, mask)
    return block


def sum_over_all(part, n_rep, n_shard, gather, stage):
    place = lax.axis_index("shard")
    bits = [(mask, (place & mask) != 0) for mask in halves(n_shard)]
    for mask, high in bits:
        half = part.shape[0] // 2
        low_rows, high_rows = part[:half], part[half:]
        keep = jnp.where(high, high_rows, low_rows)
        give = jnp.where(high, low_rows, high_rows)
        part = keep + swap(give, "shard", mask, n_shard)
    part = sum_over(part, n_rep, gather, stage)
    for mask, high in reversed(bits):
        other = swap(part, "shard", mask, n_shard)
        part = jnp.concatenate([jnp.where(high, other, part), jnp.where(high, part, other)], axis=0)
    return part


class Gather:
    def __init__(self, own, count):
        self.count = count
        self.blocks = [own]
        self.turned = []
        self.paired = count == 8
        self.waiting = {}
        if self.paired:
            self.near = swap(own, "rep", 2, count)

    def before(self, value, stage, mask):
        if not self.paired:
            return value
        if (stage, mask) == (0, 2):
            value, self.near = lax.optimization_barrier((value, self.near))
        if (stage, mask) == (1, 1):
            value, first = lax.optimization_barrier((value, self.turned[0]))
            self.turned[0] = first
        if (stage, mask) == (1, 2):
            value, self.far = lax.optimization_barrier((value, self.far))
        if (stage, mask) == (2, 2):
            value, self.last = lax.optimization_barrier((value, self.last))
        if (stage, mask) == (3, 1):
            value, second = lax.optimization_barrier((value, self.turned[1]))
            self.turned[1] = second
        return value

    def after(self, value, stage, mask):
        if not self.paired:
            return value
        if (stage, mask) == (0, 1):
            value, pair = lax.optimization_barrier((value, jnp.concatenate([self.blocks[0], self.near])))
            self.pairs = [pair]
            self.turned.append(swap(pair, "rep", 1, self.count))
        if (stage, mask) == (0, 4):
            value, own = lax.optimization_barrier((value, self.blocks[0]))
            self.far = swap(own, "rep", 4, self.count)
        if (stage, mask) == (1, 4):
            value, near = lax.optimization_barrier((value, self.near))
            self.last = swap(near, "rep", 4, self.count)
        if (stage, mask) == (2, 1):
            value, pair = lax.optimization_barrier((value, jnp.concatenate([self.far, self.last])))
            self.pairs.append(pair)
            self.turned.append(swap(pair, "rep", 1, self.count))
        return value


def eliminate(gram_q, gram_o, rank):
    width = 4 * rank
    lane = lax.broadcasted_iota(jnp.int32, (rank, width), 1)
    row = lax.broadcasted_iota(jnp.int32, (rank, width), 0)
    square = (rank, rank)
    eye = (lax.broadcasted_iota(jnp.int32, square, 0) == lax.broadcasted_iota(jnp.int32, square, 1)).astype(jnp.float32)
    work = jnp.concatenate([gram_q, eye, gram_o, eye], axis=1)
    first = lane < 2 * rank
    scale = jnp.ones((rank, width), jnp.float32)
    for base in range(0, rank, GROUP):
        columns = []
        for k in range(base, base + GROUP):
            of_q = jnp.broadcast_to(work[:, k : k + 1], (rank, width))
            of_o = jnp.broadcast_to(work[:, 2 * rank + k : 2 * rank + k + 1], (rank, width))
            columns.append(jnp.where(first, of_q, of_o))
        for j in range(GROUP):
            k = base + j
            pivot = columns[j][k : k + 1]
            factor = jnp.where(row > k, columns[j] * (1.0 / pivot), 0.0)
            scale = jnp.where(row == k, pivot, scale)
            for i in range(j + 1, GROUP):
                columns[i] = columns[i] - factor * columns[i][k : k + 1]
            work = work - factor * work[k : k + 1]
    work = work * lax.rsqrt(scale)
    return work[:, rank : 2 * rank], work[:, 3 * rank :]


def inverse_kernel(rank, left_ref, inverse_ref, *normal_ref):
    left_q, left_o = left_ref[:rank, :], left_ref[rank:, :]
    gram_q = lax.dot_general(left_q, left_q, NT, precision=highest, preferred_element_type=jnp.float32)
    gram_o = lax.dot_general(left_o, left_o, NT, precision=highest, preferred_element_type=jnp.float32)
    inverse_q, inverse_o = eliminate(gram_q, gram_o, rank)
    inverse_ref[0] = inverse_q
    inverse_ref[1] = inverse_o
    if normal_ref:
        normal_q = jnp.dot(inverse_q, left_q, precision=highest, preferred_element_type=jnp.float32)
        normal_o = jnp.dot(inverse_o, left_o, precision=highest, preferred_element_type=jnp.float32)
        normal_ref[0][...] = jnp.concatenate([normal_q, normal_o], axis=0).T


def inverse_of(left, with_normal):
    rank, size = left.shape[0] // 2, left.shape[1]
    shapes = [jax.ShapeDtypeStruct((2, rank, rank), jnp.float32)]
    if with_normal:
        shapes.append(jax.ShapeDtypeStruct((size, 2 * rank), jnp.float32))
    cost = pl.CostEstimate(flops=20_000_000, bytes_accessed=left.size * 4, transcendentals=0)
    return pl.pallas_call(functools.partial(inverse_kernel, rank), out_shape=shapes, cost_estimate=cost, name="inverse")(left)


def finish_kernel(count, rank, place_ref, corr_q, corr_o, normal, inverse, right, moment_q, moment_o, *refs):
    pairs, outs, z_ref = refs[: count // 2], refs[count // 2 : -1], refs[-1]
    weight_q, weight_o, new_moment_q, new_moment_o, error_q, error_o = outs
    step = pl.program_id(0)

    @pl.when(step == 0)
    def _():
        z_ref[0] = jnp.dot(inverse[0], right[:rank, :], precision=highest, preferred_element_type=jnp.float32)
        z_ref[1] = jnp.dot(inverse[1], right[rank:, :], precision=highest, preferred_element_type=jnp.float32)

    normal_q, normal_o = normal[:, :rank], normal[:, rank:]
    decoded_q = jnp.dot(normal_q, z_ref[0], precision=highest, preferred_element_type=jnp.float32)
    decoded_o = jnp.dot(normal_o, z_ref[1], precision=highest, preferred_element_type=jnp.float32)
    error_q[0] = corr_q[...] - decoded_q
    error_o[0] = corr_o[...] - decoded_o
    for j, pair in enumerate(pairs):

        @pl.when(step // 2 == j)
        def _(pair=pair):
            weight_q[...] = pair[0] - step_size * decoded_q
            weight_o[...] = pair[1] - step_size * decoded_o

    @pl.when(step == 0)
    def _():
        new_moment_q[...] = decay_rate * moment_q[...] + decoded_q
        new_moment_o[...] = decay_rate * moment_o[...] + decoded_o


def finish(count, corr_q, corr_o, normal, inverse, right, moment_q, moment_o, pairs):
    size, width = corr_q.shape
    rows = moment_q.shape[0]
    rank = inverse.shape[1]
    place = lax.axis_index("rep").astype(jnp.int32).reshape(1)

    def block(k, place):
        return place[0] ^ ((2 * k) % count + (2 * k) // count)

    def by_rows(columns):
        return pl.BlockSpec((rows, columns), lambda k, place: (block(k, place), 0))

    def whole(shape):
        return pl.BlockSpec(shape, lambda k, place: (0,) * len(shape))

    def pair_spec(j):
        return pl.BlockSpec((2, rows, width), lambda k, place: (jnp.clip(k - 2 * j, 0, 1), 0, 0))

    error = pl.BlockSpec((1, rows, width), lambda k, place: (0, block(k, place), 0))
    f32 = functools.partial(jax.ShapeDtypeStruct, dtype=jnp.float32)
    return pl.pallas_call(
        functools.partial(finish_kernel, count, rank),
        grid_spec=pltpu.PrefetchScalarGridSpec(
            num_scalar_prefetch=1,
            grid=(count,),
            in_specs=[by_rows(width), by_rows(width), by_rows(2 * rank), whole(inverse.shape), whole(right.shape), whole(moment_q.shape), whole(moment_o.shape)]
            + [pair_spec(j) for j in range(count // 2)],
            out_specs=[by_rows(width), by_rows(width), whole(moment_q.shape), whole(moment_o.shape), error, error],
            scratch_shapes=[pltpu.VMEM((2, rank, width), jnp.float32)],
        ),
        out_shape=[f32((size, width)), f32((size, width)), f32((rows, width)), f32((rows, width)), f32((1, size, width)), f32((1, size, width))],
        compiler_params=pltpu.CompilerParams(vmem_limit_bytes=32 * 1024 * 1024),
        name="finish",
    )(place, corr_q, corr_o, normal, inverse, right, moment_q, moment_o, *pairs)


def finish_plain(corr_q, corr_o, normal, inverse, right, moment_q, moment_o, base):
    size = corr_q.shape[0]
    rows = moment_q.shape[0]
    rank = inverse.shape[1]
    decoded_q = product(normal[:, :rank], product(inverse[0], right[:rank]))
    decoded_o = product(normal[:, rank:], product(inverse[1], right[rank:]))
    start = lax.axis_index("rep") * rows
    moment_q = decay_rate * moment_q + lax.dynamic_slice_in_dim(decoded_q, start, rows, 0)
    moment_o = decay_rate * moment_o + lax.dynamic_slice_in_dim(decoded_o, start, rows, 0)
    bases = lax.all_gather(base, "rep", axis=1, tiled=True)
    weight_q, weight_o = bases[0] - step_size * decoded_q, bases[1] - step_size * decoded_o
    return weight_q, weight_o, moment_q, moment_o, (corr_q - decoded_q)[None], (corr_o - decoded_o)[None]


def per_device(n_rep, n_shard, q_grad, o_grad, q_error, o_error, q_basis, o_basis, q_moment, o_moment, q_weight, o_weight, norm_grads, norm_moment, norm_weight):
    rank = q_basis.shape[1]
    size = q_grad.shape[1]
    flat = norm_grads.shape[-1]
    share = norm_moment.shape[0]
    device = lax.axis_index("rep") * n_shard + lax.axis_index("shard")

    base = jnp.stack([q_weight - (step_size * decay_rate) * q_moment, o_weight - (step_size * decay_rate) * o_moment])
    gather = Gather(base, n_rep)

    corr_q = q_grad[0] + q_error[0]
    corr_o = o_grad[0] + o_error[0]

    grads = norm_grads.reshape(flat)
    placed = lax.dynamic_update_slice(-step_size * grads, lax.dynamic_slice(-step_size * grads, (device * share,), (share,)) + (norm_weight - (step_size * decay_rate) * norm_moment), (device * share,))
    lanes = 128
    extra = jnp.concatenate([grads.reshape(-1, lanes), placed.reshape(-1, lanes)], axis=0)
    extra_rows = extra.shape[0]
    extra = jnp.pad(extra, ((0, 2 * rank - extra_rows), (0, 0)))

    basis_q, basis_o = q_basis.T, o_basis.T
    for sweep in range(ROUNDS):
        part_q = lax.dot_general(basis_q, corr_q, NT, precision=highest)
        part_o = lax.dot_general(basis_o, corr_o, NT, precision=highest)
        part = jnp.concatenate([part_q, part_o], axis=0)
        if sweep == ROUNDS - 1:
            part = jnp.concatenate([part, extra], axis=1)
        left = sum_over_all(part, n_rep, n_shard, gather, 2 * sweep)
        if sweep == ROUNDS - 1:
            extra_sum = left[:extra_rows, size:]
            left = left[:, :size]
        right = jnp.concatenate([product(left[:rank], corr_q), product(left[rank:], corr_o)], axis=0)
        right = sum_over(right, n_rep, gather, 2 * sweep + 1)
        if sweep < ROUNDS - 1:
            (inverse,) = inverse_of(left, False)
            basis_q = product(inverse[0], right[:rank])
            basis_o = product(inverse[1], right[rank:])
    inverse, normal = inverse_of(left, True)
    if gather.paired:
        pairs = [pair.reshape((4,) + pair.shape[1:]) for pair in (gather.pairs + gather.turned)]
        outs = finish(n_rep, corr_q, corr_o, normal, inverse, right, q_moment, o_moment, pairs)
    else:
        outs = finish_plain(corr_q, corr_o, normal, inverse, right, q_moment, o_moment, base)
    q_weight_new, o_weight_new, q_moment_new, o_moment_new, q_error_new, o_error_new = outs
    half = extra_rows // 2
    norm_sum = extra_sum[:half].reshape(flat)
    norm_weight_new = extra_sum[half:].reshape(flat)
    norm_moment_new = decay_rate * norm_moment + lax.dynamic_slice(norm_sum, (device * share,), (share,))
    return (
        q_weight_new,
        o_weight_new,
        q_moment_new,
        o_moment_new,
        q_error_new,
        o_error_new,
        norm_weight_new,
        norm_moment_new,
    )


def solution(mesh):
    n_rep, n_shard = mesh.shape["rep"], mesh.shape["shard"]

    def whole(*arrays):
        return per_device(n_rep, n_shard, *arrays)

    return jax.shard_map(
        whole,
        mesh=mesh,
        in_specs=(
            P("rep", None, "shard"),
            P("rep", None, "shard"),
            P("rep", None, "shard"),
            P("rep", None, "shard"),
            P("shard", None),
            P("shard", None),
            P("rep", "shard"),
            P("rep", "shard"),
            P("rep", "shard"),
            P("rep", "shard"),
            P("rep", "shard", None),
            P(("rep", "shard")),
            P(("rep", "shard")),
        ),
        out_specs=(
            P(None, "shard"),
            P(None, "shard"),
            P("rep", "shard"),
            P("rep", "shard"),
            P("rep", None, "shard"),
            P("rep", None, "shard"),
            P(),
            P(("rep", "shard")),
        ),
        check_vma=False,
    )
```

```python
import functools

import jax
import jax.numpy as jnp
from jax import lax
from jax.experimental import pallas as pl
from jax.experimental.pallas import tpu as pltpu
from jax.sharding import PartitionSpec as P

ROUNDS = 2
GROUP = 8
LANES = 128

highest = lax.Precision.HIGHEST
decay_rate = 0.9
step_size = 0.1
f32 = jnp.float32
bf16 = jnp.bfloat16
NN = (((1,), (0,)), ((), ()))
NT = (((1,), (1,)), ((), ()))
TN = (((0,), (0,)), ((), ()))
TT = (((0,), (1,)), ((), ()))

IN_HBM = pl.BlockSpec(memory_space=pltpu.HBM)
IN_VMEM = pl.BlockSpec(memory_space=pltpu.VMEM)
GRANT = pltpu.CompilerParams(vmem_limit_bytes=40 * 2**20)


def hold(space, *arrays):
    return [pltpu.with_memory_space_constraint(array, space) for array in arrays]


def exact(left, right, dims):
    return lax.dot_general(left, right, dims, precision=highest, preferred_element_type=f32)


def three(x):
    high = x.astype(bf16)
    rest = x - high.astype(f32)
    middle = rest.astype(bf16)
    low = (rest - middle.astype(f32)).astype(bf16)
    return high, middle, low


def stacked(left, right, dims):
    rows = left.shape[0]
    left_high, left_middle, left_low = three(left)
    right_high, right_middle, right_low = three(right)
    lefts = jnp.concatenate([left_high, left_middle, left_low], axis=0)
    of_high = lax.dot_general(lefts, right_high, dims, preferred_element_type=f32)
    of_middle = lax.dot_general(lefts[: 2 * rows], right_middle, dims, preferred_element_type=f32)
    of_low = lax.dot_general(left_high, right_low, dims, preferred_element_type=f32)
    small = (of_high[2 * rows :] + of_middle[rows:]) + of_low
    return of_high[:rows] + ((of_high[rows : 2 * rows] + of_middle[:rows]) + small)


def halves(count):
    masks = []
    mask = 1
    while mask < count:
        masks.append(mask)
        mask *= 2
    return masks


def swap(block, axis, mask, count):
    pairs = [(i, i ^ mask) for i in range(count)]
    return lax.ppermute(block, axis, pairs)


def sum_over(block, count, gather, stage):
    for mask in halves(count):
        block = gather.before(block, stage, mask)
        block = block + swap(block, "rep", mask, count)
        block = gather.after(block, stage, mask)
    return block


def sum_over_all(part, n_rep, n_shard, gather, stage):
    place = lax.axis_index("shard")
    bits = [(mask, (place & mask) != 0) for mask in halves(n_shard)]
    for mask, high in bits:
        half = part.shape[0] // 2
        low_rows, high_rows = part[:half], part[half:]
        keep = jnp.where(high, high_rows, low_rows)
        give = jnp.where(high, low_rows, high_rows)
        part = keep + swap(give, "shard", mask, n_shard)
    part = sum_over(part, n_rep, gather, stage)
    for mask, high in reversed(bits):
        other = swap(part, "shard", mask, n_shard)
        part = jnp.concatenate([jnp.where(high, other, part), jnp.where(high, part, other)], axis=0)
    return part


class Gather:
    PLAN = (
        ("turned", "own", 1, None, (0, 1)),
        ("near", "own", 2, None, (0, 2)),
        ("turned_near", "near", 1, (0, 2), (1, 1)),
        ("far", "own", 4, (0, 4), (1, 2)),
        ("turned_far", "far", 1, (1, 2), (2, 1)),
        ("last", "near", 4, (1, 4), (2, 2)),
        ("turned_last", "last", 1, (2, 2), (3, 1)),
    )
    PLACES = {"own": 0, "turned": 1, "near": 2, "far": 4, "last": 6, "turned_near": 3, "turned_far": 5, "turned_last": 7}

    def __init__(self, own, count):
        self.count = count
        self.blocks = {"own": own}
        self.paired = count == 8 and own.shape[0] % 8 == 0
        self.send(None)

    def send(self, point):
        if self.paired:
            for name, source, mask, after, _ in self.PLAN:
                if after == point:
                    self.blocks[name] = swap(self.blocks[source], "rep", mask, self.count)

    def before(self, value, stage, mask):
        if self.paired:
            for name, _, _, _, by in self.PLAN:
                if by == (stage, mask):
                    value, self.blocks[name] = lax.optimization_barrier((value, self.blocks[name]))
        return value

    def after(self, value, stage, mask):
        if self.paired:
            for name, source, _, after, _ in self.PLAN:
                if after == (stage, mask):
                    value, self.blocks[source] = lax.optimization_barrier((value, self.blocks[source]))
            self.send((stage, mask))
        return value

    def turned_rows(self):
        rows = None
        for names in (("own", "near"), ("turned", "turned_near"), ("far", "last"), ("turned_far",), ("turned_last",)):
            rows = insert(rows, [self.blocks[name] for name in names], [self.PLACES[name] for name in names], self.count)
        return rows


def insert_kernel(masks, place_ref, *refs):
    blocks, rows, out = refs[: len(masks)], refs[len(masks) : -1], refs[-1]
    if not rows:
        out[...] = jnp.zeros_like(out)
    height = out.shape[0]
    window = 2 * LANES
    lane = lax.broadcasted_iota(jnp.int32, (height, window), 1)
    for block, mask in zip(blocks, masks):
        count = block.shape[0]
        index = place_ref[0] ^ mask
        shift = index * (count - LANES)
        turned = jnp.concatenate([block[...].T, jnp.zeros((height, window - count), f32)], axis=1)
        turned = pltpu.roll(turned, shift, 1)
        at = pl.ds(pl.multiple_of(index * LANES, LANES), window)
        out[:, at] = jnp.where((lane >= shift) & (lane < shift + count), turned, out[:, at])


def insert(rows, blocks, masks, count):
    height, width = blocks[0].shape[1], blocks[0].shape[0] * count
    place = lax.axis_index("rep").astype(jnp.int32).reshape(1)
    old = [] if rows is None else hold(pltpu.VMEM, rows)
    return pl.pallas_call(
        functools.partial(insert_kernel, masks),
        in_specs=[pl.BlockSpec(memory_space=pltpu.SMEM)] + [IN_VMEM] * (len(blocks) + len(old)),
        out_specs=IN_VMEM,
        out_shape=pltpu.VMEM((height, width), f32),
        input_output_aliases={1 + len(blocks): 0} if old else {},
        cost_estimate=pl.CostEstimate(flops=1_000_000 * len(blocks), bytes_accessed=2_000_000 * len(blocks), transcendentals=0),
        name="insert",
    )(place, *blocks, *old)


def first_kernel(chunks, grad_q, grad_o, error_q, error_o, basis_q, basis_o, corr_q, corr_o, part, buffer, bases, sems, base_sems):
    rank, size = basis_q.shape[0], corr_q.shape[1]
    lanes = size // chunks
    base_copies = [pltpu.make_async_copy(source, bases.at[k], base_sems.at[k]) for k, source in enumerate((basis_q, basis_o))]
    copies = {}
    for copy in base_copies:
        copy.start()
    for c in range(chunks):
        at = pl.ds(c * lanes, lanes)
        for j, source in enumerate((grad_q, error_q, grad_o, error_o)):
            copies[c, j] = pltpu.make_async_copy(source.at[:, at], buffer.at[j, :, at], sems.at[c, j])
            copies[c, j].start()
    for copy in base_copies:
        copy.wait()
    for c in range(chunks):
        at = pl.ds(c * lanes, lanes)
        for k, corr in enumerate((corr_q, corr_o)):
            copies[c, 2 * k].wait()
            copies[c, 2 * k + 1].wait()
            total = buffer[2 * k, :, at] + buffer[2 * k + 1, :, at]
            corr[:, at] = total
            part[k * rank : (k + 1) * rank, at] = stacked(bases[k], total, NN)


def first(grads, errors, basis_q, basis_o):
    width, size = grads[0].shape
    rank = basis_q.shape[0]
    chunks = 3 if size % (3 * LANES) == 0 else 1
    return pl.pallas_call(
        functools.partial(first_kernel, chunks),
        in_specs=[IN_HBM] * 6,
        out_specs=[IN_VMEM] * 3,
        out_shape=[pltpu.VMEM((width, size), f32)] * 2 + [jax.ShapeDtypeStruct((2 * rank, size), f32)],
        scratch_shapes=[
            pltpu.VMEM((4, width, size), f32),
            pltpu.VMEM((2, rank, width), f32),
            pltpu.SemaphoreType.DMA((chunks, 4)),
            pltpu.SemaphoreType.DMA((2,)),
        ],
        compiler_params=GRANT,
        name="first",
    )(*hold(pltpu.HBM, *grads, *errors, basis_q, basis_o))


def right_kernel(left, corr_q, corr_o, out):
    rank = left.shape[0] // 2
    out[...] = jnp.concatenate([stacked(left[:rank, :], corr_q[...], NT), stacked(left[rank:, :], corr_o[...], NT)], axis=1)


def right_of(left, corr_q, corr_o):
    rank, width = left.shape[0] // 2, corr_q.shape[0]
    return pl.pallas_call(
        right_kernel,
        in_specs=[IN_VMEM] * 3,
        out_specs=IN_VMEM,
        out_shape=jax.ShapeDtypeStruct((rank, 2 * width), f32),
        compiler_params=GRANT,
        name="right",
    )(left, *hold(pltpu.VMEM, corr_q, corr_o))


def left_kernel(right, inverse, corr_q, corr_o, *refs):
    extra, out = refs[:-1], refs[-1]
    rank, width = right.shape[0], right.shape[1] // 2
    size = corr_q.shape[1]
    basis_q = exact(inverse[0], right[:, :width], NN)
    basis_o = exact(inverse[1], right[:, width:], NN)
    out[:rank, :size] = stacked(basis_q, corr_q[...], NN)
    out[rank:, :size] = stacked(basis_o, corr_o[...], NN)
    if extra:
        out[:, size:] = extra[0][...]


def left_of(right, inverse, corr_q, corr_o, extra):
    rank, size = right.shape[0], corr_q.shape[1]
    lanes = size + sum(array.shape[1] for array in extra)
    return pl.pallas_call(
        left_kernel,
        in_specs=[IN_VMEM] * (4 + len(extra)),
        out_specs=IN_VMEM,
        out_shape=jax.ShapeDtypeStruct((2 * rank, lanes), f32),
        compiler_params=GRANT,
        name="left",
    )(right, inverse, *hold(pltpu.VMEM, corr_q, corr_o), *extra)


def eliminate(gram_q, gram_o, rank):
    width = 4 * rank
    lane = lax.broadcasted_iota(jnp.int32, (rank, width), 1)
    row = lax.broadcasted_iota(jnp.int32, (rank, width), 0)
    square = (rank, rank)
    eye = (lax.broadcasted_iota(jnp.int32, square, 0) == lax.broadcasted_iota(jnp.int32, square, 1)).astype(f32)
    work = jnp.concatenate([gram_q, eye, gram_o, eye], axis=1)
    first_half = lane < 2 * rank
    scale = jnp.ones((rank, width), f32)
    for base in range(0, rank, GROUP):
        columns = []
        for k in range(base, base + GROUP):
            of_q = jnp.broadcast_to(work[:, k : k + 1], (rank, width))
            of_o = jnp.broadcast_to(work[:, 2 * rank + k : 2 * rank + k + 1], (rank, width))
            columns.append(jnp.where(first_half, of_q, of_o))
        for j in range(GROUP):
            k = base + j
            pivot = columns[j][k : k + 1]
            factor = jnp.where(row > k, columns[j] * (1.0 / pivot), 0.0)
            scale = jnp.where(row == k, pivot, scale)
            for i in range(j + 1, GROUP):
                columns[i] = columns[i] - factor * columns[i][k : k + 1]
            work = work - factor * work[k : k + 1]
    work = work * lax.rsqrt(scale)
    return work[:, rank : 2 * rank], work[:, 3 * rank :]


def inverse_kernel(left, out):
    rank, size = out.shape[1], left.shape[1]
    left_q, left_o = left[:rank, :], left[rank:, :]
    out[0], out[1] = eliminate(exact(left_q, left_q, NT), exact(left_o, left_o, NT), rank)


def inverse_of(left):
    rank = left.shape[0] // 2
    return pl.pallas_call(
        inverse_kernel,
        out_shape=jax.ShapeDtypeStruct((2, rank, rank), f32),
        cost_estimate=pl.CostEstimate(flops=20_000_000, bytes_accessed=left.size * 4, transcendentals=0),
        name="inverse",
    )(left)


def normal_kernel(left, inverse, normal, stack):
    rank = inverse.shape[1]
    for p in range(2):
        factor = exact(inverse[p], left[p * rank : (p + 1) * rank, :], NN)
        normal[p * rank : (p + 1) * rank, :] = factor
        high, middle, low = three(factor)
        stack[p] = jnp.concatenate([high, middle, low, high, middle, high], axis=0)


def normal_of(left, inverse):
    rank, size = inverse.shape[1], left.shape[1]
    return pl.pallas_call(
        normal_kernel,
        out_shape=[jax.ShapeDtypeStruct((2 * rank, size), f32), jax.ShapeDtypeStruct((2, 6 * rank, size), bf16)],
        cost_estimate=pl.CostEstimate(flops=20_000_000, bytes_accessed=left.size * 4, transcendentals=0),
        name="normal",
    )(left, inverse)


def finish_kernel(chunks, corr_q, corr_o, rows, stack, inverse, right, own, moment_q, moment_o, *refs):
    outs, buffer, new_moments, sems, moment_sems = refs[:6], refs[6], refs[7], refs[8], refs[9]
    rank, width = inverse.shape[1], moment_q.shape[1]
    height = width // chunks
    copies = []
    for p, corr in enumerate((corr_q, corr_o)):
        factor = right[:, p * width : (p + 1) * width]
        high, middle, low = three(exact(factor, inverse[p], TT))
        lefts = jnp.concatenate([high, high, high, middle, middle, low], axis=1)
        for c in range(chunks):
            at = pl.ds(c * height, height)
            decoded = lax.dot_general(lefts[c * height : (c + 1) * height], stack[p], NN, preferred_element_type=f32)
            buffer[p, at, :] = rows[pl.ds(p * width + c * height, height), :] - step_size * decoded
            buffer[2 + p, at, :] = corr[at, :] - decoded
            for k in (p, 2 + p):
                copies.append(pltpu.make_async_copy(buffer.at[k, at, :], outs[k].at[at, :], sems.at[k, c]))
                copies[-1].start()
    for p, moment in enumerate((moment_q, moment_o)):
        factor = right[:, p * width : (p + 1) * width]
        basis = exact(inverse[p], factor, NN)
        new_moments[p] = decay_rate * moment[...] + exact(own[p * rank : (p + 1) * rank, :], basis, TN)
        copies.append(pltpu.make_async_copy(new_moments.at[p], outs[4 + p], moment_sems.at[p]))
        copies[-1].start()
    for copy in copies:
        copy.wait()


def finish(corr_q, corr_o, rows, stack, inverse, right, own, moment_q, moment_o):
    width, size = corr_q.shape
    chunks = 3
    return pl.pallas_call(
        functools.partial(finish_kernel, chunks),
        in_specs=[IN_VMEM] * 9,
        out_specs=[IN_HBM] * 6,
        out_shape=[pltpu.HBM((width, size), f32)] * 4 + [pltpu.HBM(moment_q.shape, f32)] * 2,
        scratch_shapes=[
            pltpu.VMEM((4, width, size), f32),
            pltpu.VMEM((2,) + moment_q.shape, f32),
            pltpu.SemaphoreType.DMA((4, chunks)),
            pltpu.SemaphoreType.DMA((2,)),
        ],
        compiler_params=GRANT,
        name="finish",
    )(*hold(pltpu.VMEM, corr_q, corr_o, rows), stack, inverse, right, own, moment_q, moment_o)


def finish_plain(corr_q, corr_o, base, normal, inverse, right, moment_q, moment_o):
    rank, width = inverse.shape[1], moment_q.shape[1]
    rows = moment_q.shape[0]
    start = lax.axis_index("rep") * rows
    bases = lax.all_gather(base, "rep", axis=0, tiled=True)
    weights, moments, errors = [], [], []
    for p, (corr, moment) in enumerate(((corr_q, moment_q), (corr_o, moment_o))):
        at = slice(p * width, (p + 1) * width)
        basis = exact(inverse[p], right[:, at], NN)
        decoded = exact(basis, normal[p * rank : (p + 1) * rank], TN)
        weights.append(bases[:, at].T - step_size * decoded)
        moments.append(decay_rate * moment + lax.dynamic_slice_in_dim(decoded, start, rows, 1).T)
        errors.append(corr - decoded)
    return weights + errors + moments


def per_device(n_rep, n_shard, q_grad, o_grad, q_error, o_error, q_basis, o_basis, q_moment, o_moment, q_weight, o_weight, norm_grads, norm_moment, norm_weight):
    rank = q_basis.shape[1]
    size = q_grad.shape[1]
    flat = norm_grads.shape[-1]
    share = norm_moment.shape[0]
    row_count = q_moment.shape[0]
    device = lax.axis_index("rep") * n_shard + lax.axis_index("shard")
    keep = step_size * decay_rate

    base = jnp.concatenate([q_weight - keep * q_moment, o_weight - keep * o_moment], axis=1)
    gather = Gather(base, n_rep)

    grads = norm_grads.reshape(flat)
    own_grads = lax.dynamic_slice(grads, (device * share,), (share,))
    placed = lax.dynamic_update_slice(-step_size * grads, (norm_weight - keep * norm_moment) - step_size * own_grads, (device * share,))
    extra = jnp.concatenate([grads.reshape(-1, LANES), placed.reshape(-1, LANES)], axis=0)
    extra_rows = extra.shape[0]
    extra = jnp.pad(extra, ((0, 2 * rank - extra_rows), (0, 0)))

    corr_q, corr_o, part = first((q_grad[0].T, o_grad[0].T), (q_error[0].T, o_error[0].T), q_basis.T, o_basis.T)
    for sweep in range(ROUNDS):
        last = sweep == ROUNDS - 1
        left = sum_over_all(part, n_rep, n_shard, gather, 2 * sweep)
        if last:
            extra_sum = left[:extra_rows, size:]
            left = left[:, :size]
        right = right_of(left, corr_q, corr_o)
        inverse = inverse_of(left)
        right = sum_over(right, n_rep, gather, 2 * sweep + 1)
        if not last:
            part = left_of(right, inverse, corr_q, corr_o, [extra] if sweep == ROUNDS - 2 else [])
    normal, stack = normal_of(left, inverse)
    if gather.paired:
        own = lax.dynamic_slice_in_dim(normal, lax.axis_index("rep") * row_count, row_count, 1)
        outs = finish(corr_q, corr_o, gather.turned_rows(), stack, inverse, right, own, q_moment, o_moment)
    else:
        outs = finish_plain(corr_q, corr_o, base, normal, inverse, right, q_moment, o_moment)
    weight_q, weight_o, error_q, error_o, q_moment_new, o_moment_new = outs
    half = extra_rows // 2
    norm_sum = extra_sum[:half].reshape(flat)
    norm_weight_new = extra_sum[half:].reshape(flat)
    norm_moment_new = decay_rate * norm_moment + lax.dynamic_slice(norm_sum, (device * share,), (share,))
    return (
        weight_q.T,
        weight_o.T,
        q_moment_new,
        o_moment_new,
        error_q.T[None],
        error_o.T[None],
        norm_weight_new,
        norm_moment_new,
    )


def solution(mesh):
    n_rep, n_shard = mesh.shape["rep"], mesh.shape["shard"]

    def whole(*arrays):
        return per_device(n_rep, n_shard, *arrays)

    return jax.shard_map(
        whole,
        mesh=mesh,
        in_specs=(
            P("rep", None, "shard"),
            P("rep", None, "shard"),
            P("rep", None, "shard"),
            P("rep", None, "shard"),
            P("shard", None),
            P("shard", None),
            P("rep", "shard"),
            P("rep", "shard"),
            P("rep", "shard"),
            P("rep", "shard"),
            P("rep", "shard", None),
            P(("rep", "shard")),
            P(("rep", "shard")),
        ),
        out_specs=(
            P(None, "shard"),
            P(None, "shard"),
            P("rep", "shard"),
            P("rep", "shard"),
            P("rep", None, "shard"),
            P("rep", None, "shard"),
            P(),
            P(("rep", "shard")),
        ),
        check_vma=False,
    )
```

```python
import functools

import jax
import jax.numpy as jnp
from jax import lax
from jax.experimental import pallas as pl
from jax.experimental.pallas import tpu as pltpu
from jax.sharding import PartitionSpec as P

ROUNDS = 2
GROUP = 8
LANES = 128

highest = lax.Precision.HIGHEST
decay_rate = 0.9
step_size = 0.1
f32 = jnp.float32
bf16 = jnp.bfloat16
NN = (((1,), (0,)), ((), ()))
NT = (((1,), (1,)), ((), ()))
TN = (((0,), (0,)), ((), ()))

IN_HBM = pl.BlockSpec(memory_space=pltpu.HBM)
IN_VMEM = pl.BlockSpec(memory_space=pltpu.VMEM)
SMALL = pltpu.CompilerParams(vmem_limit_bytes=8 * 2**20)
LARGE = pltpu.CompilerParams(vmem_limit_bytes=16 * 2**20)
QUICK = pl.CostEstimate(flops=1000, bytes_accessed=1000, transcendentals=0)
SLOW = pl.CostEstimate(flops=1000, bytes_accessed=6_000_000, transcendentals=0)


def hold(space, *arrays):
    return [pltpu.with_memory_space_constraint(array, space) for array in arrays]


def exact(left, right, dims):
    return lax.dot_general(left, right, dims, precision=highest, preferred_element_type=f32)


def three(x):
    high = x.astype(bf16)
    rest = x - high.astype(f32)
    middle = rest.astype(bf16)
    low = (rest - middle.astype(f32)).astype(bf16)
    return high, middle, low


def stacked(left, right, dims):
    rows = left.shape[0]
    left_high, left_middle, left_low = three(left)
    right_high, right_middle, right_low = three(right)
    lefts = jnp.concatenate([left_high, left_middle, left_low], axis=0)
    of_high = lax.dot_general(lefts, right_high, dims, preferred_element_type=f32)
    of_middle = lax.dot_general(lefts[: 2 * rows], right_middle, dims, preferred_element_type=f32)
    of_low = lax.dot_general(left_high, right_low, dims, preferred_element_type=f32)
    small = (of_high[2 * rows :] + of_middle[rows:]) + of_low
    return of_high[:rows] + ((of_high[rows : 2 * rows] + of_middle[:rows]) + small)


def halves(count):
    masks = []
    mask = 1
    while mask < count:
        masks.append(mask)
        mask *= 2
    return masks


def swap(block, axis, mask, count):
    pairs = [(i, i ^ mask) for i in range(count)]
    return lax.ppermute(block, axis, pairs)


def sum_over(block, count, gather, stage):
    for mask in halves(count):
        block = gather.before(block, stage, mask)
        block = gather.start_tasks(block, stage, mask)
        block = block + gather.end_tasks(swap(block, "rep", mask, count), stage, mask)
        block = gather.after(block, stage, mask)
    return gather.before(block, stage, 0)


def sum_over_all(part, n_rep, n_shard, gather, stage):
    place = lax.axis_index("shard")
    bits = [(mask, (place & mask) != 0) for mask in halves(n_shard)]
    for mask, high in bits:
        half = part.shape[0] // 2
        low_rows, high_rows = part[:half], part[half:]
        keep = jnp.where(high, high_rows, low_rows)
        give = jnp.where(high, low_rows, high_rows)
        part = keep + swap(give, "shard", mask, n_shard)
    part = sum_over(part, n_rep, gather, stage)
    for mask, high in reversed(bits):
        other = swap(part, "shard", mask, n_shard)
        part = jnp.concatenate([jnp.where(high, other, part), jnp.where(high, part, other)], axis=0)
    return part


class Gather:
    PLAN = (
        ("near", "own", 2, None, (0, 2)),
        ("turned", "own", 1, (0, 1), (0, 0)),
        ("far", "own", 4, (0, 4), (1, 2)),
        ("turned_near", "near", 1, (1, 1), (1, 0)),
        ("last", "far", 2, (1, 4), (2, 2)),
        ("turned_far", "far", 1, (2, 1), (2, 0)),
        ("turned_last", "last", 1, (3, 1), (3, 0)),
    )
    INSERTS = {
        (1, 4): ("own", "near"),
        (2, 1): ("turned", "turned_near"),
        (2, 2): ("far",),
        (2, 4): ("last",),
        (3, 4): ("turned_far",),
    }
    PLACES = {"own": 0, "turned": 1, "near": 2, "far": 4, "last": 6, "turned_near": 3, "turned_far": 5, "turned_last": 7}

    def __init__(self, own, count):
        self.count = count
        self.blocks = {"own": own}
        self.paired = count == 8 and own.shape[0] % 8 == 0
        self.rows = None
        self.tasks = {}
        self.results = {}
        self.send(None)

    def send(self, point):
        if self.paired:
            for name, source, mask, after, _ in self.PLAN:
                if after == point:
                    self.blocks[name] = swap(self.blocks[source], "rep", mask, self.count)

    def start_tasks(self, value, stage, mask):
        point = (stage, mask)
        if point in self.tasks:
            task, *inputs = self.tasks[point]
            value, *inputs = lax.optimization_barrier((value, *inputs))
            self.results[point] = task(*inputs)
        if self.paired and point in self.INSERTS:
            value, *blocks = lax.optimization_barrier((value, *(self.blocks[name] for name in self.INSERTS[point])))
            self.insert(blocks, self.INSERTS[point])
        return value

    def end_tasks(self, value, stage, mask):
        point = (stage, mask)
        if point in self.tasks:
            value, self.results[point] = lax.optimization_barrier((value, self.results[point]))
        if self.paired and point in self.INSERTS:
            value, self.rows = lax.optimization_barrier((value, self.rows))
        return value

    def insert(self, blocks, names):
        self.rows = insert(self.rows, blocks, [self.PLACES[name] for name in names], self.count)

    def before(self, value, stage, mask):
        if self.paired:
            for name, _, _, _, by in self.PLAN:
                if by == (stage, mask):
                    value, self.blocks[name] = lax.optimization_barrier((value, self.blocks[name]))
        return value

    def after(self, value, stage, mask):
        if self.paired:
            for name, source, _, after, _ in self.PLAN:
                if after == (stage, mask):
                    value, self.blocks[source] = lax.optimization_barrier((value, self.blocks[source]))
            self.send((stage, mask))
        return value


def insert_kernel(masks, place_ref, *refs):
    blocks, rows, out = refs[: len(masks)], refs[len(masks) : -1], refs[-1]
    if not rows:
        out[...] = jnp.zeros_like(out)
    height = out.shape[0]
    window = 2 * LANES
    lane = lax.broadcasted_iota(jnp.int32, (height, window), 1)
    for block, mask in zip(blocks, masks):
        count = block.shape[0]
        index = place_ref[0] ^ mask
        shift = index * (count - LANES)
        turned = jnp.concatenate([block[...].T, jnp.zeros((height, window - count), f32)], axis=1)
        turned = pltpu.roll(turned, shift, 1)
        at = pl.ds(pl.multiple_of(index * LANES, LANES), window)
        out[:, at] = jnp.where((lane >= shift) & (lane < shift + count), turned, out[:, at])


def insert(rows, blocks, masks, count):
    height, width = blocks[0].shape[1], blocks[0].shape[0] * count
    place = lax.axis_index("rep").astype(jnp.int32).reshape(1)
    old = [] if rows is None else hold(pltpu.VMEM, rows)
    return pl.pallas_call(
        functools.partial(insert_kernel, masks),
        in_specs=[pl.BlockSpec(memory_space=pltpu.SMEM)] + [IN_VMEM] * (len(blocks) + len(old)),
        out_specs=IN_VMEM,
        out_shape=pltpu.VMEM((height, width), f32),
        input_output_aliases={1 + len(blocks): 0} if old else {},
        compiler_params=SMALL,
        cost_estimate=SLOW,
        name="insert",
    )(place, *blocks, *old)


def first_kernel(chunks, grad_q, grad_o, error_q, error_o, basis_q, basis_o, corr_q, corr_o, part, buffer, bases, sems, base_sems):
    rank, size = basis_q.shape[0], corr_q.shape[1]
    lanes = size // chunks
    base_copies = [pltpu.make_async_copy(source, bases.at[k], base_sems.at[k]) for k, source in enumerate((basis_q, basis_o))]
    copies = {}
    for copy in base_copies:
        copy.start()
    for c in range(chunks):
        at = pl.ds(c * lanes, lanes)
        for j, source in enumerate((grad_q, error_q, grad_o, error_o)):
            copies[c, j] = pltpu.make_async_copy(source.at[:, at], buffer.at[j, :, at], sems.at[c, j])
            copies[c, j].start()
    for copy in base_copies:
        copy.wait()
    for c in range(chunks):
        at = pl.ds(c * lanes, lanes)
        for k, corr in enumerate((corr_q, corr_o)):
            copies[c, 2 * k].wait()
            copies[c, 2 * k + 1].wait()
            total = buffer[2 * k, :, at] + buffer[2 * k + 1, :, at]
            corr[:, at] = total
            part[k * rank : (k + 1) * rank, at] = stacked(bases[k], total, NN)


def first(grads, errors, basis_q, basis_o):
    width, size = grads[0].shape
    rank = basis_q.shape[0]
    chunks = 3 if size % (3 * LANES) == 0 else 1
    return pl.pallas_call(
        functools.partial(first_kernel, chunks),
        in_specs=[IN_HBM] * 6,
        out_specs=[IN_VMEM] * 3,
        out_shape=[pltpu.VMEM((width, size), f32)] * 2 + [pltpu.VMEM((2 * rank, size), f32)],
        scratch_shapes=[
            pltpu.VMEM((4, width, size), f32),
            pltpu.VMEM((2, rank, width), f32),
            pltpu.SemaphoreType.DMA((chunks, 4)),
            pltpu.SemaphoreType.DMA((2,)),
        ],
        compiler_params=LARGE,
        name="first",
    )(*hold(pltpu.HBM, *grads, *errors, basis_q, basis_o))


def right_kernel(left, corr_q, corr_o, out):
    rank = left.shape[0] // 2
    out[...] = jnp.concatenate([stacked(left[:rank, :], corr_q[...], NT), stacked(left[rank:, :], corr_o[...], NT)], axis=1)


def right_of(left, corr_q, corr_o):
    rank, width = left.shape[0] // 2, corr_q.shape[0]
    return pl.pallas_call(
        right_kernel,
        in_specs=[IN_VMEM] * 3,
        out_specs=IN_VMEM,
        out_shape=pltpu.VMEM((rank, 2 * width), f32),
        compiler_params=SMALL,
        cost_estimate=QUICK,
        name="right",
    )(left, *hold(pltpu.VMEM, corr_q, corr_o))


def left_kernel(right, inverse, corr_q, corr_o, *refs):
    extra, out = refs[:-1], refs[-1]
    rank, width = right.shape[0], right.shape[1] // 2
    size = corr_q.shape[1]
    basis_q = exact(inverse[0], right[:, :width], NN)
    basis_o = exact(inverse[1], right[:, width:], NN)
    out[:rank, :size] = stacked(basis_q, corr_q[...], NN)
    out[rank:, :size] = stacked(basis_o, corr_o[...], NN)
    if extra:
        out[:, size:] = extra[0][...]


def left_of(right, inverse, corr_q, corr_o, extra):
    rank, size = right.shape[0], corr_q.shape[1]
    lanes = size + sum(array.shape[1] for array in extra)
    return pl.pallas_call(
        left_kernel,
        in_specs=[IN_VMEM] * (4 + len(extra)),
        out_specs=IN_VMEM,
        out_shape=pltpu.VMEM((2 * rank, lanes), f32),
        compiler_params=SMALL,
        cost_estimate=QUICK,
        name="left",
    )(right, inverse, *hold(pltpu.VMEM, corr_q, corr_o), *extra)


def eliminate(gram_q, gram_o, rank):
    width = 4 * rank
    lane = lax.broadcasted_iota(jnp.int32, (rank, width), 1)
    row = lax.broadcasted_iota(jnp.int32, (rank, width), 0)
    square = (rank, rank)
    eye = (lax.broadcasted_iota(jnp.int32, square, 0) == lax.broadcasted_iota(jnp.int32, square, 1)).astype(f32)
    work = jnp.concatenate([gram_q, eye, gram_o, eye], axis=1)
    first_half = lane < 2 * rank
    scale = jnp.ones((rank, width), f32)
    for base in range(0, rank, GROUP):
        columns = []
        for k in range(base, base + GROUP):
            of_q = jnp.broadcast_to(work[:, k : k + 1], (rank, width))
            of_o = jnp.broadcast_to(work[:, 2 * rank + k : 2 * rank + k + 1], (rank, width))
            columns.append(jnp.where(first_half, of_q, of_o))
        for j in range(GROUP):
            k = base + j
            pivot = columns[j][k : k + 1]
            factor = jnp.where(row > k, columns[j] * (1.0 / pivot), 0.0)
            scale = jnp.where(row == k, pivot, scale)
            for i in range(j + 1, GROUP):
                columns[i] = columns[i] - factor * columns[i][k : k + 1]
            work = work - factor * work[k : k + 1]
    work = work * lax.rsqrt(scale)
    return work[:, rank : 2 * rank], work[:, 3 * rank :]


def inverse_kernel(left, out):
    rank, size = out.shape[1], left.shape[1]
    left_q, left_o = left[:rank, :], left[rank:, :]
    out[0], out[1] = eliminate(exact(left_q, left_q, NT), exact(left_o, left_o, NT), rank)


def inverse_of(left):
    rank = left.shape[0] // 2
    return pl.pallas_call(
        inverse_kernel,
        out_shape=pltpu.VMEM((2, rank, rank), f32),
        compiler_params=SMALL,
        cost_estimate=SLOW,
        name="inverse",
    )(left)


def stack_kernel(place_ref, left, stack, own):
    rank = left.shape[0] // 2
    for p in range(2):
        high, middle, low = three(left[p * rank : (p + 1) * rank, :])
        stack[p] = jnp.concatenate([high, middle, low, high, middle, high], axis=0)
    count = own.shape[1]
    index = place_ref[0]
    window = left[:, pl.ds(pl.multiple_of(index * LANES, LANES), 2 * LANES)]
    own[...] = pltpu.roll(window, 2 * LANES - index * (count - LANES), 1)[:, :count]


def stack_of(left, count):
    rank, size = left.shape[0] // 2, left.shape[1]
    place = lax.axis_index("rep").astype(jnp.int32).reshape(1)
    return pl.pallas_call(
        stack_kernel,
        in_specs=[pl.BlockSpec(memory_space=pltpu.SMEM), IN_VMEM],
        out_specs=[IN_VMEM] * 2,
        out_shape=[pltpu.VMEM((2, 6 * rank, size), bf16), pltpu.VMEM((2 * rank, count), f32)],
        compiler_params=SMALL,
        cost_estimate=SLOW,
        name="stack",
    )(place, left)


def finish_kernel(chunks, corr_q, corr_o, rows, stack, inverse, right, own, moment_q, moment_o, *refs):
    outs, buffer, new_moments, sems, moment_sems = refs[:6], refs[6], refs[7], refs[8], refs[9]
    rank, width = inverse.shape[1], moment_q.shape[1]
    height = width // chunks
    copies = []
    for p, corr in enumerate((corr_q, corr_o)):
        factor = right[:, p * width : (p + 1) * width]
        scaled = exact(inverse[p], exact(inverse[p], factor, NN), TN)
        high, middle, low = three(scaled.T)
        lefts = jnp.concatenate([high, high, high, middle, middle, low], axis=1)
        for c in range(chunks):
            at = pl.ds(c * height, height)
            decoded = lax.dot_general(lefts[c * height : (c + 1) * height], stack[p], NN, preferred_element_type=f32)
            buffer[p, at, :] = rows[pl.ds(p * width + c * height, height), :] - step_size * decoded
            buffer[2 + p, at, :] = corr[at, :] - decoded
            for k in (p, 2 + p):
                copies.append(pltpu.make_async_copy(buffer.at[k, at, :], outs[k].at[at, :], sems.at[k, c]))
                copies[-1].start()
    for p, moment in enumerate((moment_q, moment_o)):
        factor = right[:, p * width : (p + 1) * width]
        scaled = exact(inverse[p], exact(inverse[p], factor, NN), TN)
        new_moments[p] = decay_rate * moment[...] + exact(own[p * rank : (p + 1) * rank, :], scaled, TN)
        copies.append(pltpu.make_async_copy(new_moments.at[p], outs[4 + p], moment_sems.at[p]))
        copies[-1].start()
    for copy in copies:
        copy.wait()


def finish(corr_q, corr_o, rows, stack, inverse, right, own, moment_q, moment_o):
    width, size = corr_q.shape
    chunks = 3
    return pl.pallas_call(
        functools.partial(finish_kernel, chunks),
        in_specs=[IN_VMEM] * 9,
        out_specs=[IN_HBM] * 6,
        out_shape=[pltpu.HBM((width, size), f32)] * 4 + [pltpu.HBM(moment_q.shape, f32)] * 2,
        scratch_shapes=[
            pltpu.VMEM((4, width, size), f32),
            pltpu.VMEM((2,) + moment_q.shape, f32),
            pltpu.SemaphoreType.DMA((4, chunks)),
            pltpu.SemaphoreType.DMA((2,)),
        ],
        compiler_params=LARGE,
        name="finish",
    )(*hold(pltpu.VMEM, corr_q, corr_o, rows), stack, inverse, right, own, moment_q, moment_o)


def finish_plain(corr_q, corr_o, base, left, inverse, right, moment_q, moment_o):
    rank, width = inverse.shape[1], moment_q.shape[1]
    rows = moment_q.shape[0]
    start = lax.axis_index("rep") * rows
    bases = lax.all_gather(base, "rep", axis=0, tiled=True)
    weights, moments, errors = [], [], []
    for p, (corr, moment) in enumerate(((corr_q, moment_q), (corr_o, moment_o))):
        at = slice(p * width, (p + 1) * width)
        scaled = exact(inverse[p], exact(inverse[p], right[:, at], NN), TN)
        decoded = exact(scaled, left[p * rank : (p + 1) * rank], TN)
        weights.append(bases[:, at].T - step_size * decoded)
        moments.append(decay_rate * moment + lax.dynamic_slice_in_dim(decoded, start, rows, 1).T)
        errors.append(corr - decoded)
    return weights + errors + moments


def per_device(n_rep, n_shard, q_grad, o_grad, q_error, o_error, q_basis, o_basis, q_moment, o_moment, q_weight, o_weight, norm_grads, norm_moment, norm_weight):
    rank = q_basis.shape[1]
    size = q_grad.shape[1]
    flat = norm_grads.shape[-1]
    share = norm_moment.shape[0]
    row_count = q_moment.shape[0]
    device = lax.axis_index("rep") * n_shard + lax.axis_index("shard")
    keep = step_size * decay_rate

    base = jnp.concatenate([q_weight - keep * q_moment, o_weight - keep * o_moment], axis=1)
    gather = Gather(base, n_rep)

    grads = norm_grads.reshape(flat)
    own_grads = lax.dynamic_slice(grads, (device * share,), (share,))
    placed = lax.dynamic_update_slice(-step_size * grads, (norm_weight - keep * norm_moment) - step_size * own_grads, (device * share,))
    extra = jnp.concatenate([grads.reshape(-1, LANES), placed.reshape(-1, LANES)], axis=0)
    extra_rows = extra.shape[0]
    extra = jnp.pad(extra, ((0, 2 * rank - extra_rows), (0, 0)))

    corr_q, corr_o, part = first((q_grad[0].T, o_grad[0].T), (q_error[0].T, o_error[0].T), q_basis.T, o_basis.T)
    for sweep in range(ROUNDS):
        last = sweep == ROUNDS - 1
        left = sum_over_all(part, n_rep, n_shard, gather, 2 * sweep)
        if last:
            extra_sum = left[:extra_rows, size:]
            left = left[:, :size]
        right = right_of(left, corr_q, corr_o)
        if last and gather.paired:
            gather.tasks[3, 1] = (functools.partial(stack_of, count=row_count), left)
        gather.tasks[2 * sweep + 1, 2] = (inverse_of, left)
        right = sum_over(right, n_rep, gather, 2 * sweep + 1)
        inverse = gather.results[2 * sweep + 1, 2]
        if not last:
            part = left_of(right, inverse, corr_q, corr_o, [extra] if sweep == ROUNDS - 2 else [])
    if gather.paired:
        stack, own = gather.results[3, 1]
        gather.insert([gather.blocks["turned_last"]], ["turned_last"])
        outs = finish(corr_q, corr_o, gather.rows, stack, inverse, right, own, q_moment, o_moment)
    else:
        outs = finish_plain(corr_q, corr_o, base, left, inverse, right, q_moment, o_moment)
    weight_q, weight_o, error_q, error_o, q_moment_new, o_moment_new = outs
    half = extra_rows // 2
    norm_sum = extra_sum[:half].reshape(flat)
    norm_weight_new = extra_sum[half:].reshape(flat)
    norm_moment_new = decay_rate * norm_moment + lax.dynamic_slice(norm_sum, (device * share,), (share,))
    return (
        weight_q.T,
        weight_o.T,
        q_moment_new,
        o_moment_new,
        error_q.T[None],
        error_o.T[None],
        norm_weight_new,
        norm_moment_new,
    )


def solution(mesh):
    n_rep, n_shard = mesh.shape["rep"], mesh.shape["shard"]

    def whole(*arrays):
        return per_device(n_rep, n_shard, *arrays)

    return jax.shard_map(
        whole,
        mesh=mesh,
        in_specs=(
            P("rep", None, "shard"),
            P("rep", None, "shard"),
            P("rep", None, "shard"),
            P("rep", None, "shard"),
            P("shard", None),
            P("shard", None),
            P("rep", "shard"),
            P("rep", "shard"),
            P("rep", "shard"),
            P("rep", "shard"),
            P("rep", "shard", None),
            P(("rep", "shard")),
            P(("rep", "shard")),
        ),
        out_specs=(
            P(None, "shard"),
            P(None, "shard"),
            P("rep", "shard"),
            P("rep", "shard"),
            P("rep", None, "shard"),
            P("rep", None, "shard"),
            P(),
            P(("rep", "shard")),
        ),
        check_vma=False,
    )
```

```python
import functools

import jax
import jax.numpy as jnp
from jax import lax
from jax.experimental import pallas as pl
from jax.experimental.pallas import tpu as pltpu
from jax.sharding import PartitionSpec as P

ROUNDS = 2
GROUP = 8
LANES = 128

highest = lax.Precision.HIGHEST
decay_rate = 0.9
step_size = 0.1
f32 = jnp.float32
bf16 = jnp.bfloat16
NN = (((1,), (0,)), ((), ()))
NT = (((1,), (1,)), ((), ()))
TN = (((0,), (0,)), ((), ()))

IN_HBM = pl.BlockSpec(memory_space=pltpu.HBM)
IN_VMEM = pl.BlockSpec(memory_space=pltpu.VMEM)
IN_SMEM = pl.BlockSpec(memory_space=pltpu.SMEM)
SMALL = pltpu.CompilerParams(vmem_limit_bytes=8 * 2**20)
LARGE = pltpu.CompilerParams(vmem_limit_bytes=16 * 2**20)
QUICK = pl.CostEstimate(flops=1000, bytes_accessed=1000, transcendentals=0)
SLOW = pl.CostEstimate(flops=1000, bytes_accessed=6_000_000, transcendentals=0)


def hold(space, *arrays):
    return [pltpu.with_memory_space_constraint(array, space) for array in arrays]


def exact(left, right, dims):
    return lax.dot_general(left, right, dims, precision=highest, preferred_element_type=f32)


def three(x):
    high = x.astype(bf16)
    rest = x - high.astype(f32)
    middle = rest.astype(bf16)
    low = (rest - middle.astype(f32)).astype(bf16)
    return high, middle, low


def stacked(left, right, dims):
    rows = left.shape[0]
    left_high, left_middle, left_low = three(left)
    right_high, right_middle, right_low = three(right)
    lefts = jnp.concatenate([left_high, left_middle, left_low], axis=0)
    of_high = lax.dot_general(lefts, right_high, dims, preferred_element_type=f32)
    of_middle = lax.dot_general(lefts[: 2 * rows], right_middle, dims, preferred_element_type=f32)
    of_low = lax.dot_general(left_high, right_low, dims, preferred_element_type=f32)
    small = (of_high[2 * rows :] + of_middle[rows:]) + of_low
    return of_high[:rows] + ((of_high[rows : 2 * rows] + of_middle[:rows]) + small)


def halves(count):
    masks = []
    mask = 1
    while mask < count:
        masks.append(mask)
        mask *= 2
    return masks


def swap(block, axis, mask, count):
    pairs = [(i, i ^ mask) for i in range(count)]
    return lax.ppermute(block, axis, pairs)


def sum_over(block, count, gather, stage):
    for mask in halves(count):
        block = gather.before(block, stage, mask)
        block = gather.start_tasks(block, stage, mask)
        block = block + gather.end_tasks(swap(block, "rep", mask, count), stage, mask)
        block = gather.after(block, stage, mask)
    return gather.before(block, stage, 0)


def sum_over_all(keep, give, bits, n_rep, n_shard, gather, stage):
    masks = halves(n_shard)
    for k, mask in enumerate(masks):
        got = swap(give, "shard", mask, n_shard)
        if k < len(masks) - 1:
            keep, give = split(keep, got, bits[k + 1])
            keep = gather.before(keep, stage, "core")
    part = sum_over(keep + got, n_rep, gather, stage)
    for mask, bit in reversed(list(zip(masks, bits))[1:]):
        part = join(part, swap(part, "shard", mask, n_shard), bit)
        part = gather.before(part, stage, "x")
    return part, swap(part, "shard", masks[0], n_shard)


def split_kernel(bit_ref, ours, got, keep, give):
    total = ours[...] + got[...]
    half = total.shape[0] // 2
    high = bit_ref[0] != 0
    keep[...] = jnp.where(high, total[half:], total[:half])
    give[...] = jnp.where(high, total[:half], total[half:])


def split(ours, got, bit):
    half = pltpu.VMEM((ours.shape[0] // 2, ours.shape[1]), f32)
    return pl.pallas_call(
        split_kernel,
        in_specs=[IN_SMEM, IN_VMEM, IN_VMEM],
        out_specs=[IN_VMEM] * 2,
        out_shape=[half, half],
        compiler_params=SMALL,
        cost_estimate=QUICK,
        name="split",
    )(bit, ours, got)


def joined(bit_ref, ours, got):
    high = bit_ref[0] != 0
    return jnp.concatenate([jnp.where(high, got, ours), jnp.where(high, ours, got)], axis=0)


def join_kernel(bit_ref, ours, got, whole):
    whole[...] = joined(bit_ref, ours[...], got[...])


def join(ours, got, bit):
    return pl.pallas_call(
        join_kernel,
        in_specs=[IN_SMEM, IN_VMEM, IN_VMEM],
        out_specs=IN_VMEM,
        out_shape=pltpu.VMEM((2 * ours.shape[0], ours.shape[1]), f32),
        compiler_params=SMALL,
        cost_estimate=QUICK,
        name="join",
    )(bit, ours, got)


class Gather:
    PLAN = (
        ("near", "own", 2, None, (0, 2)),
        ("turned", "own", 1, (0, 1), (0, "x")),
        ("far_a", "own_a", 4, (0, 4), (1, 2)),
        ("turned_near", "near", 1, (1, 1), (2, "core")),
        ("far_b", "own_b", 4, (1, 4), (2, 2)),
        ("turned_far", "far", 1, (2, 1), (2, "x")),
        ("last", "far", 2, (2, 4), (3, 2)),
        ("turned_last", "last", 1, ("ahead", 3, 2), (3, 0)),
    )
    INSERTS = {
        (1, 4): ("own", "near"),
        (2, 1): ("turned", "turned_near"),
        (2, 4): ("far",),
        (3, 4): ("turned_far", "last"),
    }
    PLACES = {"own": 0, "turned": 1, "near": 2, "far": 4, "last": 6, "turned_near": 3, "turned_far": 5, "turned_last": 7}

    def __init__(self, own, count):
        self.count = count
        half = own.shape[0] // 2
        self.blocks = {"own": own, "own_a": own[:half], "own_b": own[half:]}
        self.paired = count == 8 and own.shape[0] % 16 == 0
        self.rows = None
        self.tasks = {}
        self.results = {}
        self.send(None)

    def send(self, point):
        if self.paired:
            for name, source, mask, after, _ in self.PLAN:
                if after == point:
                    if source == "far" and source not in self.blocks:
                        self.blocks["far"] = jnp.concatenate([self.blocks["far_a"], self.blocks["far_b"]], axis=0)
                    self.blocks[name] = swap(self.blocks[source], "rep", mask, self.count)

    def start_tasks(self, value, stage, mask):
        point = (stage, mask)
        if point in self.tasks:
            task, *inputs = self.tasks[point]
            value, *inputs = lax.optimization_barrier((value, *inputs))
            self.results[point] = task(*inputs)
        if self.paired and point in self.INSERTS:
            value, *blocks = lax.optimization_barrier((value, *(self.blocks[name] for name in self.INSERTS[point])))
            self.insert(blocks, self.INSERTS[point])
        return value

    def end_tasks(self, value, stage, mask):
        point = (stage, mask)
        if point in self.tasks:
            value, self.results[point] = lax.optimization_barrier((value, self.results[point]))
        if self.paired and point in self.INSERTS:
            value, self.rows = lax.optimization_barrier((value, self.rows))
        return value

    def insert(self, blocks, names):
        self.rows = insert(self.rows, blocks, [self.PLACES[name] for name in names], self.count)

    def before(self, value, stage, mask):
        if self.paired:
            for name, _, _, _, by in self.PLAN:
                if by == (stage, mask):
                    value, self.blocks[name] = lax.optimization_barrier((value, self.blocks[name]))
            self.send(("ahead", stage, mask))
        return value

    def after(self, value, stage, mask):
        if self.paired:
            for name, source, _, after, _ in self.PLAN:
                if after == (stage, mask) and source in self.blocks:
                    value, self.blocks[source] = lax.optimization_barrier((value, self.blocks[source]))
            self.send((stage, mask))
        return value


def insert_kernel(masks, place_ref, *refs):
    blocks, rows, out = refs[: len(masks)], refs[len(masks) : -1], refs[-1]
    if not rows:
        out[...] = jnp.zeros_like(out)
    height = out.shape[0]
    window = 2 * LANES
    lane = lax.broadcasted_iota(jnp.int32, (height, window), 1)
    for block, mask in zip(blocks, masks):
        count = block.shape[0]
        index = place_ref[0] ^ mask
        shift = index * (count - LANES)
        turned = jnp.concatenate([block[...].T, jnp.zeros((height, window - count), f32)], axis=1)
        turned = pltpu.roll(turned, shift, 1)
        at = pl.ds(pl.multiple_of(index * LANES, LANES), window)
        out[:, at] = jnp.where((lane >= shift) & (lane < shift + count), turned, out[:, at])


def insert(rows, blocks, masks, count):
    height, width = blocks[0].shape[1], blocks[0].shape[0] * count
    place = lax.axis_index("rep").astype(jnp.int32).reshape(1)
    old = [] if rows is None else hold(pltpu.VMEM, rows)
    return pl.pallas_call(
        functools.partial(insert_kernel, masks),
        in_specs=[IN_SMEM] + [IN_VMEM] * (len(blocks) + len(old)),
        out_specs=IN_VMEM,
        out_shape=pltpu.VMEM((height, width), f32),
        input_output_aliases={1 + len(blocks): 0} if old else {},
        compiler_params=SMALL,
        cost_estimate=SLOW,
        name="insert",
    )(place, *blocks, *old)


def first_kernel(chunks, bit_ref, grad_q, grad_o, error_q, error_o, basis_q, basis_o, corr_q, corr_o, keep, give, buffer, bases, sems, base_sems):
    size = corr_q.shape[1]
    high = bit_ref[0] != 0
    lanes = size // chunks
    base_copies = [pltpu.make_async_copy(source, bases.at[k], base_sems.at[k]) for k, source in enumerate((basis_q, basis_o))]
    copies = {}
    for copy in base_copies:
        copy.start()
    for c in range(chunks):
        at = pl.ds(c * lanes, lanes)
        for j, source in enumerate((grad_q, error_q, grad_o, error_o)):
            copies[c, j] = pltpu.make_async_copy(source.at[:, at], buffer.at[j, :, at], sems.at[c, j])
            copies[c, j].start()
    for copy in base_copies:
        copy.wait()
    for c in range(chunks):
        at = pl.ds(c * lanes, lanes)
        parts = []
        for k, corr in enumerate((corr_q, corr_o)):
            copies[c, 2 * k].wait()
            copies[c, 2 * k + 1].wait()
            total = buffer[2 * k, :, at] + buffer[2 * k + 1, :, at]
            corr[:, at] = total
            parts.append(stacked(bases[k], total, NN))
        keep[:, at] = jnp.where(high, parts[1], parts[0])
        give[:, at] = jnp.where(high, parts[0], parts[1])


def first(grads, errors, basis_q, basis_o, bit):
    width, size = grads[0].shape
    rank = basis_q.shape[0]
    chunks = 3 if size % (3 * LANES) == 0 else 1
    return pl.pallas_call(
        functools.partial(first_kernel, chunks),
        in_specs=[IN_SMEM] + [IN_HBM] * 6,
        out_specs=[IN_VMEM] * 4,
        out_shape=[pltpu.VMEM((width, size), f32)] * 2 + [pltpu.VMEM((rank, size), f32)] * 2,
        scratch_shapes=[
            pltpu.VMEM((4, width, size), f32),
            pltpu.VMEM((2, rank, width), f32),
            pltpu.SemaphoreType.DMA((chunks, 4)),
            pltpu.SemaphoreType.DMA((2,)),
        ],
        compiler_params=LARGE,
        name="first",
    )(bit, *hold(pltpu.HBM, *grads, *errors, basis_q, basis_o))


def right_kernel(bit_ref, ours, got, corr_q, corr_o, right, left, *extra):
    rank, size = ours.shape[0], corr_q.shape[1]
    whole = joined(bit_ref, ours[...], got[...])
    left[...] = whole[:, :size]
    if extra:
        extra[0][...] = whole[:, size:]
    right[...] = jnp.concatenate([stacked(whole[:rank, :size], corr_q[...], NT), stacked(whole[rank:, :size], corr_o[...], NT)], axis=1)


def right_of(ours, got, bit, corr_q, corr_o):
    rank = ours.shape[0]
    width, size = corr_q.shape
    beside = ours.shape[1] - size
    shapes = [(rank, 2 * width), (2 * rank, size)] + ([(2 * rank, beside)] if beside else [])
    return pl.pallas_call(
        right_kernel,
        in_specs=[IN_SMEM] + [IN_VMEM] * 4,
        out_specs=[IN_VMEM] * len(shapes),
        out_shape=[pltpu.VMEM(shape, f32) for shape in shapes],
        compiler_params=SMALL,
        cost_estimate=QUICK,
        name="right",
    )(bit, ours, got, *hold(pltpu.VMEM, corr_q, corr_o))


def left_kernel(bit_ref, right, inverse, corr_q, corr_o, *refs):
    extra, keep, give = refs[:-2], refs[-2], refs[-1]
    rank, width = right.shape[0], right.shape[1] // 2
    size = corr_q.shape[1]
    high = bit_ref[0] != 0
    basis_q = exact(inverse[0], right[:, :width], NN)
    basis_o = exact(inverse[1], right[:, width:], NN)
    part_q = stacked(basis_q, corr_q[...], NN)
    part_o = stacked(basis_o, corr_o[...], NN)
    keep[:, :size] = jnp.where(high, part_o, part_q)
    give[:, :size] = jnp.where(high, part_q, part_o)
    if extra:
        low_rows, high_rows = extra[0][:rank, :], extra[0][rank:, :]
        keep[:, size:] = jnp.where(high, high_rows, low_rows)
        give[:, size:] = jnp.where(high, low_rows, high_rows)


def left_of(right, inverse, bit, corr_q, corr_o, extra):
    rank, size = right.shape[0], corr_q.shape[1]
    half = pltpu.VMEM((rank, size + sum(array.shape[1] for array in extra)), f32)
    return pl.pallas_call(
        left_kernel,
        in_specs=[IN_SMEM] + [IN_VMEM] * (4 + len(extra)),
        out_specs=[IN_VMEM] * 2,
        out_shape=[half, half],
        compiler_params=SMALL,
        cost_estimate=QUICK,
        name="left",
    )(bit, right, inverse, *hold(pltpu.VMEM, corr_q, corr_o), *extra)


def eliminate(gram_q, gram_o, rank):
    width = 4 * rank
    lane = lax.broadcasted_iota(jnp.int32, (rank, width), 1)
    row = lax.broadcasted_iota(jnp.int32, (rank, width), 0)
    square = (rank, rank)
    eye = (lax.broadcasted_iota(jnp.int32, square, 0) == lax.broadcasted_iota(jnp.int32, square, 1)).astype(f32)
    work = jnp.concatenate([gram_q, eye, gram_o, eye], axis=1)
    first_half = lane < 2 * rank
    scale = jnp.ones((rank, width), f32)
    for base in range(0, rank, GROUP):
        columns = []
        for k in range(base, base + GROUP):
            of_q = jnp.broadcast_to(work[:, k : k + 1], (rank, width))
            of_o = jnp.broadcast_to(work[:, 2 * rank + k : 2 * rank + k + 1], (rank, width))
            columns.append(jnp.where(first_half, of_q, of_o))
        for j in range(GROUP):
            k = base + j
            pivot = columns[j][k : k + 1]
            factor = jnp.where(row > k, columns[j] * (1.0 / pivot), 0.0)
            scale = jnp.where(row == k, pivot, scale)
            for i in range(j + 1, GROUP):
                columns[i] = columns[i] - factor * columns[i][k : k + 1]
            work = work - factor * work[k : k + 1]
    work = work * lax.rsqrt(scale)
    return work[:, rank : 2 * rank], work[:, 3 * rank :]


def inverse_kernel(left, out):
    rank, size = out.shape[1], left.shape[1]
    left_q, left_o = left[:rank, :], left[rank:, :]
    out[0], out[1] = eliminate(exact(left_q, left_q, NT), exact(left_o, left_o, NT), rank)


def inverse_of(left):
    rank = left.shape[0] // 2
    return pl.pallas_call(
        inverse_kernel,
        out_shape=pltpu.VMEM((2, rank, rank), f32),
        compiler_params=SMALL,
        cost_estimate=SLOW,
        name="inverse",
    )(left)


def stack_kernel(place_ref, left, stack, own):
    rank = left.shape[0] // 2
    for p in range(2):
        high, middle, low = three(left[p * rank : (p + 1) * rank, :])
        stack[p] = jnp.concatenate([high, middle, low, high, middle, high], axis=0)
    count = own.shape[1]
    index = place_ref[0]
    window = left[:, pl.ds(pl.multiple_of(index * LANES, LANES), 2 * LANES)]
    own[...] = pltpu.roll(window, 2 * LANES - index * (count - LANES), 1)[:, :count]


def stack_of(left, count):
    rank, size = left.shape[0] // 2, left.shape[1]
    place = lax.axis_index("rep").astype(jnp.int32).reshape(1)
    return pl.pallas_call(
        stack_kernel,
        in_specs=[IN_SMEM, IN_VMEM],
        out_specs=[IN_VMEM] * 2,
        out_shape=[pltpu.VMEM((2, 6 * rank, size), bf16), pltpu.VMEM((2 * rank, count), f32)],
        compiler_params=SMALL,
        cost_estimate=SLOW,
        name="stack",
    )(place, left)


def finish_kernel(chunks, corr_q, corr_o, rows, stack, inverse, right, own, moment_q, moment_o, *refs):
    outs, buffer, new_moments, sems, moment_sems = refs[:6], refs[6], refs[7], refs[8], refs[9]
    rank, width = inverse.shape[1], moment_q.shape[1]
    height = width // chunks
    copies = []
    for p, corr in enumerate((corr_q, corr_o)):
        factor = right[:, p * width : (p + 1) * width]
        scaled = exact(inverse[p], exact(inverse[p], factor, NN), TN)
        high, middle, low = three(scaled.T)
        lefts = jnp.concatenate([high, high, high, middle, middle, low], axis=1)
        for c in range(chunks):
            at = pl.ds(c * height, height)
            decoded = lax.dot_general(lefts[c * height : (c + 1) * height], stack[p], NN, preferred_element_type=f32)
            buffer[p, at, :] = rows[pl.ds(p * width + c * height, height), :] - step_size * decoded
            buffer[2 + p, at, :] = corr[at, :] - decoded
            for k in (p, 2 + p):
                copies.append(pltpu.make_async_copy(buffer.at[k, at, :], outs[k].at[at, :], sems.at[k, c]))
                copies[-1].start()
    for p, moment in enumerate((moment_q, moment_o)):
        factor = right[:, p * width : (p + 1) * width]
        scaled = exact(inverse[p], exact(inverse[p], factor, NN), TN)
        new_moments[p] = decay_rate * moment[...] + exact(own[p * rank : (p + 1) * rank, :], scaled, TN)
        copies.append(pltpu.make_async_copy(new_moments.at[p], outs[4 + p], moment_sems.at[p]))
        copies[-1].start()
    for copy in copies:
        copy.wait()


def finish(corr_q, corr_o, rows, stack, inverse, right, own, moment_q, moment_o):
    width, size = corr_q.shape
    chunks = 3
    return pl.pallas_call(
        functools.partial(finish_kernel, chunks),
        in_specs=[IN_VMEM] * 9,
        out_specs=[IN_HBM] * 6,
        out_shape=[pltpu.HBM((width, size), f32)] * 4 + [pltpu.HBM(moment_q.shape, f32)] * 2,
        scratch_shapes=[
            pltpu.VMEM((4, width, size), f32),
            pltpu.VMEM((2,) + moment_q.shape, f32),
            pltpu.SemaphoreType.DMA((4, chunks)),
            pltpu.SemaphoreType.DMA((2,)),
        ],
        compiler_params=LARGE,
        name="finish",
    )(*hold(pltpu.VMEM, corr_q, corr_o, rows), stack, inverse, right, own, moment_q, moment_o)


def finish_plain(corr_q, corr_o, base, left, inverse, right, moment_q, moment_o):
    rank, width = inverse.shape[1], moment_q.shape[1]
    rows = moment_q.shape[0]
    start = lax.axis_index("rep") * rows
    bases = lax.all_gather(base, "rep", axis=0, tiled=True)
    weights, moments, errors = [], [], []
    for p, (corr, moment) in enumerate(((corr_q, moment_q), (corr_o, moment_o))):
        at = slice(p * width, (p + 1) * width)
        scaled = exact(inverse[p], exact(inverse[p], right[:, at], NN), TN)
        decoded = exact(scaled, left[p * rank : (p + 1) * rank], TN)
        weights.append(bases[:, at].T - step_size * decoded)
        moments.append(decay_rate * moment + lax.dynamic_slice_in_dim(decoded, start, rows, 1).T)
        errors.append(corr - decoded)
    return weights + errors + moments


def per_device(n_rep, n_shard, q_grad, o_grad, q_error, o_error, q_basis, o_basis, q_moment, o_moment, q_weight, o_weight, norm_grads, norm_moment, norm_weight):
    rank = q_basis.shape[1]
    size = q_grad.shape[1]
    flat = norm_grads.shape[-1]
    share = norm_moment.shape[0]
    row_count = q_moment.shape[0]
    device = lax.axis_index("rep") * n_shard + lax.axis_index("shard")
    drop = step_size * decay_rate

    base = jnp.concatenate([q_weight - drop * q_moment, o_weight - drop * o_moment], axis=1)
    gather = Gather(base, n_rep)

    grads = norm_grads.reshape(flat)
    own_grads = lax.dynamic_slice(grads, (device * share,), (share,))
    placed = lax.dynamic_update_slice(-step_size * grads, (norm_weight - drop * norm_moment) - step_size * own_grads, (device * share,))
    extra = jnp.concatenate([grads.reshape(-1, LANES), placed.reshape(-1, LANES)], axis=0)
    extra_rows = extra.shape[0]
    extra = jnp.pad(extra, ((0, 2 * rank - extra_rows), (0, 0)))

    place = lax.axis_index("shard")
    bits = [((place // mask) % 2).astype(jnp.int32).reshape(1) for mask in halves(n_shard)]
    corr_q, corr_o, keep, give = first((q_grad[0].T, o_grad[0].T), (q_error[0].T, o_error[0].T), q_basis.T, o_basis.T, bits[0])
    for sweep in range(ROUNDS):
        last = sweep == ROUNDS - 1
        ours, got = sum_over_all(keep, give, bits, n_rep, n_shard, gather, 2 * sweep)
        right, left, *extra_sum = right_of(ours, got, bits[0], corr_q, corr_o)
        if last and gather.paired:
            gather.tasks[3, 4] = (functools.partial(stack_of, count=row_count), left)
        gather.tasks[2 * sweep + 1, 1] = (inverse_of, left)
        right = sum_over(right, n_rep, gather, 2 * sweep + 1)
        inverse = gather.results[2 * sweep + 1, 1]
        if not last:
            keep, give = left_of(right, inverse, bits[0], corr_q, corr_o, [extra] if sweep == ROUNDS - 2 else [])
    extra_sum = extra_sum[0][:extra_rows]
    if gather.paired:
        stack, own = gather.results[3, 4]
        gather.insert([gather.blocks["turned_last"]], ["turned_last"])
        outs = finish(corr_q, corr_o, gather.rows, stack, inverse, right, own, q_moment, o_moment)
    else:
        outs = finish_plain(corr_q, corr_o, base, left, inverse, right, q_moment, o_moment)
    weight_q, weight_o, error_q, error_o, q_moment_new, o_moment_new = outs
    half = extra_rows // 2
    norm_sum = extra_sum[:half].reshape(flat)
    norm_weight_new = extra_sum[half:].reshape(flat)
    norm_moment_new = decay_rate * norm_moment + lax.dynamic_slice(norm_sum, (device * share,), (share,))
    return (
        weight_q.T,
        weight_o.T,
        q_moment_new,
        o_moment_new,
        error_q.T[None],
        error_o.T[None],
        norm_weight_new,
        norm_moment_new,
    )


def solution(mesh):
    n_rep, n_shard = mesh.shape["rep"], mesh.shape["shard"]

    def whole(*arrays):
        return per_device(n_rep, n_shard, *arrays)

    return jax.shard_map(
        whole,
        mesh=mesh,
        in_specs=(
            P("rep", None, "shard"),
            P("rep", None, "shard"),
            P("rep", None, "shard"),
            P("rep", None, "shard"),
            P("shard", None),
            P("shard", None),
            P("rep", "shard"),
            P("rep", "shard"),
            P("rep", "shard"),
            P("rep", "shard"),
            P("rep", "shard", None),
            P(("rep", "shard")),
            P(("rep", "shard")),
        ),
        out_specs=(
            P(None, "shard"),
            P(None, "shard"),
            P("rep", "shard"),
            P("rep", "shard"),
            P("rep", None, "shard"),
            P("rep", None, "shard"),
            P(),
            P(("rep", "shard")),
        ),
        check_vma=False,
    )
```

```python
import functools

import jax
import jax.numpy as jnp
from jax import lax
from jax.experimental import pallas as pl
from jax.experimental.pallas import tpu as pltpu
from jax.sharding import PartitionSpec as P

ROUNDS = 2
GROUP = 8
LANES = 128

highest = lax.Precision.HIGHEST
decay_rate = 0.9
step_size = 0.1
f32 = jnp.float32
bf16 = jnp.bfloat16
NN = (((1,), (0,)), ((), ()))
NT = (((1,), (1,)), ((), ()))
TN = (((0,), (0,)), ((), ()))

IN_HBM = pl.BlockSpec(memory_space=pltpu.HBM)
IN_VMEM = pl.BlockSpec(memory_space=pltpu.VMEM)
IN_SMEM = pl.BlockSpec(memory_space=pltpu.SMEM)
SMALL = pltpu.CompilerParams(vmem_limit_bytes=6 * 2**20)
LARGE = pltpu.CompilerParams(vmem_limit_bytes=9 * 2**20)
QUICK = pl.CostEstimate(flops=1000, bytes_accessed=1000, transcendentals=0)
SLOW = pl.CostEstimate(flops=1000, bytes_accessed=6_000_000, transcendentals=0)


def hold(space, *arrays):
    return [pltpu.with_memory_space_constraint(array, space) for array in arrays]


def exact(left, right, dims):
    return lax.dot_general(left, right, dims, precision=highest, preferred_element_type=f32)


def three(x):
    high = x.astype(bf16)
    rest = x - high.astype(f32)
    middle = rest.astype(bf16)
    low = (rest - middle.astype(f32)).astype(bf16)
    return high, middle, low


def stacked(left, right, dims):
    rows = left.shape[0]
    left_high, left_middle, left_low = three(left)
    right_high, right_middle, right_low = three(right)
    lefts = jnp.concatenate([left_high, left_middle, left_low], axis=0)
    of_high = lax.dot_general(lefts, right_high, dims, preferred_element_type=f32)
    of_middle = lax.dot_general(lefts[: 2 * rows], right_middle, dims, preferred_element_type=f32)
    of_low = lax.dot_general(left_high, right_low, dims, preferred_element_type=f32)
    small = (of_high[2 * rows :] + of_middle[rows:]) + of_low
    return of_high[:rows] + ((of_high[rows : 2 * rows] + of_middle[:rows]) + small)


def halves(count):
    masks = []
    mask = 1
    while mask < count:
        masks.append(mask)
        mask *= 2
    return masks


def swap(block, axis, mask, count):
    pairs = [(i, i ^ mask) for i in range(count)]
    return lax.ppermute(block, axis, pairs)


def sum_over(block, count, gather, stage):
    for mask in halves(count):
        block = gather.before(block, stage, mask)
        block = gather.start_tasks(block, stage, mask)
        block = block + gather.end_tasks(swap(block, "rep", mask, count), stage, mask)
        block = gather.after(block, stage, mask)
    return gather.before(block, stage, 0)


def sum_over_all(keep, give, shard, n_rep, n_shard, gather, stage):
    masks = halves(n_shard)
    for mask, after in zip(masks, masks[1:] + [None]):
        got = swap(give, "shard", mask, n_shard)
        if after is not None:
            keep, give = split(keep, got, shard, after)
            keep = gather.before(keep, stage, "core")
    part = sum_over(keep + got, n_rep, gather, stage)
    for mask in reversed(masks[1:]):
        part = join(part, swap(part, "shard", mask, n_shard), shard, mask)
        part = gather.before(part, stage, "x")
    return part, swap(part, "shard", masks[0], n_shard)


def is_high(place_ref, mask):
    return (place_ref[0] & mask) != 0


def split_kernel(mask, shard_ref, ours, got, keep, give):
    total = ours[...] + got[...]
    half = total.shape[0] // 2
    high = is_high(shard_ref, mask)
    keep[...] = jnp.where(high, total[half:], total[:half])
    give[...] = jnp.where(high, total[:half], total[half:])


def split(ours, got, shard, mask):
    half = pltpu.VMEM((ours.shape[0] // 2, ours.shape[1]), f32)
    return pl.pallas_call(
        functools.partial(split_kernel, mask),
        in_specs=[IN_SMEM, IN_VMEM, IN_VMEM],
        out_specs=[IN_VMEM] * 2,
        out_shape=[half, half],
        compiler_params=SMALL,
        cost_estimate=QUICK,
        name="split",
    )(shard, ours, got)


def joined(shard_ref, mask, ours, got):
    high = is_high(shard_ref, mask)
    return jnp.concatenate([jnp.where(high, got, ours), jnp.where(high, ours, got)], axis=0)


def join_kernel(mask, shard_ref, ours, got, whole):
    whole[...] = joined(shard_ref, mask, ours[...], got[...])


def join(ours, got, shard, mask):
    return pl.pallas_call(
        functools.partial(join_kernel, mask),
        in_specs=[IN_SMEM, IN_VMEM, IN_VMEM],
        out_specs=IN_VMEM,
        out_shape=pltpu.VMEM((2 * ours.shape[0], ours.shape[1]), f32),
        compiler_params=SMALL,
        cost_estimate=QUICK,
        name="join",
    )(shard, ours, got)


class Gather:
    PLAN = (
        ("near", "own", 2, None, (0, 2)),
        ("turned", "own", 1, (0, 1), (0, "x")),
        ("far_a", "own_a", 4, (0, 4), (1, 2)),
        ("turned_near", "near", 1, (1, 1), (2, "core")),
        ("far_b", "own_b", 4, (1, 4), (2, 2)),
        ("turned_far", "far", 1, (2, 1), (2, "x")),
        ("last", "far", 2, (2, 4), (3, 2)),
        ("turned_last", "last", 1, ("ahead", 3, 2), (3, 0)),
    )
    INSERTS = {
        (1, 4): ("own", "near"),
        (2, 1): ("turned", "turned_near"),
        (2, 4): ("far",),
        (3, 4): ("turned_far", "last"),
    }
    PLACES = {"own": 0, "turned": 1, "near": 2, "far": 4, "last": 6, "turned_near": 3, "turned_far": 5, "turned_last": 7}

    def __init__(self, own, own_a, own_b, place, count):
        self.count = count
        self.place = place
        self.blocks = {"own": own, "own_a": own_a, "own_b": own_b}
        self.paired = count == 8 and own.shape[0] % 16 == 0
        self.rows = None
        self.tasks = {}
        self.results = {}
        self.send(None)

    def send(self, point):
        if self.paired:
            for name, source, mask, after, _ in self.PLAN:
                if after == point:
                    if source == "far" and source not in self.blocks:
                        self.blocks["far"] = jnp.concatenate([self.blocks["far_a"], self.blocks["far_b"]], axis=0)
                    self.blocks[name] = swap(self.blocks[source], "rep", mask, self.count)

    def start_tasks(self, value, stage, mask):
        point = (stage, mask)
        if point in self.tasks:
            task, *inputs = self.tasks[point]
            value, *inputs = lax.optimization_barrier((value, *inputs))
            self.results[point] = task(*inputs)
        if self.paired and point in self.INSERTS:
            value, *blocks = lax.optimization_barrier((value, *(self.blocks[name] for name in self.INSERTS[point])))
            self.insert(blocks, self.INSERTS[point])
        return value

    def end_tasks(self, value, stage, mask):
        point = (stage, mask)
        if point in self.tasks:
            value, self.results[point] = lax.optimization_barrier((value, self.results[point]))
        if self.paired and point in self.INSERTS:
            value, self.rows = lax.optimization_barrier((value, self.rows))
        return value

    def insert(self, blocks, names):
        self.rows = insert(self.place, self.rows, blocks, [self.PLACES[name] for name in names], self.count)

    def before(self, value, stage, mask):
        if self.paired:
            for name, _, _, _, by in self.PLAN:
                if by == (stage, mask):
                    value, self.blocks[name] = lax.optimization_barrier((value, self.blocks[name]))
            self.send(("ahead", stage, mask))
        return value

    def after(self, value, stage, mask):
        if self.paired:
            for name, source, _, after, _ in self.PLAN:
                if after == (stage, mask) and source in self.blocks:
                    value, self.blocks[source] = lax.optimization_barrier((value, self.blocks[source]))
            self.send((stage, mask))
        return value


def insert_kernel(masks, place_ref, *refs):
    blocks, rows, out = refs[: len(masks)], refs[len(masks) : -1], refs[-1]
    if not rows:
        out[...] = jnp.zeros_like(out)
    height = out.shape[0]
    window = 2 * LANES
    lane = lax.broadcasted_iota(jnp.int32, (height, window), 1)
    for block, mask in zip(blocks, masks):
        count = block.shape[0]
        index = place_ref[0] ^ mask
        shift = index * (count - LANES)
        turned = jnp.concatenate([block[...].T, jnp.zeros((height, window - count), f32)], axis=1)
        turned = pltpu.roll(turned, shift, 1)
        at = pl.ds(pl.multiple_of(index * LANES, LANES), window)
        out[:, at] = jnp.where((lane >= shift) & (lane < shift + count), turned, out[:, at])


def insert(place, rows, blocks, masks, count):
    height, width = blocks[0].shape[1], blocks[0].shape[0] * count
    old = [] if rows is None else hold(pltpu.VMEM, rows)
    return pl.pallas_call(
        functools.partial(insert_kernel, masks),
        in_specs=[IN_SMEM] + [IN_VMEM] * (len(blocks) + len(old)),
        out_specs=IN_VMEM,
        out_shape=pltpu.VMEM((height, width), f32),
        input_output_aliases={1 + len(blocks): 0} if old else {},
        compiler_params=SMALL,
        cost_estimate=SLOW,
        name="insert",
    )(place, *blocks, *old)


def base_kernel(weight_q, moment_q, weight_o, moment_o, own, *parts):
    drop = step_size * decay_rate
    base = jnp.concatenate([weight_q[...] - drop * moment_q[...], weight_o[...] - drop * moment_o[...]], axis=1)
    own[...] = base
    half = base.shape[0] // 2
    for k, part in enumerate(parts):
        part[...] = base[k * half : (k + 1) * half]


def base_of(weight_q, moment_q, weight_o, moment_o):
    rows, width = weight_q.shape[0], 2 * weight_q.shape[1]
    shapes = [(rows, width)] + [(rows // 2, width)] * 2
    return pl.pallas_call(
        base_kernel,
        in_specs=[IN_VMEM] * 4,
        out_specs=[IN_VMEM] * 3,
        out_shape=[pltpu.VMEM(shape, f32) for shape in shapes],
        compiler_params=SMALL,
        cost_estimate=QUICK,
        name="base",
    )(weight_q, moment_q, weight_o, moment_o)


def window_of(n_shard, share, place_ref, shard_ref, lines):
    start = (place_ref[0] * n_shard + shard_ref[0]) * share
    row = lax.broadcasted_iota(jnp.int32, (lines, LANES), 0)
    lane = lax.broadcasted_iota(jnp.int32, (lines, LANES), 1)
    flat = row * LANES + lane
    return lax.rem(start, LANES), (flat >= start) & (flat < start + share)


def norm_in_kernel(n_shard, place_ref, shard_ref, grads, moment, weight, extra):
    lines, share = grads.shape[1] // LANES, moment.shape[1]
    shift, inside = window_of(n_shard, share, place_ref, shard_ref, lines)
    kept = weight[...] - step_size * decay_rate * moment[...]
    kept = jnp.concatenate([kept, jnp.zeros((1, LANES - share), f32)], axis=1)
    kept = pltpu.roll(jnp.broadcast_to(kept, (8, LANES)), shift, 1)[:1]
    extra[...] = jnp.zeros_like(extra)
    for line in range(lines):
        extra[line : line + 1, :] = grads[:, line * LANES : (line + 1) * LANES]
    extra[extra.shape[0] // 2 : extra.shape[0] // 2 + lines, :] = jnp.where(inside, kept, 0.0) - step_size * extra[:lines, :]


def norm_in(grads, moment, weight, rows, place, shard, n_shard):
    return pl.pallas_call(
        functools.partial(norm_in_kernel, n_shard),
        in_specs=[IN_SMEM] * 2 + [IN_VMEM] * 3,
        out_specs=IN_VMEM,
        out_shape=pltpu.VMEM((rows, LANES), f32),
        compiler_params=SMALL,
        cost_estimate=QUICK,
        name="norm_in",
    )(place, shard, grads, moment, weight)


def norm_out_kernel(n_shard, place_ref, shard_ref, extra, moment, new_moment, new_weight):
    lines, share = new_weight.shape[0], moment.shape[1]
    shift, inside = window_of(n_shard, share, place_ref, shard_ref, lines)
    total = jnp.sum(jnp.where(inside, extra[:lines, :], 0.0), axis=0, keepdims=True)
    total = pltpu.roll(jnp.broadcast_to(total, (8, LANES)), LANES - shift, 1)[:1, :share]
    new_moment[...] = decay_rate * moment[...] + total
    new_weight[...] = extra[extra.shape[0] // 2 : extra.shape[0] // 2 + lines, :]


def norm_out(extra, moment, lines, place, shard, n_shard):
    return pl.pallas_call(
        functools.partial(norm_out_kernel, n_shard),
        in_specs=[IN_SMEM] * 2 + [IN_VMEM] * 2,
        out_specs=[IN_VMEM] * 2,
        out_shape=[jax.ShapeDtypeStruct(moment.shape, f32), jax.ShapeDtypeStruct((lines, LANES), f32)],
        compiler_params=SMALL,
        cost_estimate=QUICK,
        name="norm_out",
    )(place, shard, extra, moment)


def first_kernel(chunks, place_ref, shard_ref, grad_q, grad_o, error_q, error_o, basis_q, basis_o, corr_q, corr_o, keep, give, buffer, bases, sems, base_sems):
    size = corr_q.shape[1]
    high = is_high(shard_ref, 1)
    lanes = size // chunks
    base_copies = [pltpu.make_async_copy(source, bases.at[k], base_sems.at[k]) for k, source in enumerate((basis_q, basis_o))]
    copies = {}
    for copy in base_copies:
        copy.start()
    for c in range(chunks):
        at = pl.ds(c * lanes, lanes)
        for j, source in enumerate((grad_q, error_q, grad_o, error_o)):
            copies[c, j] = pltpu.make_async_copy(source.at[:, at], buffer.at[j, :, at], sems.at[c, j])
            copies[c, j].start()
    for copy in base_copies:
        copy.wait()
    for c in range(chunks):
        at = pl.ds(c * lanes, lanes)
        parts = []
        for k, corr in enumerate((corr_q, corr_o)):
            copies[c, 2 * k].wait()
            copies[c, 2 * k + 1].wait()
            total = buffer[2 * k, :, at] + buffer[2 * k + 1, :, at]
            corr[:, at] = total
            parts.append(stacked(bases[k], total, NN))
        keep[:, at] = jnp.where(high, parts[1], parts[0])
        give[:, at] = jnp.where(high, parts[0], parts[1])


def first(grads, errors, basis_q, basis_o, place, shard):
    width, size = grads[0].shape
    rank = basis_q.shape[0]
    chunks = 3 if size % (3 * LANES) == 0 else 1
    return pl.pallas_call(
        functools.partial(first_kernel, chunks),
        in_specs=[IN_SMEM] * 2 + [IN_HBM] * 6,
        out_specs=[IN_VMEM] * 4,
        out_shape=[pltpu.VMEM((width, size), f32)] * 2 + [pltpu.VMEM((rank, size), f32)] * 2,
        scratch_shapes=[
            pltpu.VMEM((4, width, size), f32),
            pltpu.VMEM((2, rank, width), f32),
            pltpu.SemaphoreType.DMA((chunks, 4)),
            pltpu.SemaphoreType.DMA((2,)),
        ],
        compiler_params=LARGE,
        name="first",
    )(place, shard, *hold(pltpu.HBM, *grads, *errors, basis_q, basis_o))


def right_kernel(shard_ref, ours, got, corr_q, corr_o, right, left, *extra):
    rank, size = ours.shape[0], corr_q.shape[1]
    whole = joined(shard_ref, 1, ours[...], got[...])
    left[...] = whole[:, :size]
    if extra:
        extra[0][...] = whole[:, size:]
    right[...] = jnp.concatenate([stacked(whole[:rank, :size], corr_q[...], NT), stacked(whole[rank:, :size], corr_o[...], NT)], axis=1)


def right_of(ours, got, shard, corr_q, corr_o):
    rank = ours.shape[0]
    width, size = corr_q.shape
    beside = ours.shape[1] - size
    shapes = [(rank, 2 * width), (2 * rank, size)] + ([(2 * rank, beside)] if beside else [])
    return pl.pallas_call(
        right_kernel,
        in_specs=[IN_SMEM] + [IN_VMEM] * 4,
        out_specs=[IN_VMEM] * len(shapes),
        out_shape=[pltpu.VMEM(shape, f32) for shape in shapes],
        compiler_params=SMALL,
        cost_estimate=QUICK,
        name="right",
    )(shard, ours, got, *hold(pltpu.VMEM, corr_q, corr_o))


def left_kernel(shard_ref, right, inverse, corr_q, corr_o, *refs):
    extra, keep, give = refs[:-2], refs[-2], refs[-1]
    rank, width = right.shape[0], right.shape[1] // 2
    size = corr_q.shape[1]
    high = is_high(shard_ref, 1)
    basis_q = exact(inverse[0], right[:, :width], NN)
    basis_o = exact(inverse[1], right[:, width:], NN)
    part_q = stacked(basis_q, corr_q[...], NN)
    part_o = stacked(basis_o, corr_o[...], NN)
    keep[:, :size] = jnp.where(high, part_o, part_q)
    give[:, :size] = jnp.where(high, part_q, part_o)
    if extra:
        low_rows, high_rows = extra[0][:rank, :], extra[0][rank:, :]
        keep[:, size:] = jnp.where(high, high_rows, low_rows)
        give[:, size:] = jnp.where(high, low_rows, high_rows)


def left_of(right, inverse, shard, corr_q, corr_o, extra):
    rank, size = right.shape[0], corr_q.shape[1]
    half = pltpu.VMEM((rank, size + sum(array.shape[1] for array in extra)), f32)
    return pl.pallas_call(
        left_kernel,
        in_specs=[IN_SMEM] + [IN_VMEM] * (4 + len(extra)),
        out_specs=[IN_VMEM] * 2,
        out_shape=[half, half],
        compiler_params=SMALL,
        cost_estimate=QUICK,
        name="left",
    )(shard, right, inverse, *hold(pltpu.VMEM, corr_q, corr_o), *extra)


def eliminate(gram_q, gram_o, rank):
    width = 4 * rank
    lane = lax.broadcasted_iota(jnp.int32, (rank, width), 1)
    row = lax.broadcasted_iota(jnp.int32, (rank, width), 0)
    square = (rank, rank)
    eye = (lax.broadcasted_iota(jnp.int32, square, 0) == lax.broadcasted_iota(jnp.int32, square, 1)).astype(f32)
    work = jnp.concatenate([gram_q, eye, gram_o, eye], axis=1)
    first_half = lane < 2 * rank
    scale = jnp.ones((rank, width), f32)
    for base in range(0, rank, GROUP):
        columns = []
        for k in range(base, base + GROUP):
            of_q = jnp.broadcast_to(work[:, k : k + 1], (rank, width))
            of_o = jnp.broadcast_to(work[:, 2 * rank + k : 2 * rank + k + 1], (rank, width))
            columns.append(jnp.where(first_half, of_q, of_o))
        for j in range(GROUP):
            k = base + j
            pivot = columns[j][k : k + 1]
            factor = jnp.where(row > k, columns[j] * (1.0 / pivot), 0.0)
            scale = jnp.where(row == k, pivot, scale)
            for i in range(j + 1, GROUP):
                columns[i] = columns[i] - factor * columns[i][k : k + 1]
            work = work - factor * work[k : k + 1]
    work = work * lax.rsqrt(scale)
    return work[:, rank : 2 * rank], work[:, 3 * rank :]


def inverse_kernel(left, out):
    rank, size = out.shape[1], left.shape[1]
    left_q, left_o = left[:rank, :], left[rank:, :]
    out[0], out[1] = eliminate(exact(left_q, left_q, NT), exact(left_o, left_o, NT), rank)


def inverse_of(left):
    rank = left.shape[0] // 2
    return pl.pallas_call(
        inverse_kernel,
        out_shape=pltpu.VMEM((2, rank, rank), f32),
        compiler_params=SMALL,
        cost_estimate=SLOW,
        name="inverse",
    )(left)


def stack_kernel(place_ref, left, stack, own):
    rank = left.shape[0] // 2
    for p in range(2):
        high, middle, low = three(left[p * rank : (p + 1) * rank, :])
        stack[p] = jnp.concatenate([high, middle, low, high, middle, high], axis=0)
    count = own.shape[1]
    index = place_ref[0]
    window = left[:, pl.ds(pl.multiple_of(index * LANES, LANES), 2 * LANES)]
    own[...] = pltpu.roll(window, 2 * LANES - index * (count - LANES), 1)[:, :count]


def stack_of(left, place, count):
    rank, size = left.shape[0] // 2, left.shape[1]
    return pl.pallas_call(
        stack_kernel,
        in_specs=[IN_SMEM, IN_VMEM],
        out_specs=[IN_VMEM] * 2,
        out_shape=[pltpu.VMEM((2, 6 * rank, size), bf16), pltpu.VMEM((2 * rank, count), f32)],
        compiler_params=SMALL,
        cost_estimate=SLOW,
        name="stack",
    )(place, left)


def finish_kernel(chunks, corr_q, corr_o, rows, stack, inverse, right, own, moment_q, moment_o, *refs):
    outs, buffer, new_moments, sems, moment_sems = refs[:6], refs[6], refs[7], refs[8], refs[9]
    rank, width = inverse.shape[1], moment_q.shape[1]
    height = width // chunks
    copies = []
    for p, corr in enumerate((corr_q, corr_o)):
        factor = right[:, p * width : (p + 1) * width]
        scaled = exact(inverse[p], exact(inverse[p], factor, NN), TN)
        high, middle, low = three(scaled.T)
        lefts = jnp.concatenate([high, high, high, middle, middle, low], axis=1)
        for c in range(chunks):
            at = pl.ds(c * height, height)
            decoded = lax.dot_general(lefts[c * height : (c + 1) * height], stack[p], NN, preferred_element_type=f32)
            buffer[p, at, :] = rows[pl.ds(p * width + c * height, height), :] - step_size * decoded
            buffer[2 + p, at, :] = corr[at, :] - decoded
            for k in (p, 2 + p):
                copies.append(pltpu.make_async_copy(buffer.at[k, at, :], outs[k].at[at, :], sems.at[k, c]))
                copies[-1].start()
    for p, moment in enumerate((moment_q, moment_o)):
        factor = right[:, p * width : (p + 1) * width]
        scaled = exact(inverse[p], exact(inverse[p], factor, NN), TN)
        new_moments[p] = decay_rate * moment[...] + exact(own[p * rank : (p + 1) * rank, :], scaled, TN)
        copies.append(pltpu.make_async_copy(new_moments.at[p], outs[4 + p], moment_sems.at[p]))
        copies[-1].start()
    for copy in copies:
        copy.wait()


def finish(corr_q, corr_o, rows, stack, inverse, right, own, moment_q, moment_o):
    width, size = corr_q.shape
    chunks = 3
    return pl.pallas_call(
        functools.partial(finish_kernel, chunks),
        in_specs=[IN_VMEM] * 9,
        out_specs=[IN_HBM] * 6,
        out_shape=[pltpu.HBM((width, size), f32)] * 4 + [pltpu.HBM(moment_q.shape, f32)] * 2,
        scratch_shapes=[
            pltpu.VMEM((4, width, size), f32),
            pltpu.VMEM((2,) + moment_q.shape, f32),
            pltpu.SemaphoreType.DMA((4, chunks)),
            pltpu.SemaphoreType.DMA((2,)),
        ],
        compiler_params=LARGE,
        name="finish",
    )(*hold(pltpu.VMEM, corr_q, corr_o, rows), stack, inverse, right, own, moment_q, moment_o)


def finish_plain(corr_q, corr_o, base, left, inverse, right, moment_q, moment_o):
    rank, width = inverse.shape[1], moment_q.shape[1]
    rows = moment_q.shape[0]
    start = lax.axis_index("rep") * rows
    bases = lax.all_gather(base, "rep", axis=0, tiled=True)
    weights, moments, errors = [], [], []
    for p, (corr, moment) in enumerate(((corr_q, moment_q), (corr_o, moment_o))):
        at = slice(p * width, (p + 1) * width)
        scaled = exact(inverse[p], exact(inverse[p], right[:, at], NN), TN)
        decoded = exact(scaled, left[p * rank : (p + 1) * rank], TN)
        weights.append(bases[:, at].T - step_size * decoded)
        moments.append(decay_rate * moment + lax.dynamic_slice_in_dim(decoded, start, rows, 1).T)
        errors.append(corr - decoded)
    return weights + errors + moments


def per_device(n_rep, n_shard, q_grad, o_grad, q_error, o_error, q_basis, o_basis, q_moment, o_moment, q_weight, o_weight, norm_grads, norm_moment, norm_weight):
    rank = q_basis.shape[1]
    size = q_grad.shape[1]
    flat = norm_grads.shape[-1]
    row_count = q_moment.shape[0]
    place = lax.axis_index("rep").astype(jnp.int32).reshape(1)
    shard = lax.axis_index("shard").astype(jnp.int32).reshape(1)

    gather = Gather(*base_of(q_weight, q_moment, o_weight, o_moment), place, n_rep)
    norm_moment, norm_weight = norm_moment.reshape(1, -1), norm_weight.reshape(1, -1)
    extra = norm_in(norm_grads[0], norm_moment, norm_weight, 2 * rank, place, shard, n_shard)
    corr_q, corr_o, keep, give = first((q_grad[0].T, o_grad[0].T), (q_error[0].T, o_error[0].T), q_basis.T, o_basis.T, place, shard)
    for sweep in range(ROUNDS):
        last = sweep == ROUNDS - 1
        ours, got = sum_over_all(keep, give, shard, n_rep, n_shard, gather, 2 * sweep)
        right, left, *extra_sum = right_of(ours, got, shard, corr_q, corr_o)
        if last and gather.paired:
            gather.tasks[3, 4] = (functools.partial(stack_of, count=row_count), left, place)
        gather.tasks[2 * sweep + 1, 1] = (inverse_of, left)
        right = sum_over(right, n_rep, gather, 2 * sweep + 1)
        inverse = gather.results[2 * sweep + 1, 1]
        if not last:
            keep, give = left_of(right, inverse, shard, corr_q, corr_o, [extra] if sweep == ROUNDS - 2 else [])
    norm_moment_new, norm_weight_new = norm_out(extra_sum[0], norm_moment, flat // LANES, place, shard, n_shard)
    if gather.paired:
        stack, own = gather.results[3, 4]
        gather.insert([gather.blocks["turned_last"]], ["turned_last"])
        outs = finish(corr_q, corr_o, gather.rows, stack, inverse, right, own, q_moment, o_moment)
    else:
        outs = finish_plain(corr_q, corr_o, gather.blocks["own"], left, inverse, right, q_moment, o_moment)
    weight_q, weight_o, error_q, error_o, q_moment_new, o_moment_new = outs
    return (
        weight_q.T,
        weight_o.T,
        q_moment_new,
        o_moment_new,
        error_q.T[None],
        error_o.T[None],
        norm_weight_new.reshape(flat),
        norm_moment_new.reshape(-1),
    )


def solution(mesh):
    n_rep, n_shard = mesh.shape["rep"], mesh.shape["shard"]

    def whole(*arrays):
        return per_device(n_rep, n_shard, *arrays)

    return jax.shard_map(
        whole,
        mesh=mesh,
        in_specs=(
            P("rep", None, "shard"),
            P("rep", None, "shard"),
            P("rep", None, "shard"),
            P("rep", None, "shard"),
            P("shard", None),
            P("shard", None),
            P("rep", "shard"),
            P("rep", "shard"),
            P("rep", "shard"),
            P("rep", "shard"),
            P("rep", "shard", None),
            P(("rep", "shard")),
            P(("rep", "shard")),
        ),
        out_specs=(
            P(None, "shard"),
            P(None, "shard"),
            P("rep", "shard"),
            P("rep", "shard"),
            P("rep", None, "shard"),
            P("rep", None, "shard"),
            P(),
            P(("rep", "shard")),
        ),
        check_vma=False,
    )
```

```python
import functools

import jax
import jax.numpy as jnp
from jax import lax
from jax.experimental import pallas as pl
from jax.experimental.pallas import tpu as pltpu
from jax.sharding import PartitionSpec as P

ROUNDS = 2
GROUP = 8
LANES = 128
BESIDE = 8

highest = lax.Precision.HIGHEST
decay_rate = 0.9
step_size = 0.1
f32 = jnp.float32
bf16 = jnp.bfloat16
NN = (((1,), (0,)), ((), ()))
NT = (((1,), (1,)), ((), ()))
TN = (((0,), (0,)), ((), ()))

IN_HBM = pl.BlockSpec(memory_space=pltpu.HBM)
IN_VMEM = pl.BlockSpec(memory_space=pltpu.VMEM)
IN_SMEM = pl.BlockSpec(memory_space=pltpu.SMEM)
SMALL = pltpu.CompilerParams(vmem_limit_bytes=6 * 2**20)
LARGE = pltpu.CompilerParams(vmem_limit_bytes=9 * 2**20)
QUICK = pl.CostEstimate(flops=1000, bytes_accessed=1000, transcendentals=0)
SLOW = pl.CostEstimate(flops=1000, bytes_accessed=6_000_000, transcendentals=0)


def hold(space, *arrays):
    return [pltpu.with_memory_space_constraint(array, space) for array in arrays]


def exact(left, right, dims):
    return lax.dot_general(left, right, dims, precision=highest, preferred_element_type=f32)


def three(x):
    high = x.astype(bf16)
    rest = x - high.astype(f32)
    middle = rest.astype(bf16)
    low = (rest - middle.astype(f32)).astype(bf16)
    return high, middle, low


def stacked(left, right, dims):
    rows = left.shape[0]
    left_high, left_middle, left_low = three(left)
    right_high, right_middle, right_low = three(right)
    lefts = jnp.concatenate([left_high, left_middle, left_low], axis=0)
    of_high = lax.dot_general(lefts, right_high, dims, preferred_element_type=f32)
    of_middle = lax.dot_general(lefts[: 2 * rows], right_middle, dims, preferred_element_type=f32)
    of_low = lax.dot_general(left_high, right_low, dims, preferred_element_type=f32)
    small = (of_high[2 * rows :] + of_middle[rows:]) + of_low
    return of_high[:rows] + ((of_high[rows : 2 * rows] + of_middle[:rows]) + small)


def halves(count):
    masks = []
    mask = 1
    while mask < count:
        masks.append(mask)
        mask *= 2
    return masks


def swap(block, axis, mask, count):
    pairs = [(i, i ^ mask) for i in range(count)]
    return lax.ppermute(block, axis, pairs)


def sum_over(block, count, gather, stage):
    for mask in halves(count):
        block = gather.before(block, stage, mask)
        block = gather.start_tasks(block, stage, mask)
        block = block + gather.end_tasks(swap(block, "rep", mask, count), stage, mask)
        block = gather.after(block, stage, mask)
    return gather.before(block, stage, 0)


def sum_over_all(keep, give, shard, n_rep, n_shard, gather, stage):
    masks = halves(n_shard)
    for mask, after in zip(masks, masks[1:] + [None]):
        got = swap(give, "shard", mask, n_shard)
        if after is not None:
            keep, give = split(keep, got, shard, after)
            keep = gather.after(gather.before(keep, stage, "core"), stage, "core")
    part = sum_over(keep + got, n_rep, gather, stage)
    for mask in reversed(masks[1:]):
        part = gather.start_tasks(part, stage, "x")
        got = gather.end_tasks(swap(part, "shard", mask, n_shard), stage, "x")
        part = gather.before(join(part, got, shard, mask), stage, "joined")
    return part, swap(part, "shard", masks[0], n_shard)


def is_high(place_ref, mask):
    return (place_ref[0] & mask) != 0


def split_kernel(mask, shard_ref, ours, got, keep, give):
    total = ours[...] + got[...]
    half = total.shape[0] // 2
    high = is_high(shard_ref, mask)
    keep[...] = jnp.where(high, total[half:], total[:half])
    give[...] = jnp.where(high, total[:half], total[half:])


def split(ours, got, shard, mask):
    half = pltpu.VMEM((ours.shape[0] // 2, ours.shape[1]), f32)
    return pl.pallas_call(
        functools.partial(split_kernel, mask),
        in_specs=[IN_SMEM, IN_VMEM, IN_VMEM],
        out_specs=[IN_VMEM] * 2,
        out_shape=[half, half],
        compiler_params=SMALL,
        cost_estimate=QUICK,
        name="split",
    )(shard, ours, got)


def joined(shard_ref, mask, ours, got):
    high = is_high(shard_ref, mask)
    return jnp.concatenate([jnp.where(high, got, ours), jnp.where(high, ours, got)], axis=0)


def join_kernel(mask, shard_ref, ours, got, whole):
    whole[...] = joined(shard_ref, mask, ours[...], got[...])


def join(ours, got, shard, mask):
    return pl.pallas_call(
        functools.partial(join_kernel, mask),
        in_specs=[IN_SMEM, IN_VMEM, IN_VMEM],
        out_specs=IN_VMEM,
        out_shape=pltpu.VMEM((2 * ours.shape[0], ours.shape[1]), f32),
        compiler_params=SMALL,
        cost_estimate=QUICK,
        name="join",
    )(shard, ours, got)


class Gather:
    PLAN = (
        ("far_a", "own_a", 4, (0, "core"), (0, 4)),
        ("turned", "own", 1, (0, 1), (1, 1)),
        ("near", "own", 2, (0, 4), (1, 4)),
        ("turned_near", "near", 1, ("beside", 1, 4), (2, 2)),
        ("far_b", "own_b", 4, (2, "core"), (2, 4)),
        ("turned_far", "far", 1, (2, 2), (3, 1)),
        ("last", "far", 2, (2, 4), (3, 2)),
        ("turned_last", "last", 1, ("beside", 3, 2), (3, 0)),
    )
    INSERTS = {
        (1, 4): ("own",),
        (2, 1): ("near",),
        (2, 2): ("turned",),
        (2, 4): ("turned_near",),
        (2, "x"): ("far",),
        (3, 4): ("turned_far", "last"),
    }
    PLACES = {"own": 0, "turned": 1, "near": 2, "far": 4, "last": 6, "turned_near": 3, "turned_far": 5, "turned_last": 7}

    def __init__(self, own, own_a, own_b, place, count):
        self.count = count
        self.place = place
        self.blocks = {"own": own, "own_a": own_a, "own_b": own_b}
        self.paired = count == 8 and own.shape[0] % 16 == 0
        self.rows = None
        self.tasks = {}
        self.results = {}
        self.send(None)

    def send(self, point):
        if self.paired:
            for name, source, mask, after, _ in self.PLAN:
                if after == point:
                    if source == "far" and source not in self.blocks:
                        self.blocks["far"] = jnp.concatenate([self.blocks["far_a"], self.blocks["far_b"][BESIDE:]], axis=0)
                    self.blocks[name] = swap(self.blocks[source], "rep", mask, self.count)

    def start_tasks(self, value, stage, mask):
        point = (stage, mask)
        if point in self.tasks:
            task, *inputs = self.tasks[point]
            value, *inputs = lax.optimization_barrier((value, *inputs))
            self.results[point] = task(*inputs)
        if self.paired and point in self.INSERTS:
            value, *blocks = lax.optimization_barrier((value, *(self.blocks[name] for name in self.INSERTS[point])))
            self.insert(blocks, self.INSERTS[point])
        if self.paired:
            for name, source, _, after, _ in self.PLAN:
                if after == ("beside",) + point:
                    if point in self.INSERTS:
                        self.rows, self.blocks[source] = lax.optimization_barrier((self.rows, self.blocks[source]))
                    else:
                        self.results[point], self.blocks[source] = lax.optimization_barrier((self.results[point], self.blocks[source]))
            self.send(("beside",) + point)
        return value

    def end_tasks(self, value, stage, mask):
        point = (stage, mask)
        if point in self.tasks:
            value, self.results[point] = lax.optimization_barrier((value, self.results[point]))
        if self.paired and point in self.INSERTS:
            value, self.rows = lax.optimization_barrier((value, self.rows))
        return value

    def insert(self, blocks, names):
        self.rows = insert(self.place, self.rows, blocks, [self.PLACES[name] for name in names], self.count)

    def before(self, value, stage, mask):
        if self.paired:
            for name, _, _, _, by in self.PLAN:
                if by == (stage, mask):
                    value, self.blocks[name] = lax.optimization_barrier((value, self.blocks[name]))
        return value

    def after(self, value, stage, mask):
        if self.paired:
            for name, source, _, after, _ in self.PLAN:
                if after == (stage, mask) and source in self.blocks:
                    value, self.blocks[source] = lax.optimization_barrier((value, self.blocks[source]))
            self.send((stage, mask))
        return value


def insert_kernel(masks, place_ref, *refs):
    blocks, rows, out = refs[: len(masks)], refs[len(masks) : -1], refs[-1]
    if not rows:
        out[...] = jnp.zeros_like(out)
    height = out.shape[0]
    window = 2 * LANES
    lane = lax.broadcasted_iota(jnp.int32, (height, window), 1)
    for block, mask in zip(blocks, masks):
        count = block.shape[0]
        index = place_ref[0] ^ mask
        shift = index * (count - LANES)
        turned = jnp.concatenate([block[...].T, jnp.zeros((height, window - count), f32)], axis=1)
        turned = pltpu.roll(turned, shift, 1)
        at = pl.ds(pl.multiple_of(index * LANES, LANES), window)
        out[:, at] = jnp.where((lane >= shift) & (lane < shift + count), turned, out[:, at])


def insert(place, rows, blocks, masks, count):
    height, width = blocks[0].shape[1], blocks[0].shape[0] * count
    old = [] if rows is None else hold(pltpu.VMEM, rows)
    return pl.pallas_call(
        functools.partial(insert_kernel, masks),
        in_specs=[IN_SMEM] + [IN_VMEM] * (len(blocks) + len(old)),
        out_specs=IN_VMEM,
        out_shape=pltpu.VMEM((height, width), f32),
        input_output_aliases={1 + len(blocks): 0} if old else {},
        compiler_params=SMALL,
        cost_estimate=SLOW,
        name="insert",
    )(place, *blocks, *old)


def base_kernel(weight_q, moment_q, weight_o, moment_o, own, *parts):
    drop = step_size * decay_rate
    base = jnp.concatenate([weight_q[...] - drop * moment_q[...], weight_o[...] - drop * moment_o[...]], axis=1)
    own[...] = base
    rows = base.shape[0]
    first_part, second_part = parts
    first_part[...] = base[: first_part.shape[0]]
    second_part[...] = base[rows - second_part.shape[0] :]


def base_of(weight_q, moment_q, weight_o, moment_o):
    rows, width = weight_q.shape[0], 2 * weight_q.shape[1]
    half = rows // 2
    shapes = [(rows, width), (half, width), (rows - half + BESIDE * (half > BESIDE), width)]
    return pl.pallas_call(
        base_kernel,
        in_specs=[IN_VMEM] * 4,
        out_specs=[IN_VMEM] * 3,
        out_shape=[pltpu.VMEM(shape, f32) for shape in shapes],
        compiler_params=SMALL,
        cost_estimate=QUICK,
        name="base",
    )(weight_q, moment_q, weight_o, moment_o)


def window_of(n_shard, share, place_ref, shard_ref, lines):
    start = (place_ref[0] * n_shard + shard_ref[0]) * share
    row = lax.broadcasted_iota(jnp.int32, (lines, LANES), 0)
    lane = lax.broadcasted_iota(jnp.int32, (lines, LANES), 1)
    flat = row * LANES + lane
    return lax.rem(start, LANES), (flat >= start) & (flat < start + share)


def norm_in_kernel(n_shard, place_ref, shard_ref, grads, moment, weight, extra):
    lines, share = grads.shape[1] // LANES, moment.shape[1]
    shift, inside = window_of(n_shard, share, place_ref, shard_ref, lines)
    kept = weight[...] - step_size * decay_rate * moment[...]
    kept = jnp.concatenate([kept, jnp.zeros((1, LANES - share), f32)], axis=1)
    kept = pltpu.roll(jnp.broadcast_to(kept, (8, LANES)), shift, 1)[:1]
    extra[...] = jnp.zeros_like(extra)
    for line in range(lines):
        extra[line : line + 1, :] = grads[:, line * LANES : (line + 1) * LANES]
    extra[extra.shape[0] // 2 : extra.shape[0] // 2 + lines, :] = jnp.where(inside, kept, 0.0) - step_size * extra[:lines, :]


def norm_in(grads, moment, weight, rows, place, shard, n_shard):
    return pl.pallas_call(
        functools.partial(norm_in_kernel, n_shard),
        in_specs=[IN_SMEM] * 2 + [IN_VMEM] * 3,
        out_specs=IN_VMEM,
        out_shape=pltpu.VMEM((rows, LANES), f32),
        compiler_params=SMALL,
        cost_estimate=QUICK,
        name="norm_in",
    )(place, shard, grads, moment, weight)


def norm_out_kernel(n_shard, place_ref, shard_ref, extra, moment, new_moment, new_weight):
    lines, share = new_weight.shape[0], moment.shape[1]
    shift, inside = window_of(n_shard, share, place_ref, shard_ref, lines)
    total = jnp.sum(jnp.where(inside, extra[:lines, :], 0.0), axis=0, keepdims=True)
    total = pltpu.roll(jnp.broadcast_to(total, (8, LANES)), LANES - shift, 1)[:1, :share]
    new_moment[...] = decay_rate * moment[...] + total
    new_weight[...] = extra[extra.shape[0] // 2 : extra.shape[0] // 2 + lines, :]


def norm_out(extra, moment, lines, place, shard, n_shard):
    return pl.pallas_call(
        functools.partial(norm_out_kernel, n_shard),
        in_specs=[IN_SMEM] * 2 + [IN_VMEM] * 2,
        out_specs=[IN_VMEM] * 2,
        out_shape=[jax.ShapeDtypeStruct(moment.shape, f32), jax.ShapeDtypeStruct((lines, LANES), f32)],
        compiler_params=SMALL,
        cost_estimate=QUICK,
        name="norm_out",
    )(place, shard, extra, moment)


def first_kernel(chunks, place_ref, shard_ref, grad_q, grad_o, error_q, error_o, basis_q, basis_o, corr_q, corr_o, keep, give, buffer, bases, sems, base_sems):
    size = corr_q.shape[1]
    high = is_high(shard_ref, 1)
    lanes = size // chunks
    base_copies = [pltpu.make_async_copy(source, bases.at[k], base_sems.at[k]) for k, source in enumerate((basis_q, basis_o))]
    copies = {}
    for copy in base_copies:
        copy.start()
    for c in range(chunks):
        at = pl.ds(c * lanes, lanes)
        for j, source in enumerate((grad_q, error_q, grad_o, error_o)):
            copies[c, j] = pltpu.make_async_copy(source.at[:, at], buffer.at[j, :, at], sems.at[c, j])
            copies[c, j].start()
    for copy in base_copies:
        copy.wait()
    for c in range(chunks):
        at = pl.ds(c * lanes, lanes)
        parts = []
        for k, corr in enumerate((corr_q, corr_o)):
            copies[c, 2 * k].wait()
            copies[c, 2 * k + 1].wait()
            total = buffer[2 * k, :, at] + buffer[2 * k + 1, :, at]
            corr[:, at] = total
            parts.append(stacked(bases[k], total, NN))
        keep[:, at] = jnp.where(high, parts[1], parts[0])
        give[:, at] = jnp.where(high, parts[0], parts[1])


def first(grads, errors, basis_q, basis_o, place, shard):
    width, size = grads[0].shape
    rank = basis_q.shape[0]
    chunks = 3 if size % (3 * LANES) == 0 else 1
    return pl.pallas_call(
        functools.partial(first_kernel, chunks),
        in_specs=[IN_SMEM] * 2 + [IN_HBM] * 6,
        out_specs=[IN_VMEM] * 4,
        out_shape=[pltpu.VMEM((width, size), f32)] * 2 + [pltpu.VMEM((rank, size), f32)] * 2,
        scratch_shapes=[
            pltpu.VMEM((4, width, size), f32),
            pltpu.VMEM((2, rank, width), f32),
            pltpu.SemaphoreType.DMA((chunks, 4)),
            pltpu.SemaphoreType.DMA((2,)),
        ],
        compiler_params=LARGE,
        name="first",
    )(place, shard, *hold(pltpu.HBM, *grads, *errors, basis_q, basis_o))


def right_kernel(shard_ref, ours, got, corr_q, corr_o, right, left, *extra):
    rank, size = ours.shape[0], corr_q.shape[1]
    whole = joined(shard_ref, 1, ours[...], got[...])
    left[...] = whole[:, :size]
    if extra:
        extra[0][...] = whole[:, size:]
    right[...] = jnp.concatenate([stacked(whole[:rank, :size], corr_q[...], NT), stacked(whole[rank:, :size], corr_o[...], NT)], axis=1)


def right_of(ours, got, shard, corr_q, corr_o):
    rank = ours.shape[0]
    width, size = corr_q.shape
    beside = ours.shape[1] - size
    shapes = [(rank, 2 * width), (2 * rank, size)] + ([(2 * rank, beside)] if beside else [])
    return pl.pallas_call(
        right_kernel,
        in_specs=[IN_SMEM] + [IN_VMEM] * 4,
        out_specs=[IN_VMEM] * len(shapes),
        out_shape=[pltpu.VMEM(shape, f32) for shape in shapes],
        compiler_params=SMALL,
        cost_estimate=QUICK,
        name="right",
    )(shard, ours, got, *hold(pltpu.VMEM, corr_q, corr_o))


def left_kernel(shard_ref, right, inverse, corr_q, corr_o, *refs):
    extra, keep, give = refs[:-2], refs[-2], refs[-1]
    rank, width = right.shape[0], right.shape[1] // 2
    size = corr_q.shape[1]
    high = is_high(shard_ref, 1)
    basis_q = exact(inverse[0], right[:, :width], NN)
    basis_o = exact(inverse[1], right[:, width:], NN)
    part_q = stacked(basis_q, corr_q[...], NN)
    part_o = stacked(basis_o, corr_o[...], NN)
    keep[:, :size] = jnp.where(high, part_o, part_q)
    give[:, :size] = jnp.where(high, part_q, part_o)
    if extra:
        low_rows, high_rows = extra[0][:rank, :], extra[0][rank:, :]
        keep[:, size:] = jnp.where(high, high_rows, low_rows)
        give[:, size:] = jnp.where(high, low_rows, high_rows)


def left_of(right, inverse, shard, corr_q, corr_o, extra):
    rank, size = right.shape[0], corr_q.shape[1]
    half = pltpu.VMEM((rank, size + sum(array.shape[1] for array in extra)), f32)
    return pl.pallas_call(
        left_kernel,
        in_specs=[IN_SMEM] + [IN_VMEM] * (4 + len(extra)),
        out_specs=[IN_VMEM] * 2,
        out_shape=[half, half],
        compiler_params=SMALL,
        cost_estimate=QUICK,
        name="left",
    )(shard, right, inverse, *hold(pltpu.VMEM, corr_q, corr_o), *extra)


def eliminate(gram_q, gram_o, rank):
    width = 4 * rank
    lane = lax.broadcasted_iota(jnp.int32, (rank, width), 1)
    row = lax.broadcasted_iota(jnp.int32, (rank, width), 0)
    square = (rank, rank)
    eye = (lax.broadcasted_iota(jnp.int32, square, 0) == lax.broadcasted_iota(jnp.int32, square, 1)).astype(f32)
    work = jnp.concatenate([gram_q, eye, gram_o, eye], axis=1)
    first_half = lane < 2 * rank
    scale = jnp.ones((rank, width), f32)
    for base in range(0, rank, GROUP):
        columns = []
        for k in range(base, base + GROUP):
            of_q = jnp.broadcast_to(work[:, k : k + 1], (rank, width))
            of_o = jnp.broadcast_to(work[:, 2 * rank + k : 2 * rank + k + 1], (rank, width))
            columns.append(jnp.where(first_half, of_q, of_o))
        for j in range(GROUP):
            k = base + j
            pivot = columns[j][k : k + 1]
            factor = jnp.where(row > k, columns[j] * (1.0 / pivot), 0.0)
            scale = jnp.where(row == k, pivot, scale)
            for i in range(j + 1, GROUP):
                columns[i] = columns[i] - factor * columns[i][k : k + 1]
            work = work - factor * work[k : k + 1]
    work = work * lax.rsqrt(scale)
    return work[:, rank : 2 * rank], work[:, 3 * rank :]


def inverse_kernel(left, out):
    rank, size = out.shape[1], left.shape[1]
    left_q, left_o = left[:rank, :], left[rank:, :]
    out[0], out[1] = eliminate(exact(left_q, left_q, NT), exact(left_o, left_o, NT), rank)


def inverse_of(left):
    rank = left.shape[0] // 2
    return pl.pallas_call(
        inverse_kernel,
        out_shape=pltpu.VMEM((2, rank, rank), f32),
        compiler_params=SMALL,
        cost_estimate=SLOW,
        name="inverse",
    )(left)


def stack_kernel(place_ref, left, stack, own):
    rank = left.shape[0] // 2
    for p in range(2):
        high, middle, low = three(left[p * rank : (p + 1) * rank, :])
        stack[p] = jnp.concatenate([high, middle, low, high, middle, high], axis=0)
    count = own.shape[1]
    index = place_ref[0]
    window = left[:, pl.ds(pl.multiple_of(index * LANES, LANES), 2 * LANES)]
    own[...] = pltpu.roll(window, 2 * LANES - index * (count - LANES), 1)[:, :count]


def stack_of(left, place, count):
    rank, size = left.shape[0] // 2, left.shape[1]
    return pl.pallas_call(
        stack_kernel,
        in_specs=[IN_SMEM, IN_VMEM],
        out_specs=[IN_VMEM] * 2,
        out_shape=[pltpu.VMEM((2, 6 * rank, size), bf16), pltpu.VMEM((2 * rank, count), f32)],
        compiler_params=SMALL,
        cost_estimate=SLOW,
        name="stack",
    )(place, left)


def finish_kernel(chunks, corr_q, corr_o, rows, stack, inverse, right, own, moment_q, moment_o, *refs):
    outs, buffer, new_moments, sems, moment_sems = refs[:6], refs[6], refs[7], refs[8], refs[9]
    rank, width = inverse.shape[1], moment_q.shape[1]
    height = width // chunks
    copies = []
    for p, corr in enumerate((corr_q, corr_o)):
        factor = right[:, p * width : (p + 1) * width]
        scaled = exact(inverse[p], exact(inverse[p], factor, NN), TN)
        high, middle, low = three(scaled.T)
        lefts = jnp.concatenate([high, high, high, middle, middle, low], axis=1)
        for c in range(chunks):
            at = pl.ds(c * height, height)
            decoded = lax.dot_general(lefts[c * height : (c + 1) * height], stack[p], NN, preferred_element_type=f32)
            buffer[p, at, :] = rows[pl.ds(p * width + c * height, height), :] - step_size * decoded
            buffer[2 + p, at, :] = corr[at, :] - decoded
            for k in (p, 2 + p):
                copies.append(pltpu.make_async_copy(buffer.at[k, at, :], outs[k].at[at, :], sems.at[k, c]))
                copies[-1].start()
    for p, moment in enumerate((moment_q, moment_o)):
        factor = right[:, p * width : (p + 1) * width]
        scaled = exact(inverse[p], exact(inverse[p], factor, NN), TN)
        new_moments[p] = decay_rate * moment[...] + exact(own[p * rank : (p + 1) * rank, :], scaled, TN)
        copies.append(pltpu.make_async_copy(new_moments.at[p], outs[4 + p], moment_sems.at[p]))
        copies[-1].start()
    for copy in copies:
        copy.wait()


def finish(corr_q, corr_o, rows, stack, inverse, right, own, moment_q, moment_o):
    width, size = corr_q.shape
    chunks = 3
    return pl.pallas_call(
        functools.partial(finish_kernel, chunks),
        in_specs=[IN_VMEM] * 9,
        out_specs=[IN_HBM] * 6,
        out_shape=[pltpu.HBM((width, size), f32)] * 4 + [pltpu.HBM(moment_q.shape, f32)] * 2,
        scratch_shapes=[
            pltpu.VMEM((4, width, size), f32),
            pltpu.VMEM((2,) + moment_q.shape, f32),
            pltpu.SemaphoreType.DMA((4, chunks)),
            pltpu.SemaphoreType.DMA((2,)),
        ],
        compiler_params=LARGE,
        name="finish",
    )(*hold(pltpu.VMEM, corr_q, corr_o, rows), stack, inverse, right, own, moment_q, moment_o)


def finish_plain(corr_q, corr_o, base, left, inverse, right, moment_q, moment_o):
    rank, width = inverse.shape[1], moment_q.shape[1]
    rows = moment_q.shape[0]
    start = lax.axis_index("rep") * rows
    bases = lax.all_gather(base, "rep", axis=0, tiled=True)
    weights, moments, errors = [], [], []
    for p, (corr, moment) in enumerate(((corr_q, moment_q), (corr_o, moment_o))):
        at = slice(p * width, (p + 1) * width)
        scaled = exact(inverse[p], exact(inverse[p], right[:, at], NN), TN)
        decoded = exact(scaled, left[p * rank : (p + 1) * rank], TN)
        weights.append(bases[:, at].T - step_size * decoded)
        moments.append(decay_rate * moment + lax.dynamic_slice_in_dim(decoded, start, rows, 1).T)
        errors.append(corr - decoded)
    return weights + errors + moments


def per_device(n_rep, n_shard, q_grad, o_grad, q_error, o_error, q_basis, o_basis, q_moment, o_moment, q_weight, o_weight, norm_grads, norm_moment, norm_weight):
    rank = q_basis.shape[1]
    size = q_grad.shape[1]
    flat = norm_grads.shape[-1]
    row_count = q_moment.shape[0]
    place = lax.axis_index("rep").astype(jnp.int32).reshape(1)
    shard = lax.axis_index("shard").astype(jnp.int32).reshape(1)

    gather = Gather(*base_of(q_weight, q_moment, o_weight, o_moment), place, n_rep)
    norm_moment, norm_weight = norm_moment.reshape(1, -1), norm_weight.reshape(1, -1)
    extra = norm_in(norm_grads[0], norm_moment, norm_weight, 2 * rank, place, shard, n_shard)
    corr_q, corr_o, keep, give = first((q_grad[0].T, o_grad[0].T), (q_error[0].T, o_error[0].T), q_basis.T, o_basis.T, place, shard)
    for sweep in range(ROUNDS):
        last = sweep == ROUNDS - 1
        ours, got = sum_over_all(keep, give, shard, n_rep, n_shard, gather, 2 * sweep)
        right, left, *extra_sum = right_of(ours, got, shard, corr_q, corr_o)
        if last and gather.paired:
            gather.tasks[3, 2] = (functools.partial(stack_of, count=row_count), left, place)
        gather.tasks[2 * sweep + 1, 1] = (inverse_of, left)
        right = sum_over(right, n_rep, gather, 2 * sweep + 1)
        inverse = gather.results[2 * sweep + 1, 1]
        if not last:
            keep, give = left_of(right, inverse, shard, corr_q, corr_o, [extra] if sweep == ROUNDS - 2 else [])
    norm_moment_new, norm_weight_new = norm_out(extra_sum[0], norm_moment, flat // LANES, place, shard, n_shard)
    if gather.paired:
        stack, own = gather.results[3, 2]
        gather.insert([gather.blocks["turned_last"]], ["turned_last"])
        outs = finish(corr_q, corr_o, gather.rows, stack, inverse, right, own, q_moment, o_moment)
    else:
        outs = finish_plain(corr_q, corr_o, gather.blocks["own"], left, inverse, right, q_moment, o_moment)
    weight_q, weight_o, error_q, error_o, q_moment_new, o_moment_new = outs
    return (
        weight_q.T,
        weight_o.T,
        q_moment_new,
        o_moment_new,
        error_q.T[None],
        error_o.T[None],
        norm_weight_new.reshape(flat),
        norm_moment_new.reshape(-1),
    )


def solution(mesh):
    n_rep, n_shard = mesh.shape["rep"], mesh.shape["shard"]

    def whole(*arrays):
        return per_device(n_rep, n_shard, *arrays)

    return jax.shard_map(
        whole,
        mesh=mesh,
        in_specs=(
            P("rep", None, "shard"),
            P("rep", None, "shard"),
            P("rep", None, "shard"),
            P("rep", None, "shard"),
            P("shard", None),
            P("shard", None),
            P("rep", "shard"),
            P("rep", "shard"),
            P("rep", "shard"),
            P("rep", "shard"),
            P("rep", "shard", None),
            P(("rep", "shard")),
            P(("rep", "shard")),
        ),
        out_specs=(
            P(None, "shard"),
            P(None, "shard"),
            P("rep", "shard"),
            P("rep", "shard"),
            P("rep", None, "shard"),
            P("rep", None, "shard"),
            P(),
            P(("rep", "shard")),
        ),
        check_vma=False,
    )
```

```python
import functools

import jax
import jax.numpy as jnp
from jax import lax
from jax.experimental import pallas as pl
from jax.experimental.pallas import tpu as pltpu
from jax.sharding import PartitionSpec as P

ROUNDS = 2
GROUP = 8
LANES = 128

highest = lax.Precision.HIGHEST
decay_rate = 0.9
step_size = 0.1
f32 = jnp.float32
bf16 = jnp.bfloat16
NN = (((1,), (0,)), ((), ()))
NT = (((1,), (1,)), ((), ()))
TN = (((0,), (0,)), ((), ()))

IN_HBM = pl.BlockSpec(memory_space=pltpu.HBM)
IN_VMEM = pl.BlockSpec(memory_space=pltpu.VMEM)
IN_SMEM = pl.BlockSpec(memory_space=pltpu.SMEM)
SMALL = pltpu.CompilerParams(vmem_limit_bytes=6 * 2**20)
LARGE = pltpu.CompilerParams(vmem_limit_bytes=12 * 2**20)
QUICK = pl.CostEstimate(flops=1000, bytes_accessed=1000, transcendentals=0)
SLOW = pl.CostEstimate(flops=1000, bytes_accessed=6_000_000, transcendentals=0)


def hold(space, *arrays):
    return [pltpu.with_memory_space_constraint(array, space) for array in arrays]


def exact(left, right, dims):
    return lax.dot_general(left, right, dims, precision=highest, preferred_element_type=f32)


def three(x):
    high = x.astype(bf16)
    rest = x - high.astype(f32)
    middle = rest.astype(bf16)
    low = (rest - middle.astype(f32)).astype(bf16)
    return high, middle, low


def stacked(left, right, dims):
    rows = left.shape[0]
    left_high, left_middle, left_low = three(left)
    right_high, right_middle, right_low = three(right)
    lefts = jnp.concatenate([left_high, left_middle, left_low], axis=0)
    of_high = lax.dot_general(lefts, right_high, dims, preferred_element_type=f32)
    of_middle = lax.dot_general(lefts[: 2 * rows], right_middle, dims, preferred_element_type=f32)
    of_low = lax.dot_general(left_high, right_low, dims, preferred_element_type=f32)
    small = (of_high[2 * rows :] + of_middle[rows:]) + of_low
    return of_high[:rows] + ((of_high[rows : 2 * rows] + of_middle[:rows]) + small)


def halves(count):
    masks = []
    mask = 1
    while mask < count:
        masks.append(mask)
        mask *= 2
    return masks


def swap(block, axis, mask, count):
    pairs = [(i, i ^ mask) for i in range(count)]
    return lax.ppermute(block, axis, pairs)


def sum_over(block, count, gather, stage):
    for mask in halves(count):
        block = gather.before(block, stage, mask)
        block = gather.start_tasks(block, stage, mask)
        block = block + gather.end_tasks(swap(block, "rep", mask, count), stage, mask)
        block = gather.after(block, stage, mask)
    return gather.after(gather.before(block, stage, 0), stage, 0)


def sum_over_all(keep, give, shard, masks, n_rep, n_shard, gather, stage, along=None):
    keep = gather.after(keep, stage, "begin")
    partner = None
    for mask, after in zip(masks, masks[1:] + [None]):
        got = swap(give, "shard", mask, n_shard)
        if after is not None:
            keep, give = split(keep, got, shard, after)
            if along is not None and partner is None:
                give, along = lax.optimization_barrier((give, along))
                partner = swap(along, "shard", mask, n_shard)
            keep = gather.after(gather.before(keep, stage, "core"), stage, "core")
    part = sum_over(keep + got, n_rep, gather, stage)
    for mask in reversed(halves(n_shard)[1:]):
        part = gather.start_tasks(part, stage, "x")
        got = gather.end_tasks(swap(part, "shard", mask, n_shard), stage, "x")
        part = gather.before(join(part, got, shard, mask), stage, "joined")
    return part, partner


def is_high(place_ref, mask):
    return (place_ref[0] & mask) != 0


def split_kernel(mask, shard_ref, ours, got, keep, give):
    total = ours[...] + got[...]
    half = total.shape[0] // 2
    high = is_high(shard_ref, mask)
    keep[...] = jnp.where(high, total[half:], total[:half])
    give[...] = jnp.where(high, total[:half], total[half:])


def split(ours, got, shard, mask):
    half = pltpu.VMEM((ours.shape[0] // 2, ours.shape[1]), f32)
    return pl.pallas_call(
        functools.partial(split_kernel, mask),
        in_specs=[IN_SMEM, IN_VMEM, IN_VMEM],
        out_specs=[IN_VMEM] * 2,
        out_shape=[half, half],
        compiler_params=SMALL,
        cost_estimate=QUICK,
        name="split",
    )(shard, ours, got)


def joined(shard_ref, mask, ours, got):
    high = is_high(shard_ref, mask)
    return jnp.concatenate([jnp.where(high, got, ours), jnp.where(high, ours, got)], axis=0)


def join_kernel(mask, shard_ref, ours, got, whole):
    whole[...] = joined(shard_ref, mask, ours[...], got[...])


def join(ours, got, shard, mask):
    return pl.pallas_call(
        functools.partial(join_kernel, mask),
        in_specs=[IN_SMEM, IN_VMEM, IN_VMEM],
        out_specs=IN_VMEM,
        out_shape=pltpu.VMEM((2 * ours.shape[0], ours.shape[1]), f32),
        compiler_params=SMALL,
        cost_estimate=QUICK,
        name="join",
    )(shard, ours, got)


class Gather:
    PLAN = (
        ("near", "own", 2, None, (0, 4)),
        ("turned", "own", 1, (0, 1), (1, 4)),
        ("far_a", "own_a", 4, (0, 4), (1, 4)),
        ("turned_near", "near", 1, (1, 1), (2, 4)),
        ("last_a", "far_a", 2, (1, 2), (2, 2)),
        ("turned_far_a", "far_a", 1, (1, 2), (2, 2)),
        ("far_b", "own_b", 4, (2, "begin"), (2, 4)),
        ("turned_last_a", "last_a", 1, (2, 1), (2, "joined")),
        ("last_b", "far_b", 2, (2, 2), (3, 2)),
        ("turned_far_b", "far_b", 1, (2, 2), (3, 2)),
        ("turned_last_b", "last_b", 1, (3, 1), (3, 0)),
    )
    INSERTS = {
        (1, 1): ("own",),
        (1, 4): ("near",),
        (2, 1): ("turned",),
        (2, 2): ("far_a", "last_a"),
        (2, 4): ("turned_near",),
        (2, "x"): ("turned_far_a",),
        (3, 1): ("far_b",),
        (3, 4): ("turned_far_b", "last_b", "turned_last_a"),
    }
    PLACES = {"own": 0, "turned": 1, "near": 2, "far": 4, "last": 6, "turned_near": 3, "turned_far": 5, "turned_last": 7}

    def place_of(self, name):
        whole = name.removesuffix("_a").removesuffix("_b")
        skipped = self.blocks["own"].shape[0] - self.blocks[name].shape[0]
        return self.PLACES[whole], skipped if name.endswith("_b") else 0

    def __init__(self, own, own_a, own_b, place, count):
        self.count = count
        self.place = place
        self.blocks = {"own": own, "own_a": own_a, "own_b": own_b}
        self.paired = count == 8 and own.shape[0] % 16 == 0
        self.rows = None
        self.tasks = {}
        self.results = {}
        self.send(None)

    def send(self, point):
        if self.paired:
            for name, source, mask, after, _ in self.PLAN:
                if after == point:
                    self.blocks[name] = swap(self.blocks[source], "rep", mask, self.count)

    def start_tasks(self, value, stage, mask):
        point = (stage, mask)
        if point in self.tasks:
            task, *inputs = self.tasks[point]
            value, *inputs = lax.optimization_barrier((value, *inputs))
            self.results[point] = task(*inputs)
        if self.paired and point in self.INSERTS:
            value, *blocks = lax.optimization_barrier((value, *(self.blocks[name] for name in self.INSERTS[point])))
            self.insert(blocks, self.INSERTS[point])
        if self.paired:
            for name, source, _, after, _ in self.PLAN:
                if after == ("beside",) + point:
                    if point in self.INSERTS:
                        self.rows, self.blocks[source] = lax.optimization_barrier((self.rows, self.blocks[source]))
                    else:
                        self.results[point], self.blocks[source] = lax.optimization_barrier((self.results[point], self.blocks[source]))
            self.send(("beside",) + point)
        return value

    def end_tasks(self, value, stage, mask):
        point = (stage, mask)
        if point in self.tasks:
            value, self.results[point] = lax.optimization_barrier((value, self.results[point]))
        if self.paired and point in self.INSERTS:
            value, self.rows = lax.optimization_barrier((value, self.rows))
        return value

    def insert(self, blocks, names):
        self.rows = insert(self.place, self.rows, blocks, [self.place_of(name) for name in names], self.blocks["own"].shape[0], self.count)

    def before(self, value, stage, mask):
        if self.paired:
            for name, _, _, _, by in self.PLAN:
                if by == (stage, mask):
                    value, self.blocks[name] = lax.optimization_barrier((value, self.blocks[name]))
        return value

    def after(self, value, stage, mask):
        if self.paired:
            for name, source, _, after, _ in self.PLAN:
                if after == (stage, mask) and source in self.blocks:
                    value, self.blocks[source] = lax.optimization_barrier((value, self.blocks[source]))
            self.send((stage, mask))
        return value


def insert_kernel(masks, rows_each, place_ref, *refs):
    blocks, rows, out = refs[: len(masks)], refs[len(masks) : -1], refs[-1]
    if not rows:
        out[...] = jnp.zeros_like(out)
    height = out.shape[0]
    window = 2 * LANES
    lane = lax.broadcasted_iota(jnp.int32, (height, window), 1)
    for block, (mask, skipped) in zip(blocks, masks):
        count = block.shape[0]
        index = place_ref[0] ^ mask
        shift = index * (rows_each - LANES) + skipped
        turned = jnp.concatenate([block[...].T, jnp.zeros((height, window - count), f32)], axis=1)
        turned = pltpu.roll(turned, shift, 1)
        at = pl.ds(pl.multiple_of(index * LANES, LANES), window)
        out[:, at] = jnp.where((lane >= shift) & (lane < shift + count), turned, out[:, at])


def insert(place, rows, blocks, masks, rows_each, count):
    height, width = blocks[0].shape[1], rows_each * count
    old = [] if rows is None else hold(pltpu.VMEM, rows)
    return pl.pallas_call(
        functools.partial(insert_kernel, masks, rows_each),
        in_specs=[IN_SMEM] + [IN_VMEM] * (len(blocks) + len(old)),
        out_specs=IN_VMEM,
        out_shape=pltpu.VMEM((height, width), f32),
        input_output_aliases={1 + len(blocks): 0} if old else {},
        compiler_params=SMALL,
        cost_estimate=SLOW,
        name="insert",
    )(place, *blocks, *old)


def base_kernel(weight_q, moment_q, weight_o, moment_o, own, *parts):
    drop = step_size * decay_rate
    base = jnp.concatenate([weight_q[...] - drop * moment_q[...], weight_o[...] - drop * moment_o[...]], axis=1)
    own[...] = base
    rows = base.shape[0]
    first_part, second_part = parts
    first_part[...] = base[: first_part.shape[0]]
    second_part[...] = base[rows - second_part.shape[0] :]


def base_of(weight_q, moment_q, weight_o, moment_o):
    rows, width = weight_q.shape[0], 2 * weight_q.shape[1]
    half = rows // 2
    shapes = [(rows, width), (half, width), (rows - half, width)]
    return pl.pallas_call(
        base_kernel,
        in_specs=[IN_VMEM] * 4,
        out_specs=[IN_VMEM] * 3,
        out_shape=[pltpu.VMEM(shape, f32) for shape in shapes],
        compiler_params=SMALL,
        cost_estimate=QUICK,
        name="base",
    )(weight_q, moment_q, weight_o, moment_o)


def window_of(n_shard, share, place_ref, shard_ref, lines):
    start = (place_ref[0] * n_shard + shard_ref[0]) * share
    row = lax.broadcasted_iota(jnp.int32, (lines, LANES), 0)
    lane = lax.broadcasted_iota(jnp.int32, (lines, LANES), 1)
    flat = row * LANES + lane
    return lax.rem(start, LANES), (flat >= start) & (flat < start + share)


def norm_terms(n_shard, rows, place_ref, shard_ref, grads, moment, weight):
    lines, share = grads.shape[1] // LANES, moment.shape[1]
    shift, inside = window_of(n_shard, share, place_ref, shard_ref, lines)
    kept = weight[...] - step_size * decay_rate * moment[...]
    kept = jnp.concatenate([kept, jnp.zeros((1, LANES - share), f32)], axis=1)
    kept = pltpu.roll(jnp.broadcast_to(kept, (8, LANES)), shift, 1)[:1]
    square = jnp.concatenate([grads[:, line * LANES : (line + 1) * LANES] for line in range(lines)], axis=0)
    rest = jnp.zeros((rows - lines, LANES), f32)
    shares = jnp.where(inside, kept, 0.0) - step_size * square
    return jnp.concatenate([square, rest], axis=0), jnp.concatenate([shares, rest], axis=0)


def norm_out_kernel(n_shard, place_ref, shard_ref, ours, got, moment, new_moment, new_weight):
    lines, share = new_weight.shape[0], moment.shape[1]
    high = is_high(shard_ref, 1)
    sums = jnp.where(high, got[:lines, :], ours[:lines, :])
    shift, inside = window_of(n_shard, share, place_ref, shard_ref, lines)
    total = jnp.sum(jnp.where(inside, sums, 0.0), axis=0, keepdims=True)
    total = pltpu.roll(jnp.broadcast_to(total, (8, LANES)), LANES - shift, 1)[:1, :share]
    new_moment[...] = decay_rate * moment[...] + total
    new_weight[...] = jnp.where(high, ours[:lines, :], got[:lines, :])


def norm_out(ours, got, moment, place, shard, lines, n_shard):
    return pl.pallas_call(
        functools.partial(norm_out_kernel, n_shard),
        in_specs=[IN_SMEM] * 2 + [IN_VMEM] * 3,
        out_specs=[IN_VMEM] * 2,
        out_shape=[jax.ShapeDtypeStruct(moment.shape, f32), jax.ShapeDtypeStruct((lines, LANES), f32)],
        compiler_params=SMALL,
        cost_estimate=QUICK,
        name="norm_out",
    )(place, shard, ours, got, moment)


def first_kernel(chunks, n_shard, place_ref, shard_ref, *refs):
    sources, norms, (corr, give_corr, keep, give) = refs[:6], refs[6:9], refs[9:13]
    buffer, bases, norm_buffers, sems, small_sems = refs[13], refs[14], refs[15:18], refs[18], refs[19]
    rank, size = bases.shape[1], corr.shape[2]
    high = is_high(shard_ref, 1)
    lanes = size // chunks
    small = zip(sources[4:] + norms, [bases.at[0], bases.at[1], *norm_buffers])
    small_copies = [pltpu.make_async_copy(source, target, small_sems.at[k]) for k, (source, target) in enumerate(small)]
    copies = {}
    for copy in small_copies:
        copy.start()
    for c in range(chunks):
        at = pl.ds(c * lanes, lanes)
        for j, source in enumerate(sources[:4]):
            copies[c, j] = pltpu.make_async_copy(source.at[:, at], buffer.at[j, :, at], sems.at[c, j])
            copies[c, j].start()
    for copy in small_copies:
        copy.wait()
    sums, shares = norm_terms(n_shard, rank, place_ref, shard_ref, *norm_buffers)
    keep[:, size:] = jnp.where(high, shares, sums)
    give[:, size:] = jnp.where(high, sums, shares)
    for c in range(chunks):
        at = pl.ds(c * lanes, lanes)
        totals, parts = [], []
        for p in range(2):
            copies[c, p].wait()
            copies[c, 2 + p].wait()
            totals.append(buffer[p, :, at] + buffer[2 + p, :, at])
            corr[p, :, at] = totals[p]
            parts.append(stacked(bases[p], totals[p], NN))
        give_corr[:, at] = jnp.where(high, totals[0], totals[1])
        keep[:, at] = jnp.where(high, parts[1], parts[0])
        give[:, at] = jnp.where(high, parts[0], parts[1])


def first(grads, errors, bases, norms, place, shard, n_shard):
    width, size = grads[0].shape
    rank = bases[0].shape[0]
    chunks = 3 if size % (3 * LANES) == 0 else 1
    part = pltpu.VMEM((rank, size + LANES), f32)
    return pl.pallas_call(
        functools.partial(first_kernel, chunks, n_shard),
        in_specs=[IN_SMEM] * 2 + [IN_HBM] * 9,
        out_specs=[IN_VMEM] * 4,
        out_shape=[pltpu.VMEM((2, width, size), f32), pltpu.VMEM((width, size), f32), part, part],
        scratch_shapes=[
            pltpu.VMEM((4, width, size), f32),
            pltpu.VMEM((2, rank, width), f32),
            *(pltpu.VMEM(array.shape, f32) for array in norms),
            pltpu.SemaphoreType.DMA((chunks, 4)),
            pltpu.SemaphoreType.DMA((5,)),
        ],
        compiler_params=LARGE,
        name="first",
    )(place, shard, *hold(pltpu.HBM, *grads, *errors, *bases, *norms))


def both_shares(shard_ref, corr, other):
    return jnp.concatenate([corr[shard_ref[0] & 1], other[...]], axis=0)


def right_kernel(shard_ref, whole, corr, other, right, left, *extra):
    size = corr.shape[2]
    left[...] = whole[:, :size]
    if extra:
        extra[0][...] = whole[:, size:]
    right[...] = stacked(whole[:, :size], both_shares(shard_ref, corr, other), NT)


def right_of(whole, shard, corr, other):
    rank = whole.shape[0]
    width, size = other.shape
    beside = whole.shape[1] - size
    shapes = [(rank, 2 * width), (rank, size)] + ([(rank, beside)] if beside else [])
    return pl.pallas_call(
        right_kernel,
        in_specs=[IN_SMEM] + [IN_VMEM] * 3,
        out_specs=[IN_VMEM] * len(shapes),
        out_shape=[pltpu.VMEM(shape, f32) for shape in shapes],
        compiler_params=SMALL,
        cost_estimate=QUICK,
        name="right",
    )(shard, whole, *hold(pltpu.VMEM, corr, other))


def left_kernel(mask, shard_ref, right, inverse, corr, other, keep, give):
    basis = exact(inverse[0], right[...], NN)
    part = stacked(basis, both_shares(shard_ref, corr, other), NN)
    half = part.shape[0] // 2
    high = is_high(shard_ref, mask)
    keep[...] = jnp.where(high, part[half:], part[:half])
    give[...] = jnp.where(high, part[:half], part[half:])


def left_of(right, inverse, shard, mask, corr, other):
    half = pltpu.VMEM((right.shape[0] // 2, other.shape[1]), f32)
    return pl.pallas_call(
        functools.partial(left_kernel, mask),
        in_specs=[IN_SMEM] + [IN_VMEM] * 4,
        out_specs=[IN_VMEM] * 2,
        out_shape=[half, half],
        compiler_params=SMALL,
        cost_estimate=QUICK,
        name="left",
    )(shard, right, inverse, *hold(pltpu.VMEM, corr, other))


def eliminate(gram_q, gram_o, rank):
    width = 4 * rank
    lane = lax.broadcasted_iota(jnp.int32, (rank, width), 1)
    row = lax.broadcasted_iota(jnp.int32, (rank, width), 0)
    square = (rank, rank)
    eye = (lax.broadcasted_iota(jnp.int32, square, 0) == lax.broadcasted_iota(jnp.int32, square, 1)).astype(f32)
    work = jnp.concatenate([gram_q, eye, gram_o, eye], axis=1)
    first_half = lane < 2 * rank
    scale = jnp.ones((rank, width), f32)
    for base in range(0, rank, GROUP):
        columns = []
        for k in range(base, base + GROUP):
            of_q = jnp.broadcast_to(work[:, k : k + 1], (rank, width))
            of_o = jnp.broadcast_to(work[:, 2 * rank + k : 2 * rank + k + 1], (rank, width))
            columns.append(jnp.where(first_half, of_q, of_o))
        for j in range(GROUP):
            k = base + j
            pivot = columns[j][k : k + 1]
            factor = jnp.where(row > k, columns[j] * (1.0 / pivot), 0.0)
            scale = jnp.where(row == k, pivot, scale)
            for i in range(j + 1, GROUP):
                columns[i] = columns[i] - factor * columns[i][k : k + 1]
            work = work - factor * work[k : k + 1]
    work = work * lax.rsqrt(scale)
    return work[:, rank : 2 * rank], work[:, 3 * rank :]


def inverse_kernel(ours, theirs, out):
    rank = out.shape[1]
    out[0], out[1] = eliminate(exact(ours[...], ours[...], NT), exact(theirs[...], theirs[...], NT), rank)


def inverse_of(ours, theirs):
    rank = ours.shape[0]
    return pl.pallas_call(
        inverse_kernel,
        out_shape=pltpu.VMEM((2, rank, rank), f32),
        compiler_params=SMALL,
        cost_estimate=SLOW,
        name="inverse",
    )(ours, theirs)


def stack_kernel(place_ref, ours, theirs, stack, own):
    count = own.shape[2]
    index = place_ref[0]
    for p, left in enumerate((ours, theirs)):
        high, middle, low = three(left[...])
        stack[p] = jnp.concatenate([high, middle, low, high, middle, high], axis=0)
        window = left[:, pl.ds(pl.multiple_of(index * LANES, LANES), 2 * LANES)]
        own[p] = pltpu.roll(window, 2 * LANES - index * (count - LANES), 1)[:, :count]


def stack_of(ours, theirs, place, count):
    rank, size = ours.shape
    return pl.pallas_call(
        stack_kernel,
        in_specs=[IN_SMEM, IN_VMEM, IN_VMEM],
        out_specs=[IN_VMEM] * 2,
        out_shape=[pltpu.VMEM((2, 6 * rank, size), bf16), pltpu.VMEM((2, rank, count), f32)],
        compiler_params=SMALL,
        cost_estimate=SLOW,
        name="stack",
    )(place, ours, theirs)


def finish_kernel(chunks, shard_ref, corr, rows, stack, inverse, right, their_right, own, moment_q, moment_o, *refs):
    outs, (buffer, new_moments, sems) = refs[:6], refs[6:]
    width = moment_q.shape[1]
    height = width // chunks
    copies = []

    def send(index, source, to_q, to_o, sem):
        for p, target in enumerate((to_q, to_o)):

            @pl.when(index == p)
            def _(target=target):
                pltpu.make_async_copy(source, target, sem).start()

        copies.append(pltpu.make_async_copy(source, to_q, sem))

    for theirs, factor in enumerate((right, their_right)):
        index = (shard_ref[0] & 1) ^ theirs
        factor = factor[:, width * theirs : width * (theirs + 1)]
        scaled = exact(inverse[theirs], exact(inverse[theirs], factor, NN), TN)
        high, middle, low = three(scaled.T)
        lefts = jnp.concatenate([high, high, high, middle, middle, low], axis=1)
        for c in range(chunks):
            at = pl.ds(c * height, height)
            decoded = lax.dot_general(lefts[c * height : (c + 1) * height], stack[theirs], NN, preferred_element_type=f32)
            buffer[theirs, 0, at, :] = rows[pl.ds(pl.multiple_of(index * width + c * height, 8), height), :] - step_size * decoded
            buffer[theirs, 1, at, :] = corr[index, at, :] - decoded
            for k in range(2):
                send(index, buffer.at[theirs, k, at, :], outs[2 * k].at[at, :], outs[2 * k + 1].at[at, :], sems.at[theirs, k, c])
        moment = jnp.where(index == 0, moment_q[...], moment_o[...])
        new_moments[theirs] = decay_rate * moment + exact(own[theirs], scaled, TN)
        send(index, new_moments.at[theirs], outs[4], outs[5], sems.at[theirs, 2, 0])
    for copy in copies:
        copy.wait()


def finish(shard, corr, rows, stack, inverse, right, their_right, own, moment_q, moment_o):
    width, size = corr.shape[1:]
    chunks = 3
    return pl.pallas_call(
        functools.partial(finish_kernel, chunks),
        in_specs=[IN_SMEM] + [IN_VMEM] * 9,
        out_specs=[IN_HBM] * 6,
        out_shape=[pltpu.HBM((width, size), f32)] * 4 + [pltpu.HBM(moment_q.shape, f32)] * 2,
        scratch_shapes=[
            pltpu.VMEM((2, 2, width, size), f32),
            pltpu.VMEM((2,) + moment_q.shape, f32),
            pltpu.SemaphoreType.DMA((2, 3, chunks)),
        ],
        compiler_params=LARGE,
        name="finish",
    )(shard, *hold(pltpu.VMEM, corr, rows), stack, inverse, right, their_right, own, moment_q, moment_o)


def finish_plain(high, corr, base, lefts, inverse, rights, moments):
    rows, width = moments[0].shape
    start = lax.axis_index("rep") * rows
    bases = lax.all_gather(base, "rep", axis=0, tiled=True)
    decodeds = []
    for p in range(2):
        factor = rights[p][:, p * width : (p + 1) * width]
        scaled = exact(inverse[p], exact(inverse[p], factor, NN), TN)
        decodeds.append(exact(scaled, lefts[p], TN))
    ours, theirs = decodeds
    weights, new_moments, errors = [], [], []
    for p, decoded in enumerate((jnp.where(high, theirs, ours), jnp.where(high, ours, theirs))):
        weights.append(bases[:, p * width : (p + 1) * width].T - step_size * decoded)
        new_moments.append(decay_rate * moments[p] + lax.dynamic_slice_in_dim(decoded, start, rows, 1).T)
        errors.append(corr[p] - decoded)
    return weights + errors + new_moments


def per_device(n_rep, n_shard, q_grad, o_grad, q_error, o_error, q_basis, o_basis, q_moment, o_moment, q_weight, o_weight, norm_grads, norm_moment, norm_weight):
    rank = q_basis.shape[1]
    size = q_grad.shape[1]
    flat = norm_grads.shape[-1]
    row_count = q_moment.shape[0]
    place = lax.axis_index("rep").astype(jnp.int32).reshape(1)
    shard = lax.axis_index("shard").astype(jnp.int32).reshape(1)

    gather = Gather(*base_of(q_weight, q_moment, o_weight, o_moment), place, n_rep)
    norm_moment, norm_weight = norm_moment.reshape(1, -1), norm_weight.reshape(1, -1)
    norms = (norm_grads[0], norm_moment, norm_weight)
    corr, give_corr, keep, give = first((q_grad[0].T, o_grad[0].T), (q_error[0].T, o_error[0].T), (q_basis.T, o_basis.T), norms, place, shard, n_shard)
    masks = halves(n_shard)
    for sweep in range(ROUNDS):
        last = sweep == ROUNDS - 1
        if sweep == 0:
            whole, other_corr = sum_over_all(keep, give, shard, masks, n_rep, n_shard, gather, 0, give_corr)
        else:
            whole, _ = sum_over_all(keep, give, shard, masks[1:], n_rep, n_shard, gather, 2 * sweep)
        right, left, *beside = right_of(whole, shard, corr, other_corr)
        if sweep == 0:
            norm_got = swap(beside[0], "shard", masks[0], n_shard)
            gather.tasks[2, 1] = (functools.partial(norm_out, lines=flat // LANES, n_shard=n_shard), beside[0], norm_got, norm_moment, place, shard)
        theirs = swap(left, "shard", masks[0], n_shard) if last else left
        gather.tasks[2 * sweep + 1, 4 if last else 2] = (inverse_of, left, theirs)
        if last and gather.paired:
            gather.tasks[3, 2] = (functools.partial(stack_of, count=row_count), left, theirs, place)
        right = sum_over(right, n_rep, gather, 2 * sweep + 1)
        inverse = gather.results[2 * sweep + 1, 4 if last else 2]
        if not last:
            keep, give = left_of(right, inverse, shard, masks[1], corr, other_corr)
    their_right = swap(right, "shard", masks[0], n_shard)
    norm_moment_new, norm_weight_new = gather.results[2, 1]
    if gather.paired:
        stack, own = gather.results[3, 2]
        gather.insert([gather.blocks["turned_last_b"]], ["turned_last_b"])
        outs = finish(shard, corr, gather.rows, stack, inverse, right, their_right, own, q_moment, o_moment)
    else:
        outs = finish_plain((shard[0] & 1) != 0, corr, gather.blocks["own"], (left, theirs), inverse, (right, their_right), (q_moment, o_moment))
    weight_q, weight_o, error_q, error_o, q_moment_new, o_moment_new = outs
    return (
        weight_q.T,
        weight_o.T,
        q_moment_new,
        o_moment_new,
        error_q.T[None],
        error_o.T[None],
        norm_weight_new.reshape(flat),
        norm_moment_new.reshape(-1),
    )


def solution(mesh):
    n_rep, n_shard = mesh.shape["rep"], mesh.shape["shard"]

    def whole(*arrays):
        return per_device(n_rep, n_shard, *arrays)

    return jax.shard_map(
        whole,
        mesh=mesh,
        in_specs=(
            P("rep", None, "shard"),
            P("rep", None, "shard"),
            P("rep", None, "shard"),
            P("rep", None, "shard"),
            P("shard", None),
            P("shard", None),
            P("rep", "shard"),
            P("rep", "shard"),
            P("rep", "shard"),
            P("rep", "shard"),
            P("rep", "shard", None),
            P(("rep", "shard")),
            P(("rep", "shard")),
        ),
        out_specs=(
            P(None, "shard"),
            P(None, "shard"),
            P("rep", "shard"),
            P("rep", "shard"),
            P("rep", None, "shard"),
            P("rep", None, "shard"),
            P(),
            P(("rep", "shard")),
        ),
        check_vma=False,
    )
```

```python
import functools

import jax
import jax.numpy as jnp
from jax import lax
from jax.experimental import pallas as pl
from jax.experimental.pallas import tpu as pltpu
from jax.sharding import PartitionSpec as P

ROUNDS = 2
GROUP = 8
LANES = 128

highest = lax.Precision.HIGHEST
decay_rate = 0.9
step_size = 0.1
f32 = jnp.float32
bf16 = jnp.bfloat16
NN = (((1,), (0,)), ((), ()))
NT = (((1,), (1,)), ((), ()))
TN = (((0,), (0,)), ((), ()))

IN_HBM = pl.BlockSpec(memory_space=pltpu.HBM)
IN_VMEM = pl.BlockSpec(memory_space=pltpu.VMEM)
IN_SMEM = pl.BlockSpec(memory_space=pltpu.SMEM)
SMALL = pltpu.CompilerParams(vmem_limit_bytes=6 * 2**20)
LARGE = pltpu.CompilerParams(vmem_limit_bytes=12 * 2**20)
QUICK = pl.CostEstimate(flops=1000, bytes_accessed=1000, transcendentals=0)
SLOW = pl.CostEstimate(flops=1000, bytes_accessed=6_000_000, transcendentals=0)


def hold(space, *arrays):
    return [pltpu.with_memory_space_constraint(array, space) for array in arrays]


def exact(left, right, dims):
    return lax.dot_general(left, right, dims, precision=highest, preferred_element_type=f32)


def three(x):
    high = x.astype(bf16)
    rest = x - high.astype(f32)
    middle = rest.astype(bf16)
    low = (rest - middle.astype(f32)).astype(bf16)
    return high, middle, low


def stacked(left, right, dims):
    rows = left.shape[0]
    left_high, left_middle, left_low = three(left)
    right_high, right_middle, right_low = three(right)
    lefts = jnp.concatenate([left_high, left_middle, left_low], axis=0)
    of_high = lax.dot_general(lefts, right_high, dims, preferred_element_type=f32)
    of_middle = lax.dot_general(lefts[: 2 * rows], right_middle, dims, preferred_element_type=f32)
    of_low = lax.dot_general(left_high, right_low, dims, preferred_element_type=f32)
    small = (of_high[2 * rows :] + of_middle[rows:]) + of_low
    return of_high[:rows] + ((of_high[rows : 2 * rows] + of_middle[:rows]) + small)


def halves(count):
    masks = []
    mask = 1
    while mask < count:
        masks.append(mask)
        mask *= 2
    return masks


def swap(block, axis, mask, count):
    pairs = [(i, i ^ mask) for i in range(count)]
    return lax.ppermute(block, axis, pairs)


def sum_over(block, count, gather, stage):
    for mask in halves(count):
        block = gather.before(block, stage, mask)
        block = gather.start_tasks(block, stage, mask)
        block = block + gather.end_tasks(swap(block, "rep", mask, count), stage, mask)
        block = gather.after(block, stage, mask)
    return gather.after(gather.before(block, stage, 0), stage, 0)


def sum_over_all(keep, give, shard, masks, n_rep, n_shard, gather, stage, along=None):
    keep = gather.after(keep, stage, "begin")
    partner = None
    for mask, after in zip(masks, masks[1:] + [None]):
        got = swap(give, "shard", mask, n_shard)
        if after is not None:
            keep, give = split(keep, got, shard, after)
            if along is not None and partner is None:
                give, along = lax.optimization_barrier((give, along))
                partner = swap(along, "shard", mask, n_shard)
            keep = gather.after(gather.before(keep, stage, "core"), stage, "core")
    part = sum_over(keep + got, n_rep, gather, stage)
    for mask in reversed(halves(n_shard)[1:]):
        part = gather.start_tasks(part, stage, "x")
        got = gather.end_tasks(swap(part, "shard", mask, n_shard), stage, "x")
        part = gather.before(join(part, got, shard, mask), stage, "joined")
    return part, partner


def is_high(place_ref, mask):
    return (place_ref[0] & mask) != 0


def split_kernel(mask, shard_ref, ours, got, keep, give):
    total = ours[...] + got[...]
    half = total.shape[0] // 2
    high = is_high(shard_ref, mask)
    keep[...] = jnp.where(high, total[half:], total[:half])
    give[...] = jnp.where(high, total[:half], total[half:])


def split(ours, got, shard, mask):
    half = pltpu.VMEM((ours.shape[0] // 2, ours.shape[1]), f32)
    return pl.pallas_call(
        functools.partial(split_kernel, mask),
        in_specs=[IN_SMEM, IN_VMEM, IN_VMEM],
        out_specs=[IN_VMEM] * 2,
        out_shape=[half, half],
        compiler_params=SMALL,
        cost_estimate=QUICK,
        name="split",
    )(shard, ours, got)


def joined(shard_ref, mask, ours, got):
    high = is_high(shard_ref, mask)
    return jnp.concatenate([jnp.where(high, got, ours), jnp.where(high, ours, got)], axis=0)


def join_kernel(mask, shard_ref, ours, got, whole):
    whole[...] = joined(shard_ref, mask, ours[...], got[...])


def join(ours, got, shard, mask):
    return pl.pallas_call(
        functools.partial(join_kernel, mask),
        in_specs=[IN_SMEM, IN_VMEM, IN_VMEM],
        out_specs=IN_VMEM,
        out_shape=pltpu.VMEM((2 * ours.shape[0], ours.shape[1]), f32),
        compiler_params=SMALL,
        cost_estimate=QUICK,
        name="join",
    )(shard, ours, got)


class Gather:
    PLAN = (
        ("near", "own", 2, (0, "core"), (0, "joined")),
        ("turned", "own", 1, (0, 1), (1, 4)),
        ("far_a", "own_a", 4, (0, 4), (1, 4)),
        ("turned_near", "near", 1, (1, 1), (2, 4)),
        ("last_a", "far_a", 2, (1, 2), (2, 2)),
        ("turned_far_a", "far_a", 1, (1, 2), (2, 2)),
        ("far_b", "own_b", 4, (2, "begin"), (2, 4)),
        ("turned_last_a", "last_a", 1, (2, 1), (2, "joined")),
        ("last_b", "far_b", 2, (2, 2), (3, 2)),
        ("turned_far_b", "far_b", 1, (2, 2), (3, 2)),
        ("turned_last_b", "last_b", 1, (3, 1), None),
    )
    INSERTS = {
        (1, 1): ("own",),
        (2, 1): ("near", "turned"),
        (2, 2): ("far_a", "last_a"),
        (2, 4): ("turned_near",),
        (2, "x"): ("turned_far_a",),
        (3, 1): ("far_b",),
        (3, 4): ("turned_far_b", "last_b", "turned_last_a"),
    }
    PLACES = {"own": 0, "turned": 1, "near": 2, "far": 4, "last": 6, "turned_near": 3, "turned_far": 5, "turned_last": 7}

    def place_of(self, name):
        whole = name.removesuffix("_a").removesuffix("_b")
        skipped = self.blocks["own"].shape[0] - self.blocks[name].shape[0]
        return self.PLACES[whole], skipped if name.endswith("_b") else 0

    def __init__(self, own, own_a, own_b, place, count):
        self.count = count
        self.place = place
        self.blocks = {"own": own, "own_a": own_a, "own_b": own_b}
        self.paired = count == 8 and own.shape[0] % 16 == 0
        self.rows = None
        self.tasks = {}
        self.results = {}
        self.send(None)

    def send(self, point):
        if self.paired:
            for name, source, mask, after, _ in self.PLAN:
                if after == point:
                    self.blocks[name] = swap(self.blocks[source], "rep", mask, self.count)

    def start_tasks(self, value, stage, mask):
        point = (stage, mask)
        if point in self.tasks:
            task, *inputs = self.tasks[point]
            value, *inputs = lax.optimization_barrier((value, *inputs))
            self.results[point] = task(*inputs)
        if self.paired and point in self.INSERTS:
            value, *blocks = lax.optimization_barrier((value, *(self.blocks[name] for name in self.INSERTS[point])))
            self.insert(blocks, self.INSERTS[point])
        if self.paired:
            for name, source, _, after, _ in self.PLAN:
                if after == ("beside",) + point:
                    if point in self.INSERTS:
                        self.rows, self.blocks[source] = lax.optimization_barrier((self.rows, self.blocks[source]))
                    else:
                        self.results[point], self.blocks[source] = lax.optimization_barrier((self.results[point], self.blocks[source]))
            self.send(("beside",) + point)
        return value

    def end_tasks(self, value, stage, mask):
        point = (stage, mask)
        if point in self.tasks:
            value, self.results[point] = lax.optimization_barrier((value, self.results[point]))
        if self.paired and point in self.INSERTS:
            value, self.rows = lax.optimization_barrier((value, self.rows))
        return value

    def insert(self, blocks, names):
        self.rows = insert(self.place, self.rows, blocks, [self.place_of(name) for name in names], self.blocks["own"].shape[0], self.count)

    def before(self, value, stage, mask):
        if self.paired:
            for name, _, _, _, by in self.PLAN:
                if by == (stage, mask):
                    value, self.blocks[name] = lax.optimization_barrier((value, self.blocks[name]))
        return value

    def after(self, value, stage, mask):
        if self.paired:
            for name, source, _, after, _ in self.PLAN:
                if after == (stage, mask) and source in self.blocks:
                    value, self.blocks[source] = lax.optimization_barrier((value, self.blocks[source]))
            self.send((stage, mask))
        return value


def insert_kernel(masks, rows_each, place_ref, *refs):
    blocks, rows, out = refs[: len(masks)], refs[len(masks) : -1], refs[-1]
    if not rows:
        out[...] = jnp.zeros_like(out)
    height = out.shape[0]
    window = 2 * LANES
    lane = lax.broadcasted_iota(jnp.int32, (height, window), 1)
    for block, (mask, skipped) in zip(blocks, masks):
        count = block.shape[0]
        index = place_ref[0] ^ mask
        shift = index * (rows_each - LANES) + skipped
        turned = jnp.concatenate([block[...].T, jnp.zeros((height, window - count), f32)], axis=1)
        turned = pltpu.roll(turned, shift, 1)
        at = pl.ds(pl.multiple_of(index * LANES, LANES), window)
        out[:, at] = jnp.where((lane >= shift) & (lane < shift + count), turned, out[:, at])


def insert(place, rows, blocks, masks, rows_each, count):
    height, width = blocks[0].shape[1], rows_each * count
    old = [] if rows is None else hold(pltpu.VMEM, rows)
    return pl.pallas_call(
        functools.partial(insert_kernel, masks, rows_each),
        in_specs=[IN_SMEM] + [IN_VMEM] * (len(blocks) + len(old)),
        out_specs=IN_VMEM,
        out_shape=pltpu.VMEM((height, width), f32),
        input_output_aliases={1 + len(blocks): 0} if old else {},
        compiler_params=SMALL,
        cost_estimate=SLOW,
        name="insert",
    )(place, *blocks, *old)


def base_kernel(weight_q, moment_q, weight_o, moment_o, own, *parts):
    drop = step_size * decay_rate
    base = jnp.concatenate([weight_q[...] - drop * moment_q[...], weight_o[...] - drop * moment_o[...]], axis=1)
    own[...] = base
    rows = base.shape[0]
    first_part, second_part = parts
    first_part[...] = base[: first_part.shape[0]]
    second_part[...] = base[rows - second_part.shape[0] :]


def base_of(weight_q, moment_q, weight_o, moment_o):
    rows, width = weight_q.shape[0], 2 * weight_q.shape[1]
    half = rows // 2
    shapes = [(rows, width), (half, width), (rows - half, width)]
    return pl.pallas_call(
        base_kernel,
        in_specs=[IN_VMEM] * 4,
        out_specs=[IN_VMEM] * 3,
        out_shape=[pltpu.VMEM(shape, f32) for shape in shapes],
        compiler_params=SMALL,
        cost_estimate=QUICK,
        name="base",
    )(weight_q, moment_q, weight_o, moment_o)


def window_of(n_shard, share, place_ref, shard_ref, lines):
    start = (place_ref[0] * n_shard + shard_ref[0]) * share
    row = lax.broadcasted_iota(jnp.int32, (lines, LANES), 0)
    lane = lax.broadcasted_iota(jnp.int32, (lines, LANES), 1)
    flat = row * LANES + lane
    return lax.rem(start, LANES), (flat >= start) & (flat < start + share)


def norm_terms(n_shard, rows, place_ref, shard_ref, grads, moment, weight):
    lines, share = grads.shape[1] // LANES, moment.shape[1]
    shift, inside = window_of(n_shard, share, place_ref, shard_ref, lines)
    kept = weight[...] - step_size * decay_rate * moment[...]
    kept = jnp.concatenate([kept, jnp.zeros((1, LANES - share), f32)], axis=1)
    kept = pltpu.roll(jnp.broadcast_to(kept, (8, LANES)), shift, 1)[:1]
    square = jnp.concatenate([grads[:, line * LANES : (line + 1) * LANES] for line in range(lines)], axis=0)
    rest = jnp.zeros((rows - lines, LANES), f32)
    shares = jnp.where(inside, kept, 0.0) - step_size * square
    return jnp.concatenate([square, rest], axis=0), jnp.concatenate([shares, rest], axis=0)


def norm_out_kernel(n_shard, place_ref, shard_ref, ours, got, moment, new_moment, new_weight):
    lines, share = new_weight.shape[0], moment.shape[1]
    high = is_high(shard_ref, 1)
    size = ours.shape[1] - LANES
    ours, got = ours[:lines, size:], got[:lines, size:]
    sums = jnp.where(high, got, ours)
    shift, inside = window_of(n_shard, share, place_ref, shard_ref, lines)
    total = jnp.sum(jnp.where(inside, sums, 0.0), axis=0, keepdims=True)
    total = pltpu.roll(jnp.broadcast_to(total, (8, LANES)), LANES - shift, 1)[:1, :share]
    new_moment[...] = decay_rate * moment[...] + total
    new_weight[...] = jnp.where(high, ours, got)


def norm_out(ours, got, moment, place, shard, lines, n_shard):
    return pl.pallas_call(
        functools.partial(norm_out_kernel, n_shard),
        in_specs=[IN_SMEM] * 2 + [IN_VMEM] * 3,
        out_specs=[IN_VMEM] * 2,
        out_shape=[jax.ShapeDtypeStruct(moment.shape, f32), jax.ShapeDtypeStruct((lines, LANES), f32)],
        compiler_params=SMALL,
        cost_estimate=QUICK,
        name="norm_out",
    )(place, shard, ours, got, moment)


def first_kernel(n_shard, place_ref, shard_ref, *refs):
    sources, norms, (corr, give_corr, keep, give) = refs[:6], refs[6:9], refs[9:13]
    buffer, bases, norm_buffers, sems, small_sems = refs[13], refs[14], refs[15:18], refs[18], refs[19]
    rank, size = bases.shape[1], corr.shape[2]
    high = is_high(shard_ref, 1)
    small = zip(sources[4:] + norms, [bases.at[0], bases.at[1], *norm_buffers])
    small_copies = [pltpu.make_async_copy(source, target, small_sems.at[k]) for k, (source, target) in enumerate(small)]
    copies = [pltpu.make_async_copy(source, buffer.at[j], sems.at[j]) for j, source in enumerate(sources[:4])]
    for copy in small_copies + copies:
        copy.start()
    for copy in small_copies:
        copy.wait()
    sums, shares = norm_terms(n_shard, rank, place_ref, shard_ref, *norm_buffers)
    keep[:, size:] = jnp.where(high, shares, sums)
    give[:, size:] = jnp.where(high, sums, shares)
    totals, parts = [], []
    for p in range(2):
        copies[p].wait()
        copies[2 + p].wait()
        totals.append(buffer[p] + buffer[2 + p])
        corr[p] = totals[p]
        parts.append(stacked(bases[p], totals[p], NN))
    give_corr[...] = jnp.where(high, totals[0], totals[1])
    keep[:, :size] = jnp.where(high, parts[1], parts[0])
    give[:, :size] = jnp.where(high, parts[0], parts[1])


def first(grads, errors, bases, norms, place, shard, n_shard):
    width, size = grads[0].shape
    rank = bases[0].shape[0]
    part = pltpu.VMEM((rank, size + LANES), f32)
    return pl.pallas_call(
        functools.partial(first_kernel, n_shard),
        in_specs=[IN_SMEM] * 2 + [IN_HBM] * 9,
        out_specs=[IN_VMEM] * 4,
        out_shape=[pltpu.VMEM((2, width, size), f32), pltpu.VMEM((width, size), f32), part, part],
        scratch_shapes=[
            pltpu.VMEM((4, width, size), f32),
            pltpu.VMEM((2, rank, width), f32),
            *(pltpu.VMEM(array.shape, f32) for array in norms),
            pltpu.SemaphoreType.DMA((4,)),
            pltpu.SemaphoreType.DMA((5,)),
        ],
        compiler_params=LARGE,
        name="first",
    )(place, shard, *hold(pltpu.HBM, *grads, *errors, *bases, *norms))


def both_shares(shard_ref, corr, other):
    return jnp.concatenate([corr[shard_ref[0] & 1], other[...]], axis=0)


def right_kernel(count, shard_ref, whole, corr, other, *refs):
    size = corr.shape[2]
    right, left, *extra = refs[count:]
    left[:, :size] = whole[:, :size]
    if count:
        left[:, size:] = refs[0][...]
    if extra:
        extra[0][...] = whole[:, size:]
    right[...] = stacked(whole[:, :size], both_shares(shard_ref, corr, other), NT)


def right_of(whole, shard, corr, other, *more):
    rank = whole.shape[0]
    width, size = other.shape
    beside = whole.shape[1] - size
    shapes = [(rank, 2 * width), (rank, size + sum(array.shape[1] for array in more))] + ([(rank, beside)] if beside else [])
    return pl.pallas_call(
        functools.partial(right_kernel, len(more)),
        in_specs=[IN_SMEM] + [IN_VMEM] * (3 + len(more)),
        out_specs=[IN_VMEM] * len(shapes),
        out_shape=[pltpu.VMEM(shape, f32) for shape in shapes],
        compiler_params=SMALL,
        cost_estimate=QUICK,
        name="right",
    )(shard, whole, *hold(pltpu.VMEM, corr, other), *more)


def left_kernel(mask, shard_ref, right, inverse, corr, other, keep, give):
    basis = exact(inverse[0], right[...], NN)
    part = stacked(basis, both_shares(shard_ref, corr, other), NN)
    half = part.shape[0] // 2
    high = is_high(shard_ref, mask)
    keep[...] = jnp.where(high, part[half:], part[:half])
    give[...] = jnp.where(high, part[:half], part[half:])


def left_of(right, inverse, shard, mask, corr, other):
    half = pltpu.VMEM((right.shape[0] // 2, other.shape[1]), f32)
    return pl.pallas_call(
        functools.partial(left_kernel, mask),
        in_specs=[IN_SMEM] + [IN_VMEM] * 4,
        out_specs=[IN_VMEM] * 2,
        out_shape=[half, half],
        compiler_params=SMALL,
        cost_estimate=QUICK,
        name="left",
    )(shard, right, inverse, *hold(pltpu.VMEM, corr, other))


def eliminate(gram_q, gram_o, rank):
    width = 4 * rank
    lane = lax.broadcasted_iota(jnp.int32, (rank, width), 1)
    row = lax.broadcasted_iota(jnp.int32, (rank, width), 0)
    square = (rank, rank)
    eye = (lax.broadcasted_iota(jnp.int32, square, 0) == lax.broadcasted_iota(jnp.int32, square, 1)).astype(f32)
    work = jnp.concatenate([gram_q, eye, gram_o, eye], axis=1)
    first_half = lane < 2 * rank
    scale = jnp.ones((rank, width), f32)
    for base in range(0, rank, GROUP):
        columns = []
        for k in range(base, base + GROUP):
            of_q = jnp.broadcast_to(work[:, k : k + 1], (rank, width))
            of_o = jnp.broadcast_to(work[:, 2 * rank + k : 2 * rank + k + 1], (rank, width))
            columns.append(jnp.where(first_half, of_q, of_o))
        for j in range(GROUP):
            k = base + j
            pivot = columns[j][k : k + 1]
            factor = jnp.where(row > k, columns[j] * (1.0 / pivot), 0.0)
            scale = jnp.where(row == k, pivot, scale)
            for i in range(j + 1, GROUP):
                columns[i] = columns[i] - factor * columns[i][k : k + 1]
            work = work - factor * work[k : k + 1]
    work = work * lax.rsqrt(scale)
    return work[:, rank : 2 * rank], work[:, 3 * rank :]


def inverse_kernel(size, ours, theirs, out):
    rank = out.shape[1]
    left, other = ours[:, :size], theirs[:, :size]
    out[0], out[1] = eliminate(exact(left, left, NT), exact(other, other, NT), rank)


def inverse_of(ours, theirs, size):
    rank = ours.shape[0]
    return pl.pallas_call(
        functools.partial(inverse_kernel, size),
        out_shape=pltpu.VMEM((2, rank, rank), f32),
        compiler_params=SMALL,
        cost_estimate=SLOW,
        name="inverse",
    )(ours, theirs)


def stack_kernel(place_ref, ours, theirs, stack, own):
    count = own.shape[2]
    index = place_ref[0]
    for p, left in enumerate((ours, theirs)):
        high, middle, low = three(left[:, : stack.shape[2]])
        stack[p] = jnp.concatenate([high, middle, low, high, middle, high], axis=0)
        window = left[:, pl.ds(pl.multiple_of(index * LANES, LANES), 2 * LANES)]
        own[p] = pltpu.roll(window, 2 * LANES - index * (count - LANES), 1)[:, :count]


def stack_of(ours, theirs, place, size, count):
    rank = ours.shape[0]
    return pl.pallas_call(
        stack_kernel,
        in_specs=[IN_SMEM, IN_VMEM, IN_VMEM],
        out_specs=[IN_VMEM] * 2,
        out_shape=[pltpu.VMEM((2, 6 * rank, size), bf16), pltpu.VMEM((2, rank, count), f32)],
        compiler_params=SMALL,
        cost_estimate=SLOW,
        name="stack",
    )(place, ours, theirs)


def finish_kernel(chunks, shard_ref, corr, rows, stack, inverse, right, their_right, own, moment_q, moment_o, *refs):
    outs, (buffer, new_moments, sems) = refs[:6], refs[6:]
    width = moment_q.shape[1]
    height = width // chunks
    copies = []

    def send(index, source, to_q, to_o, sem):
        for p, target in enumerate((to_q, to_o)):

            @pl.when(index == p)
            def _(target=target):
                pltpu.make_async_copy(source, target, sem).start()

        copies.append(pltpu.make_async_copy(source, to_q, sem))

    for theirs, factor in enumerate((right, their_right)):
        index = (shard_ref[0] & 1) ^ theirs
        factor = factor[:, width * theirs : width * (theirs + 1)]
        scaled = exact(inverse[theirs], exact(inverse[theirs], factor, NN), TN)
        high, middle, low = three(scaled.T)
        lefts = jnp.concatenate([high, high, high, middle, middle, low], axis=1)
        for c in range(chunks):
            at = pl.ds(c * height, height)
            decoded = lax.dot_general(lefts[c * height : (c + 1) * height], stack[theirs], NN, preferred_element_type=f32)
            buffer[theirs, 0, at, :] = rows[pl.ds(pl.multiple_of(index * width + c * height, 8), height), :] - step_size * decoded
            buffer[theirs, 1, at, :] = corr[index, at, :] - decoded
            for k in range(2):
                send(index, buffer.at[theirs, k, at, :], outs[2 * k].at[at, :], outs[2 * k + 1].at[at, :], sems.at[theirs, k, c])
        moment = jnp.where(index == 0, moment_q[...], moment_o[...])
        new_moments[theirs] = decay_rate * moment + exact(own[theirs], scaled, TN)
        send(index, new_moments.at[theirs], outs[4], outs[5], sems.at[theirs, 2, 0])
    for copy in copies:
        copy.wait()


def finish(shard, corr, rows, stack, inverse, right, their_right, own, moment_q, moment_o):
    width, size = corr.shape[1:]
    chunks = 3
    return pl.pallas_call(
        functools.partial(finish_kernel, chunks),
        in_specs=[IN_SMEM] + [IN_VMEM] * 9,
        out_specs=[IN_HBM] * 6,
        out_shape=[pltpu.HBM((width, size), f32)] * 4 + [pltpu.HBM(moment_q.shape, f32)] * 2,
        scratch_shapes=[
            pltpu.VMEM((2, 2, width, size), f32),
            pltpu.VMEM((2,) + moment_q.shape, f32),
            pltpu.SemaphoreType.DMA((2, 3, chunks)),
        ],
        compiler_params=LARGE,
        name="finish",
    )(shard, *hold(pltpu.VMEM, corr, rows), stack, inverse, right, their_right, own, moment_q, moment_o)


def finish_plain(high, corr, base, lefts, inverse, rights, moments):
    rows, width = moments[0].shape
    start = lax.axis_index("rep") * rows
    bases = lax.all_gather(base, "rep", axis=0, tiled=True)
    decodeds = []
    for p in range(2):
        factor = rights[p][:, p * width : (p + 1) * width]
        scaled = exact(inverse[p], exact(inverse[p], factor, NN), TN)
        decodeds.append(exact(scaled, lefts[p], TN))
    ours, theirs = decodeds
    weights, new_moments, errors = [], [], []
    for p, decoded in enumerate((jnp.where(high, theirs, ours), jnp.where(high, ours, theirs))):
        weights.append(bases[:, p * width : (p + 1) * width].T - step_size * decoded)
        new_moments.append(decay_rate * moments[p] + lax.dynamic_slice_in_dim(decoded, start, rows, 1).T)
        errors.append(corr[p] - decoded)
    return weights + errors + new_moments


def per_device(n_rep, n_shard, q_grad, o_grad, q_error, o_error, q_basis, o_basis, q_moment, o_moment, q_weight, o_weight, norm_grads, norm_moment, norm_weight):
    rank = q_basis.shape[1]
    size = q_grad.shape[1]
    flat = norm_grads.shape[-1]
    row_count = q_moment.shape[0]
    place = lax.axis_index("rep").astype(jnp.int32).reshape(1)
    shard = lax.axis_index("shard").astype(jnp.int32).reshape(1)

    gather = Gather(*base_of(q_weight, q_moment, o_weight, o_moment), place, n_rep)
    norm_moment, norm_weight = norm_moment.reshape(1, -1), norm_weight.reshape(1, -1)
    norms = (norm_grads[0], norm_moment, norm_weight)
    corr, give_corr, keep, give = first((q_grad[0].T, o_grad[0].T), (q_error[0].T, o_error[0].T), (q_basis.T, o_basis.T), norms, place, shard, n_shard)
    masks = halves(n_shard)

    def ending(left, theirs):
        gains = norm_out(left, theirs, norm_moment, place, shard, flat // LANES, n_shard)
        return (gains, *stack_of(left, theirs, place, size, row_count)) if gather.paired else (gains,)

    for sweep in range(ROUNDS):
        last = sweep == ROUNDS - 1
        if sweep == 0:
            whole, other_corr = sum_over_all(keep, give, shard, masks, n_rep, n_shard, gather, 0, give_corr)
        else:
            whole, _ = sum_over_all(keep, give, shard, masks[1:], n_rep, n_shard, gather, 2 * sweep)
        right, left, *beside = right_of(whole, shard, corr, other_corr, *([norms] if last else []))
        if sweep == 0:
            (norms,) = beside
        theirs = swap(left, "shard", masks[0], n_shard) if last else left
        gather.tasks[2 * sweep + 1, 4 if last else 1] = (functools.partial(inverse_of, size=size), left, theirs)
        if last:
            gather.tasks[3, 2] = (ending, left, theirs)
        right = sum_over(right, n_rep, gather, 2 * sweep + 1)
        inverse = gather.results[2 * sweep + 1, 4 if last else 1]
        if not last:
            keep, give = left_of(right, inverse, shard, masks[1], corr, other_corr)
    their_right = swap(right, "shard", masks[0], n_shard)
    (norm_moment_new, norm_weight_new), *terms = gather.results[3, 2]
    if gather.paired:
        stack, own = terms
        their_right, turned = lax.optimization_barrier((their_right, gather.blocks["turned_last_b"]))
        gather.insert([turned], ["turned_last_b"])
        outs = finish(shard, corr, gather.rows, stack, inverse, right, their_right, own, q_moment, o_moment)
    else:
        outs = finish_plain((shard[0] & 1) != 0, corr, gather.blocks["own"], (left[:, :size], theirs[:, :size]), inverse, (right, their_right), (q_moment, o_moment))
    weight_q, weight_o, error_q, error_o, q_moment_new, o_moment_new = outs
    return (
        weight_q.T,
        weight_o.T,
        q_moment_new,
        o_moment_new,
        error_q.T[None],
        error_o.T[None],
        norm_weight_new.reshape(flat),
        norm_moment_new.reshape(-1),
    )


def solution(mesh):
    n_rep, n_shard = mesh.shape["rep"], mesh.shape["shard"]

    def whole(*arrays):
        return per_device(n_rep, n_shard, *arrays)

    return jax.shard_map(
        whole,
        mesh=mesh,
        in_specs=(
            P("rep", None, "shard"),
            P("rep", None, "shard"),
            P("rep", None, "shard"),
            P("rep", None, "shard"),
            P("shard", None),
            P("shard", None),
            P("rep", "shard"),
            P("rep", "shard"),
            P("rep", "shard"),
            P("rep", "shard"),
            P("rep", "shard", None),
            P(("rep", "shard")),
            P(("rep", "shard")),
        ),
        out_specs=(
            P(None, "shard"),
            P(None, "shard"),
            P("rep", "shard"),
            P("rep", "shard"),
            P("rep", None, "shard"),
            P("rep", None, "shard"),
            P(),
            P(("rep", "shard")),
        ),
        check_vma=False,
    )
```

```python
import functools

import jax
import jax.numpy as jnp
from jax import lax
from jax.experimental import pallas as pl
from jax.experimental.pallas import tpu as pltpu
from jax.sharding import PartitionSpec as P

ROUNDS = 2
GROUP = 8
LANES = 128
MEETINGS = (1, 2)

highest = lax.Precision.HIGHEST
decay_rate = 0.9
step_size = 0.1
f32 = jnp.float32
bf16 = jnp.bfloat16
NN = (((1,), (0,)), ((), ()))
NT = (((1,), (1,)), ((), ()))
TN = (((0,), (0,)), ((), ()))

IN_HBM = pl.BlockSpec(memory_space=pltpu.HBM)
IN_VMEM = pl.BlockSpec(memory_space=pltpu.VMEM)
IN_SMEM = pl.BlockSpec(memory_space=pltpu.SMEM)
SMALL = pltpu.CompilerParams(vmem_limit_bytes=6 * 2**20)
LARGE = pltpu.CompilerParams(vmem_limit_bytes=12 * 2**20)
QUICK = pl.CostEstimate(flops=1000, bytes_accessed=1000, transcendentals=0)
SLOW = pl.CostEstimate(flops=1000, bytes_accessed=6_000_000, transcendentals=0)


def hold(space, *arrays):
    return [pltpu.with_memory_space_constraint(array, space) for array in arrays]


def exact(left, right, dims):
    return lax.dot_general(left, right, dims, precision=highest, preferred_element_type=f32)


def three(x):
    high = x.astype(bf16)
    rest = x - high.astype(f32)
    middle = rest.astype(bf16)
    low = (rest - middle.astype(f32)).astype(bf16)
    return high, middle, low


def stacked(left, right, dims):
    rows = left.shape[0]
    left_high, left_middle, left_low = three(left)
    right_high, right_middle, right_low = three(right)
    lefts = jnp.concatenate([left_high, left_middle, left_low], axis=0)
    of_high = lax.dot_general(lefts, right_high, dims, preferred_element_type=f32)
    of_middle = lax.dot_general(lefts[: 2 * rows], right_middle, dims, preferred_element_type=f32)
    of_low = lax.dot_general(left_high, right_low, dims, preferred_element_type=f32)
    small = (of_high[2 * rows :] + of_middle[rows:]) + of_low
    return of_high[:rows] + ((of_high[rows : 2 * rows] + of_middle[:rows]) + small)


def halves(count):
    masks = []
    mask = 1
    while mask < count:
        masks.append(mask)
        mask *= 2
    return masks


def swap(block, axis, mask, count):
    pairs = [(i, i ^ mask) for i in range(count)]
    return lax.ppermute(block, axis, pairs)


def sum_over(block, count, gather, stage):
    for mask in halves(count):
        block = gather.before(block, stage, mask)
        block = gather.start_tasks(block, stage, mask)
        block = block + gather.end_tasks(swap(block, "rep", mask, count), stage, mask)
        block = gather.after(block, stage, mask)
    return gather.after(gather.before(block, stage, 0), stage, 0)


def sum_over_all(keep, give, shard, masks, n_rep, n_shard, gather, stage, along=None):
    keep = gather.after(keep, stage, "begin")
    partner = None
    for mask, after in zip(masks, masks[1:] + [None]):
        got = swap(give, "shard", mask, n_shard)
        if after is not None:
            keep, give = split(keep, got, shard, after)
            if along is not None and partner is None:
                give, along = lax.optimization_barrier((give, along))
                partner = swap(along, "shard", mask, n_shard)
            keep = gather.after(gather.before(keep, stage, "core"), stage, "core")
    if stage in MEETINGS:
        gather.meet(stage, keep)
    part = sum_over(keep + got, n_rep, gather, stage)
    for mask in reversed(halves(n_shard)[1:]):
        part = gather.start_tasks(part, stage, "x")
        got = gather.end_tasks(swap(part, "shard", mask, n_shard), stage, "x")
        part = gather.before(join(part, got, shard, mask), stage, "joined")
    return part, partner


def is_high(place_ref, mask):
    return (place_ref[0] & mask) != 0


def split_kernel(mask, shard_ref, ours, got, keep, give):
    total = ours[...] + got[...]
    half = total.shape[0] // 2
    high = is_high(shard_ref, mask)
    keep[...] = jnp.where(high, total[half:], total[:half])
    give[...] = jnp.where(high, total[:half], total[half:])


def split(ours, got, shard, mask):
    half = pltpu.VMEM((ours.shape[0] // 2, ours.shape[1]), f32)
    return pl.pallas_call(
        functools.partial(split_kernel, mask),
        in_specs=[IN_SMEM, IN_VMEM, IN_VMEM],
        out_specs=[IN_VMEM] * 2,
        out_shape=[half, half],
        compiler_params=SMALL,
        cost_estimate=QUICK,
        name="split",
    )(shard, ours, got)


def joined(shard_ref, mask, ours, got):
    high = is_high(shard_ref, mask)
    return jnp.concatenate([jnp.where(high, got, ours), jnp.where(high, ours, got)], axis=0)


def join_kernel(mask, shard_ref, ours, got, whole):
    whole[...] = joined(shard_ref, mask, ours[...], got[...])


def join(ours, got, shard, mask):
    return pl.pallas_call(
        functools.partial(join_kernel, mask),
        in_specs=[IN_SMEM, IN_VMEM, IN_VMEM],
        out_specs=IN_VMEM,
        out_shape=pltpu.VMEM((2 * ours.shape[0], ours.shape[1]), f32),
        compiler_params=SMALL,
        cost_estimate=QUICK,
        name="join",
    )(shard, ours, got)


class Gather:
    PLAN = (
        ("near", "own", 2, (0, "core"), (0, "joined")),
        ("turned", "own", 1, (0, 1), (1, 4)),
        ("far_a", "own_a", 4, (0, 4), (1, 2)),
        ("turned_near", "near", 1, (1, 1), (2, 2)),
        ("last_a", "far_a", 2, (1, 2), (2, 2)),
        ("turned_far_a", "far_a", 1, (1, 2), (2, 2)),
        ("far_b", "own_b", 4, (2, "begin"), (2, 4)),
        ("turned_last_a", "last_a", 1, (2, 1), (2, "joined")),
        ("last_b", "far_b", 2, (2, 2), (3, 2)),
        ("turned_far_b", "far_b", 1, (2, 2), (3, 2)),
        ("turned_last_b", "last_b", 1, (3, 1), None),
    )
    INSERTS = {
        (1, 1): ("own",),
        (2, 1): ("near", "turned"),
        (2, 2): ("far_a", "last_a"),
        (2, 4): ("turned_near",),
        (2, "x"): ("turned_far_a",),
        (3, 1): ("far_b",),
        (3, 4): ("turned_far_b", "last_b", "turned_last_a"),
    }
    PLACES = {"own": 0, "turned": 1, "near": 2, "far": 4, "last": 6, "turned_near": 3, "turned_far": 5, "turned_last": 7}

    def place_of(self, name):
        whole = name.removesuffix("_a").removesuffix("_b")
        skipped = self.blocks["own"].shape[0] - self.blocks[name].shape[0]
        return self.PLACES[whole], skipped if name.endswith("_b") else 0

    def __init__(self, own, own_a, own_b, place, count, n_shard):
        self.count = count
        self.n_shard = n_shard
        self.place = place
        self.blocks = {"own": own, "own_a": own_a, "own_b": own_b}
        self.paired = count == 8 and own.shape[0] % 16 == 0
        self.rows = None
        self.tasks = {}
        self.results = {}
        self.send(None)

    def send(self, point):
        if self.paired:
            for name, source, mask, after, _ in self.PLAN:
                if after == point:
                    self.blocks[name] = swap(self.blocks[source], "rep", mask, self.count)

    def meet(self, stage, array):
        self.tasks[stage, 4] = (functools.partial(swap, axis="shard", mask=1, count=self.n_shard), array)

    def met(self, stage):
        return [self.results[stage, 4]] if stage in MEETINGS else []

    def start_tasks(self, value, stage, mask):
        point = (stage, mask)
        if point in self.tasks:
            task, *inputs = self.tasks[point]
            value, *inputs = lax.optimization_barrier((value, *inputs))
            self.results[point] = task(*inputs)
        if self.paired and point in self.INSERTS:
            value, *blocks = lax.optimization_barrier((value, *(self.blocks[name] for name in self.INSERTS[point])))
            self.insert(blocks, self.INSERTS[point])
        if self.paired:
            for name, source, _, after, _ in self.PLAN:
                if after == ("beside",) + point:
                    if point in self.INSERTS:
                        self.rows, self.blocks[source] = lax.optimization_barrier((self.rows, self.blocks[source]))
                    else:
                        self.results[point], self.blocks[source] = lax.optimization_barrier((self.results[point], self.blocks[source]))
            self.send(("beside",) + point)
        return value

    def end_tasks(self, value, stage, mask):
        point = (stage, mask)
        if point in self.tasks:
            value, self.results[point] = lax.optimization_barrier((value, self.results[point]))
        if self.paired and point in self.INSERTS:
            value, self.rows = lax.optimization_barrier((value, self.rows))
        return value

    def insert(self, blocks, names):
        self.rows = insert(self.place, self.rows, blocks, [self.place_of(name) for name in names], self.blocks["own"].shape[0], self.count)

    def before(self, value, stage, mask):
        if self.paired:
            for name, _, _, _, by in self.PLAN:
                if by == (stage, mask):
                    value, self.blocks[name] = lax.optimization_barrier((value, self.blocks[name]))
        return value

    def after(self, value, stage, mask):
        if self.paired:
            for name, source, _, after, _ in self.PLAN:
                if after == (stage, mask) and source in self.blocks:
                    value, self.blocks[source] = lax.optimization_barrier((value, self.blocks[source]))
            self.send((stage, mask))
        return value


def insert_kernel(masks, rows_each, place_ref, *refs):
    blocks, rows, out = refs[: len(masks)], refs[len(masks) : -1], refs[-1]
    if not rows:
        out[...] = jnp.zeros_like(out)
    height = out.shape[0]
    window = 2 * LANES
    lane = lax.broadcasted_iota(jnp.int32, (height, window), 1)
    for block, (mask, skipped) in zip(blocks, masks):
        count = block.shape[0]
        index = place_ref[0] ^ mask
        shift = index * (rows_each - LANES) + skipped
        turned = jnp.concatenate([block[...].T, jnp.zeros((height, window - count), f32)], axis=1)
        turned = pltpu.roll(turned, shift, 1)
        at = pl.ds(pl.multiple_of(index * LANES, LANES), window)
        out[:, at] = jnp.where((lane >= shift) & (lane < shift + count), turned, out[:, at])


def insert(place, rows, blocks, masks, rows_each, count):
    height, width = blocks[0].shape[1], rows_each * count
    old = [] if rows is None else hold(pltpu.VMEM, rows)
    return pl.pallas_call(
        functools.partial(insert_kernel, masks, rows_each),
        in_specs=[IN_SMEM] + [IN_VMEM] * (len(blocks) + len(old)),
        out_specs=IN_VMEM,
        out_shape=pltpu.VMEM((height, width), f32),
        input_output_aliases={1 + len(blocks): 0} if old else {},
        compiler_params=SMALL,
        cost_estimate=SLOW,
        name="insert",
    )(place, *blocks, *old)


def base_kernel(weight_q, moment_q, weight_o, moment_o, own, *parts):
    drop = step_size * decay_rate
    base = jnp.concatenate([weight_q[...] - drop * moment_q[...], weight_o[...] - drop * moment_o[...]], axis=1)
    own[...] = base
    rows = base.shape[0]
    first_part, second_part = parts
    first_part[...] = base[: first_part.shape[0]]
    second_part[...] = base[rows - second_part.shape[0] :]


def base_of(weight_q, moment_q, weight_o, moment_o):
    rows, width = weight_q.shape[0], 2 * weight_q.shape[1]
    half = rows // 2
    shapes = [(rows, width), (half, width), (rows - half, width)]
    return pl.pallas_call(
        base_kernel,
        in_specs=[IN_VMEM] * 4,
        out_specs=[IN_VMEM] * 3,
        out_shape=[pltpu.VMEM(shape, f32) for shape in shapes],
        compiler_params=SMALL,
        cost_estimate=QUICK,
        name="base",
    )(weight_q, moment_q, weight_o, moment_o)


def window_of(n_shard, share, place_ref, shard_ref, lines):
    start = (place_ref[0] * n_shard + shard_ref[0]) * share
    row = lax.broadcasted_iota(jnp.int32, (lines, LANES), 0)
    lane = lax.broadcasted_iota(jnp.int32, (lines, LANES), 1)
    flat = row * LANES + lane
    return lax.rem(start, LANES), (flat >= start) & (flat < start + share)


def norm_terms(n_shard, rows, place_ref, shard_ref, grads, moment, weight):
    lines, share = grads.shape[1] // LANES, moment.shape[1]
    shift, inside = window_of(n_shard, share, place_ref, shard_ref, lines)
    kept = weight[...] - step_size * decay_rate * moment[...]
    kept = jnp.concatenate([kept, jnp.zeros((1, LANES - share), f32)], axis=1)
    kept = pltpu.roll(jnp.broadcast_to(kept, (8, LANES)), shift, 1)[:1]
    square = jnp.concatenate([grads[:, line * LANES : (line + 1) * LANES] for line in range(lines)], axis=0)
    rest = jnp.zeros((rows - lines, LANES), f32)
    shares = jnp.where(inside, kept, 0.0) - step_size * square
    return jnp.concatenate([square, rest], axis=0), jnp.concatenate([shares, rest], axis=0)


def norm_out_kernel(n_shard, place_ref, shard_ref, ours, got, moment, new_moment, new_weight):
    lines, share = new_weight.shape[0], moment.shape[1]
    high = is_high(shard_ref, 1)
    size = ours.shape[1] - LANES
    ours, got = ours[:lines, size:], got[:lines, size:]
    sums = jnp.where(high, got, ours)
    shift, inside = window_of(n_shard, share, place_ref, shard_ref, lines)
    total = jnp.sum(jnp.where(inside, sums, 0.0), axis=0, keepdims=True)
    total = pltpu.roll(jnp.broadcast_to(total, (8, LANES)), LANES - shift, 1)[:1, :share]
    new_moment[...] = decay_rate * moment[...] + total
    new_weight[...] = jnp.where(high, ours, got)


def norm_out(ours, got, moment, place, shard, lines, n_shard):
    return pl.pallas_call(
        functools.partial(norm_out_kernel, n_shard),
        in_specs=[IN_SMEM] * 2 + [IN_VMEM] * 3,
        out_specs=[IN_VMEM] * 2,
        out_shape=[jax.ShapeDtypeStruct(moment.shape, f32), jax.ShapeDtypeStruct((lines, LANES), f32)],
        compiler_params=SMALL,
        cost_estimate=QUICK,
        name="norm_out",
    )(place, shard, ours, got, moment)


def first_kernel(n_shard, place_ref, shard_ref, *refs):
    sources, norms, (corr, give_corr, keep, give) = refs[:6], refs[6:9], refs[9:13]
    buffer, bases, norm_buffers, sems, small_sems = refs[13], refs[14], refs[15:18], refs[18], refs[19]
    rank, size = bases.shape[1], corr.shape[2]
    high = is_high(shard_ref, 1)
    small = zip(sources[4:] + norms, [bases.at[0], bases.at[1], *norm_buffers])
    small_copies = [pltpu.make_async_copy(source, target, small_sems.at[k]) for k, (source, target) in enumerate(small)]
    copies = [pltpu.make_async_copy(source, buffer.at[j], sems.at[j]) for j, source in enumerate(sources[:4])]
    for copy in small_copies + copies:
        copy.start()
    for copy in small_copies:
        copy.wait()
    sums, shares = norm_terms(n_shard, rank, place_ref, shard_ref, *norm_buffers)
    keep[:, size:] = jnp.where(high, shares, sums)
    give[:, size:] = jnp.where(high, sums, shares)
    totals, parts = [], []
    for p in range(2):
        copies[p].wait()
        copies[2 + p].wait()
        totals.append(buffer[p] + buffer[2 + p])
        corr[p] = totals[p]
        parts.append(stacked(bases[p], totals[p], NN))
    give_corr[...] = jnp.where(high, totals[0], totals[1])
    keep[:, :size] = jnp.where(high, parts[1], parts[0])
    give[:, :size] = jnp.where(high, parts[0], parts[1])


def first(grads, errors, bases, norms, place, shard, n_shard):
    width, size = grads[0].shape
    rank = bases[0].shape[0]
    part = pltpu.VMEM((rank, size + LANES), f32)
    return pl.pallas_call(
        functools.partial(first_kernel, n_shard),
        in_specs=[IN_SMEM] * 2 + [IN_HBM] * 9,
        out_specs=[IN_VMEM] * 4,
        out_shape=[pltpu.VMEM((2, width, size), f32), pltpu.VMEM((width, size), f32), part, part],
        scratch_shapes=[
            pltpu.VMEM((4, width, size), f32),
            pltpu.VMEM((2, rank, width), f32),
            *(pltpu.VMEM(array.shape, f32) for array in norms),
            pltpu.SemaphoreType.DMA((4,)),
            pltpu.SemaphoreType.DMA((5,)),
        ],
        compiler_params=LARGE,
        name="first",
    )(place, shard, *hold(pltpu.HBM, *grads, *errors, *bases, *norms))


def both_shares(shard_ref, corr, other):
    return jnp.concatenate([corr[shard_ref[0] & 1], other[...]], axis=0)


def right_kernel(count, waits, shard_ref, whole, corr, other, *refs):
    size = corr.shape[2]
    right, left, *extra = refs[count + waits :]
    left[:, :size] = whole[:, :size]
    if count:
        left[:, size:] = refs[0][...]
    if extra:
        extra[0][...] = whole[:, size:]
    right[...] = stacked(whole[:, :size], both_shares(shard_ref, corr, other), NT)


def right_of(whole, shard, corr, other, more, waits):
    rank = whole.shape[0]
    width, size = other.shape
    beside = whole.shape[1] - size
    shapes = [(rank, 2 * width), (rank, size + sum(array.shape[1] for array in more))] + ([(rank, beside)] if beside else [])
    return pl.pallas_call(
        functools.partial(right_kernel, len(more), len(waits)),
        in_specs=[IN_SMEM] + [IN_VMEM] * (3 + len(more) + len(waits)),
        out_specs=[IN_VMEM] * len(shapes),
        out_shape=[pltpu.VMEM(shape, f32) for shape in shapes],
        compiler_params=SMALL,
        cost_estimate=QUICK,
        name="right",
    )(shard, whole, *hold(pltpu.VMEM, corr, other), *more, *waits)


def left_kernel(mask, shard_ref, right, inverse, corr, other, *refs):
    keep, give = refs[-2:]
    basis = exact(inverse[0], right[...], NN)
    part = stacked(basis, both_shares(shard_ref, corr, other), NN)
    half = part.shape[0] // 2
    high = is_high(shard_ref, mask)
    keep[...] = jnp.where(high, part[half:], part[:half])
    give[...] = jnp.where(high, part[:half], part[half:])


def left_of(right, inverse, shard, mask, corr, other, waits):
    half = pltpu.VMEM((right.shape[0] // 2, other.shape[1]), f32)
    return pl.pallas_call(
        functools.partial(left_kernel, mask),
        in_specs=[IN_SMEM] + [IN_VMEM] * (4 + len(waits)),
        out_specs=[IN_VMEM] * 2,
        out_shape=[half, half],
        compiler_params=SMALL,
        cost_estimate=QUICK,
        name="left",
    )(shard, right, inverse, *hold(pltpu.VMEM, corr, other), *waits)


def eliminate(gram_q, gram_o, rank):
    width = 4 * rank
    lane = lax.broadcasted_iota(jnp.int32, (rank, width), 1)
    row = lax.broadcasted_iota(jnp.int32, (rank, width), 0)
    square = (rank, rank)
    eye = (lax.broadcasted_iota(jnp.int32, square, 0) == lax.broadcasted_iota(jnp.int32, square, 1)).astype(f32)
    work = jnp.concatenate([gram_q, eye, gram_o, eye], axis=1)
    first_half = lane < 2 * rank
    scale = jnp.ones((rank, width), f32)
    for base in range(0, rank, GROUP):
        columns = []
        for k in range(base, base + GROUP):
            of_q = jnp.broadcast_to(work[:, k : k + 1], (rank, width))
            of_o = jnp.broadcast_to(work[:, 2 * rank + k : 2 * rank + k + 1], (rank, width))
            columns.append(jnp.where(first_half, of_q, of_o))
        for j in range(GROUP):
            k = base + j
            pivot = columns[j][k : k + 1]
            factor = jnp.where(row > k, columns[j] * (1.0 / pivot), 0.0)
            scale = jnp.where(row == k, pivot, scale)
            for i in range(j + 1, GROUP):
                columns[i] = columns[i] - factor * columns[i][k : k + 1]
            work = work - factor * work[k : k + 1]
    work = work * lax.rsqrt(scale)
    return work[:, rank : 2 * rank], work[:, 3 * rank :]


def inverse_kernel(size, ours, theirs, out):
    rank = out.shape[1]
    left, other = ours[:, :size], theirs[:, :size]
    out[0], out[1] = eliminate(exact(left, left, NT), exact(other, other, NT), rank)


def inverse_of(ours, theirs, size):
    rank = ours.shape[0]
    return pl.pallas_call(
        functools.partial(inverse_kernel, size),
        out_shape=pltpu.VMEM((2, rank, rank), f32),
        compiler_params=SMALL,
        cost_estimate=SLOW,
        name="inverse",
    )(ours, theirs)


def stack_kernel(place_ref, ours, theirs, stack, own):
    count = own.shape[2]
    index = place_ref[0]
    for p, left in enumerate((ours, theirs)):
        high, middle, low = three(left[:, : stack.shape[2]])
        stack[p] = jnp.concatenate([high, middle, low, high, middle, high], axis=0)
        window = left[:, pl.ds(pl.multiple_of(index * LANES, LANES), 2 * LANES)]
        own[p] = pltpu.roll(window, 2 * LANES - index * (count - LANES), 1)[:, :count]


def stack_of(ours, theirs, place, size, count):
    rank = ours.shape[0]
    return pl.pallas_call(
        stack_kernel,
        in_specs=[IN_SMEM, IN_VMEM, IN_VMEM],
        out_specs=[IN_VMEM] * 2,
        out_shape=[pltpu.VMEM((2, 6 * rank, size), bf16), pltpu.VMEM((2, rank, count), f32)],
        compiler_params=SMALL,
        cost_estimate=SLOW,
        name="stack",
    )(place, ours, theirs)


def finish_kernel(chunks, shard_ref, corr, rows, stack, inverse, right, their_right, own, moment_q, moment_o, *refs):
    outs, (buffer, new_moments, sems) = refs[:6], refs[6:]
    width = moment_q.shape[1]
    height = width // chunks
    copies = []

    def send(index, source, to_q, to_o, sem):
        for p, target in enumerate((to_q, to_o)):

            @pl.when(index == p)
            def _(target=target):
                pltpu.make_async_copy(source, target, sem).start()

        copies.append(pltpu.make_async_copy(source, to_q, sem))

    for theirs, factor in enumerate((right, their_right)):
        index = (shard_ref[0] & 1) ^ theirs
        factor = factor[:, width * theirs : width * (theirs + 1)]
        scaled = exact(inverse[theirs], exact(inverse[theirs], factor, NN), TN)
        high, middle, low = three(scaled.T)
        lefts = jnp.concatenate([high, high, high, middle, middle, low], axis=1)
        for c in range(chunks):
            at = pl.ds(c * height, height)
            decoded = lax.dot_general(lefts[c * height : (c + 1) * height], stack[theirs], NN, preferred_element_type=f32)
            buffer[theirs, 0, at, :] = rows[pl.ds(pl.multiple_of(index * width + c * height, 8), height), :] - step_size * decoded
            buffer[theirs, 1, at, :] = corr[index, at, :] - decoded
            for k in range(2):
                send(index, buffer.at[theirs, k, at, :], outs[2 * k].at[at, :], outs[2 * k + 1].at[at, :], sems.at[theirs, k, c])
        moment = jnp.where(index == 0, moment_q[...], moment_o[...])
        new_moments[theirs] = decay_rate * moment + exact(own[theirs], scaled, TN)
        send(index, new_moments.at[theirs], outs[4], outs[5], sems.at[theirs, 2, 0])
    for copy in copies:
        copy.wait()


def finish(shard, corr, rows, stack, inverse, right, their_right, own, moment_q, moment_o):
    width, size = corr.shape[1:]
    chunks = 3
    return pl.pallas_call(
        functools.partial(finish_kernel, chunks),
        in_specs=[IN_SMEM] + [IN_VMEM] * 9,
        out_specs=[IN_HBM] * 6,
        out_shape=[pltpu.HBM((width, size), f32)] * 4 + [pltpu.HBM(moment_q.shape, f32)] * 2,
        scratch_shapes=[
            pltpu.VMEM((2, 2, width, size), f32),
            pltpu.VMEM((2,) + moment_q.shape, f32),
            pltpu.SemaphoreType.DMA((2, 3, chunks)),
        ],
        compiler_params=LARGE,
        name="finish",
    )(shard, *hold(pltpu.VMEM, corr, rows), stack, inverse, right, their_right, own, moment_q, moment_o)


def finish_plain(high, corr, base, lefts, inverse, rights, moments):
    rows, width = moments[0].shape
    start = lax.axis_index("rep") * rows
    bases = lax.all_gather(base, "rep", axis=0, tiled=True)
    decodeds = []
    for p in range(2):
        factor = rights[p][:, p * width : (p + 1) * width]
        scaled = exact(inverse[p], exact(inverse[p], factor, NN), TN)
        decodeds.append(exact(scaled, lefts[p], TN))
    ours, theirs = decodeds
    weights, new_moments, errors = [], [], []
    for p, decoded in enumerate((jnp.where(high, theirs, ours), jnp.where(high, ours, theirs))):
        weights.append(bases[:, p * width : (p + 1) * width].T - step_size * decoded)
        new_moments.append(decay_rate * moments[p] + lax.dynamic_slice_in_dim(decoded, start, rows, 1).T)
        errors.append(corr[p] - decoded)
    return weights + errors + new_moments


def per_device(n_rep, n_shard, q_grad, o_grad, q_error, o_error, q_basis, o_basis, q_moment, o_moment, q_weight, o_weight, norm_grads, norm_moment, norm_weight):
    rank = q_basis.shape[1]
    size = q_grad.shape[1]
    flat = norm_grads.shape[-1]
    row_count = q_moment.shape[0]
    place = lax.axis_index("rep").astype(jnp.int32).reshape(1)
    shard = lax.axis_index("shard").astype(jnp.int32).reshape(1)

    gather = Gather(*base_of(q_weight, q_moment, o_weight, o_moment), place, n_rep, n_shard)
    norm_moment, norm_weight = norm_moment.reshape(1, -1), norm_weight.reshape(1, -1)
    norms = (norm_grads[0], norm_moment, norm_weight)
    corr, give_corr, keep, give = first((q_grad[0].T, o_grad[0].T), (q_error[0].T, o_error[0].T), (q_basis.T, o_basis.T), norms, place, shard, n_shard)
    masks = halves(n_shard)

    def ending(left, theirs):
        gains = norm_out(left, theirs, norm_moment, place, shard, flat // LANES, n_shard)
        return (gains, *stack_of(left, theirs, place, size, row_count)) if gather.paired else (gains,)

    for sweep in range(ROUNDS):
        last = sweep == ROUNDS - 1
        if sweep == 0:
            whole, other_corr = sum_over_all(keep, give, shard, masks, n_rep, n_shard, gather, 0, give_corr)
        else:
            whole, _ = sum_over_all(keep, give, shard, masks[1:], n_rep, n_shard, gather, 2 * sweep)
        right, left, *beside = right_of(whole, shard, corr, other_corr, [norms] if last else [], gather.met(2 * sweep))
        if sweep == 0:
            (norms,) = beside
        theirs = swap(left, "shard", masks[0], n_shard)
        gather.tasks[2 * sweep + 1, 4 if last else 2] = (functools.partial(inverse_of, size=size), left, theirs)
        if last:
            gather.tasks[3, 2] = (ending, left, theirs)
        if 2 * sweep + 1 in MEETINGS:
            gather.meet(2 * sweep + 1, keep)
        right = sum_over(right, n_rep, gather, 2 * sweep + 1)
        inverse = gather.results[2 * sweep + 1, 4 if last else 2]
        if not last:
            keep, give = left_of(right, inverse, shard, masks[1], corr, other_corr, gather.met(1))
    their_right = swap(right, "shard", masks[0], n_shard)
    (norm_moment_new, norm_weight_new), *terms = gather.results[3, 2]
    if gather.paired:
        stack, own = terms
        their_right, turned = lax.optimization_barrier((their_right, gather.blocks["turned_last_b"]))
        gather.insert([turned], ["turned_last_b"])
        outs = finish(shard, corr, gather.rows, stack, inverse, right, their_right, own, q_moment, o_moment)
    else:
        outs = finish_plain((shard[0] & 1) != 0, corr, gather.blocks["own"], (left[:, :size], theirs[:, :size]), inverse, (right, their_right), (q_moment, o_moment))
    weight_q, weight_o, error_q, error_o, q_moment_new, o_moment_new = outs
    return (
        weight_q.T,
        weight_o.T,
        q_moment_new,
        o_moment_new,
        error_q.T[None],
        error_o.T[None],
        norm_weight_new.reshape(flat),
        norm_moment_new.reshape(-1),
    )


def solution(mesh):
    n_rep, n_shard = mesh.shape["rep"], mesh.shape["shard"]

    def whole(*arrays):
        return per_device(n_rep, n_shard, *arrays)

    return jax.shard_map(
        whole,
        mesh=mesh,
        in_specs=(
            P("rep", None, "shard"),
            P("rep", None, "shard"),
            P("rep", None, "shard"),
            P("rep", None, "shard"),
            P("shard", None),
            P("shard", None),
            P("rep", "shard"),
            P("rep", "shard"),
            P("rep", "shard"),
            P("rep", "shard"),
            P("rep", "shard", None),
            P(("rep", "shard")),
            P(("rep", "shard")),
        ),
        out_specs=(
            P(None, "shard"),
            P(None, "shard"),
            P("rep", "shard"),
            P("rep", "shard"),
            P("rep", None, "shard"),
            P("rep", None, "shard"),
            P(),
            P(("rep", "shard")),
        ),
        check_vma=False,
    )
```

```python
import functools

import jax
import jax.numpy as jnp
from jax import lax
from jax.experimental import pallas as pl
from jax.experimental.pallas import tpu as pltpu
from jax.sharding import PartitionSpec as P

ROUNDS = 2
GROUP = 8
LANES = 128
MEETINGS = (1, 2)

highest = lax.Precision.HIGHEST
decay_rate = 0.9
step_size = 0.1
f32 = jnp.float32
bf16 = jnp.bfloat16
NN = (((1,), (0,)), ((), ()))
NT = (((1,), (1,)), ((), ()))
TN = (((0,), (0,)), ((), ()))

IN_HBM = pl.BlockSpec(memory_space=pltpu.HBM)
IN_VMEM = pl.BlockSpec(memory_space=pltpu.VMEM)
IN_SMEM = pl.BlockSpec(memory_space=pltpu.SMEM)
SMALL = pltpu.CompilerParams(vmem_limit_bytes=6 * 2**20)
LARGE = pltpu.CompilerParams(vmem_limit_bytes=12 * 2**20)
QUICK = pl.CostEstimate(flops=1000, bytes_accessed=1000, transcendentals=0)
SLOW = pl.CostEstimate(flops=1000, bytes_accessed=6_000_000, transcendentals=0)


def hold(space, *arrays):
    return [pltpu.with_memory_space_constraint(array, space) for array in arrays]


def exact(left, right, dims):
    return lax.dot_general(left, right, dims, precision=highest, preferred_element_type=f32)


def three(x):
    high = x.astype(bf16)
    rest = x - high.astype(f32)
    middle = rest.astype(bf16)
    low = (rest - middle.astype(f32)).astype(bf16)
    return high, middle, low


def stacked(left, right, dims):
    rows = left.shape[0]
    left_high, left_middle, left_low = three(left)
    right_high, right_middle, right_low = three(right)
    lefts = jnp.concatenate([left_high, left_middle, left_low], axis=0)
    of_high = lax.dot_general(lefts, right_high, dims, preferred_element_type=f32)
    of_middle = lax.dot_general(lefts[: 2 * rows], right_middle, dims, preferred_element_type=f32)
    of_low = lax.dot_general(left_high, right_low, dims, preferred_element_type=f32)
    small = (of_high[2 * rows :] + of_middle[rows:]) + of_low
    return of_high[:rows] + ((of_high[rows : 2 * rows] + of_middle[:rows]) + small)


def halves(count):
    masks = []
    mask = 1
    while mask < count:
        masks.append(mask)
        mask *= 2
    return masks


def swap(block, axis, mask, count):
    pairs = [(i, i ^ mask) for i in range(count)]
    return lax.ppermute(block, axis, pairs)


def sum_over(block, count, gather, stage):
    for mask in halves(count):
        block = gather.before(block, stage, mask)
        block = gather.start_tasks(block, stage, mask)
        block = block + gather.end_tasks(swap(block, "rep", mask, count), stage, mask)
        block = gather.after(block, stage, mask)
    return gather.after(gather.before(block, stage, 0), stage, 0)


def sum_over_all(keep, give, shard, masks, n_rep, n_shard, gather, stage, along=None):
    keep = gather.after(keep, stage, "begin")
    partner = None
    for mask, after in zip(masks, masks[1:] + [None]):
        got = swap(give, "shard", mask, n_shard)
        if after is not None:
            keep, give = split(keep, got, shard, after)
            if along is not None and partner is None:
                give, along = lax.optimization_barrier((give, along))
                partner = swap(along, "shard", mask, n_shard)
            keep = gather.after(gather.before(keep, stage, "core"), stage, "core")
    if stage in MEETINGS:
        gather.meet(stage, keep)
    part = sum_over(keep + got, n_rep, gather, stage)
    for mask in reversed(halves(n_shard)[1:]):
        part = gather.start_tasks(part, stage, "x")
        got = gather.end_tasks(swap(part, "shard", mask, n_shard), stage, "x")
        part = gather.before(join(part, got, shard, mask), stage, "joined")
    return part, partner


def is_high(place_ref, mask):
    return (place_ref[0] & mask) != 0


def split_kernel(mask, shard_ref, ours, got, keep, give):
    total = ours[...] + got[...]
    half = total.shape[0] // 2
    high = is_high(shard_ref, mask)
    keep[...] = jnp.where(high, total[half:], total[:half])
    give[...] = jnp.where(high, total[:half], total[half:])


def split(ours, got, shard, mask):
    half = pltpu.VMEM((ours.shape[0] // 2, ours.shape[1]), f32)
    return pl.pallas_call(
        functools.partial(split_kernel, mask),
        in_specs=[IN_SMEM, IN_VMEM, IN_VMEM],
        out_specs=[IN_VMEM] * 2,
        out_shape=[half, half],
        compiler_params=SMALL,
        cost_estimate=QUICK,
        name="split",
    )(shard, ours, got)


def joined(shard_ref, mask, ours, got):
    high = is_high(shard_ref, mask)
    return jnp.concatenate([jnp.where(high, got, ours), jnp.where(high, ours, got)], axis=0)


def join_kernel(mask, shard_ref, ours, got, whole):
    whole[...] = joined(shard_ref, mask, ours[...], got[...])


def join(ours, got, shard, mask):
    return pl.pallas_call(
        functools.partial(join_kernel, mask),
        in_specs=[IN_SMEM, IN_VMEM, IN_VMEM],
        out_specs=IN_VMEM,
        out_shape=pltpu.VMEM((2 * ours.shape[0], ours.shape[1]), f32),
        compiler_params=SMALL,
        cost_estimate=QUICK,
        name="join",
    )(shard, ours, got)


class Gather:
    PLAN = (
        ("near", "own", 2, (0, "core"), (0, "joined")),
        ("turned", "own", 1, (0, 1), (1, 4)),
        ("far_a", "own_a", 4, (0, 4), (1, 2)),
        ("turned_near", "near", 1, (1, 1), (2, 4)),
        ("last_a", "far_a", 2, (1, 2), (2, 2)),
        ("turned_far_a", "far_a", 1, (1, 2), (2, 2)),
        ("far_b", "own_b", 4, (2, "begin"), (2, 4)),
        ("turned_last_a", "last_a", 1, (2, 1), (2, "joined")),
        ("last_b", "far_b", 2, (2, 2), (3, 2)),
        ("turned_far_b", "far_b", 1, (2, 2), (3, 2)),
        ("turned_last_b", "last_b", 1, (3, 1), None),
    )
    INSERTS = {
        (1, 1): ("own",),
        (2, 1): ("near", "turned"),
        (2, 2): ("far_a", "last_a"),
        (2, 4): ("turned_near",),
        (2, "x"): ("turned_far_a",),
        (3, 1): ("far_b",),
        (3, 4): ("turned_far_b", "last_b", "turned_last_a"),
    }
    PLACES = {"own": 0, "turned": 1, "near": 2, "far": 4, "last": 6, "turned_near": 3, "turned_far": 5, "turned_last": 7}

    def place_of(self, name):
        whole = name.removesuffix("_a").removesuffix("_b")
        skipped = self.blocks["own"].shape[0] - self.blocks[name].shape[0]
        return self.PLACES[whole], skipped if name.endswith("_b") else 0

    def __init__(self, own, own_a, own_b, place, count, n_shard):
        self.count = count
        self.n_shard = n_shard
        self.place = place
        self.blocks = {"own": own, "own_a": own_a, "own_b": own_b}
        self.paired = count == 8 and own.shape[0] % 16 == 0
        self.rows = None
        self.tasks = {}
        self.results = {}
        self.send(None)

    def send(self, point):
        if self.paired:
            for name, source, mask, after, _ in self.PLAN:
                if after == point:
                    self.blocks[name] = swap(self.blocks[source], "rep", mask, self.count)

    def meet(self, stage, array):
        self.tasks[stage, 4] = (functools.partial(swap, axis="shard", mask=1, count=self.n_shard), array)

    def met(self, stage):
        return [self.results[stage, 4]] if stage in MEETINGS else []

    def start_tasks(self, value, stage, mask):
        point = (stage, mask)
        if point in self.tasks:
            task, *inputs = self.tasks[point]
            value, *inputs = lax.optimization_barrier((value, *inputs))
            self.results[point] = task(*inputs)
        if self.paired and point in self.INSERTS:
            value, *blocks = lax.optimization_barrier((value, *(self.blocks[name] for name in self.INSERTS[point])))
            self.insert(blocks, self.INSERTS[point])
        if self.paired:
            for name, source, _, after, _ in self.PLAN:
                if after == ("beside",) + point:
                    if point in self.INSERTS:
                        self.rows, self.blocks[source] = lax.optimization_barrier((self.rows, self.blocks[source]))
                    else:
                        self.results[point], self.blocks[source] = lax.optimization_barrier((self.results[point], self.blocks[source]))
            self.send(("beside",) + point)
        return value

    def end_tasks(self, value, stage, mask):
        point = (stage, mask)
        if point in self.tasks:
            value, self.results[point] = lax.optimization_barrier((value, self.results[point]))
        if self.paired and point in self.INSERTS:
            value, self.rows = lax.optimization_barrier((value, self.rows))
        return value

    def insert(self, blocks, names):
        self.rows = insert(self.place, self.rows, blocks, [self.place_of(name) for name in names], self.blocks["own"].shape[0], self.count)

    def before(self, value, stage, mask):
        if self.paired:
            for name, _, _, _, by in self.PLAN:
                if by == (stage, mask):
                    value, self.blocks[name] = lax.optimization_barrier((value, self.blocks[name]))
        return value

    def after(self, value, stage, mask):
        if self.paired:
            for name, source, _, after, _ in self.PLAN:
                if after == (stage, mask) and source in self.blocks:
                    value, self.blocks[source] = lax.optimization_barrier((value, self.blocks[source]))
            self.send((stage, mask))
        return value


def insert_kernel(masks, rows_each, place_ref, *refs):
    blocks, rows, out = refs[: len(masks)], refs[len(masks) : -1], refs[-1]
    if not rows:
        out[...] = jnp.zeros_like(out)
    height = out.shape[0]
    window = 2 * LANES
    lane = lax.broadcasted_iota(jnp.int32, (height, window), 1)
    for block, (mask, skipped) in zip(blocks, masks):
        count = block.shape[0]
        index = place_ref[0] ^ mask
        shift = index * (rows_each - LANES) + skipped
        turned = jnp.concatenate([block[...].T, jnp.zeros((height, window - count), f32)], axis=1)
        turned = pltpu.roll(turned, shift, 1)
        at = pl.ds(pl.multiple_of(index * LANES, LANES), window)
        out[:, at] = jnp.where((lane >= shift) & (lane < shift + count), turned, out[:, at])


def insert(place, rows, blocks, masks, rows_each, count):
    height, width = blocks[0].shape[1], rows_each * count
    old = [] if rows is None else hold(pltpu.VMEM, rows)
    return pl.pallas_call(
        functools.partial(insert_kernel, masks, rows_each),
        in_specs=[IN_SMEM] + [IN_VMEM] * (len(blocks) + len(old)),
        out_specs=IN_VMEM,
        out_shape=pltpu.VMEM((height, width), f32),
        input_output_aliases={1 + len(blocks): 0} if old else {},
        compiler_params=SMALL,
        cost_estimate=SLOW,
        name="insert",
    )(place, *blocks, *old)


def base_kernel(weight_q, moment_q, weight_o, moment_o, own, *parts):
    drop = step_size * decay_rate
    base = jnp.concatenate([weight_q[...] - drop * moment_q[...], weight_o[...] - drop * moment_o[...]], axis=1)
    own[...] = base
    rows = base.shape[0]
    first_part, second_part = parts
    first_part[...] = base[: first_part.shape[0]]
    second_part[...] = base[rows - second_part.shape[0] :]


def base_of(weight_q, moment_q, weight_o, moment_o):
    rows, width = weight_q.shape[0], 2 * weight_q.shape[1]
    half = rows // 2
    shapes = [(rows, width), (half, width), (rows - half, width)]
    return pl.pallas_call(
        base_kernel,
        in_specs=[IN_VMEM] * 4,
        out_specs=[IN_VMEM] * 3,
        out_shape=[pltpu.VMEM(shape, f32) for shape in shapes],
        compiler_params=SMALL,
        cost_estimate=QUICK,
        name="base",
    )(weight_q, moment_q, weight_o, moment_o)


def window_of(n_shard, share, place_ref, shard_ref, lines):
    start = (place_ref[0] * n_shard + shard_ref[0]) * share
    row = lax.broadcasted_iota(jnp.int32, (lines, LANES), 0)
    lane = lax.broadcasted_iota(jnp.int32, (lines, LANES), 1)
    flat = row * LANES + lane
    return lax.rem(start, LANES), (flat >= start) & (flat < start + share)


def norm_terms(n_shard, rows, place_ref, shard_ref, grads, moment, weight):
    lines, share = grads.shape[1] // LANES, moment.shape[1]
    shift, inside = window_of(n_shard, share, place_ref, shard_ref, lines)
    kept = weight[...] - step_size * decay_rate * moment[...]
    kept = jnp.concatenate([kept, jnp.zeros((1, LANES - share), f32)], axis=1)
    kept = pltpu.roll(jnp.broadcast_to(kept, (8, LANES)), shift, 1)[:1]
    square = jnp.concatenate([grads[:, line * LANES : (line + 1) * LANES] for line in range(lines)], axis=0)
    rest = jnp.zeros((rows - lines, LANES), f32)
    shares = jnp.where(inside, kept, 0.0) - step_size * square
    return jnp.concatenate([square, rest], axis=0), jnp.concatenate([shares, rest], axis=0)


def norm_out_kernel(n_shard, place_ref, shard_ref, ours, got, moment, new_moment, new_weight):
    lines, share = new_weight.shape[0], moment.shape[1]
    high = is_high(shard_ref, 1)
    size = ours.shape[1] - LANES
    ours, got = ours[:lines, size:], got[:lines, size:]
    sums = jnp.where(high, got, ours)
    shift, inside = window_of(n_shard, share, place_ref, shard_ref, lines)
    total = jnp.sum(jnp.where(inside, sums, 0.0), axis=0, keepdims=True)
    total = pltpu.roll(jnp.broadcast_to(total, (8, LANES)), LANES - shift, 1)[:1, :share]
    new_moment[...] = decay_rate * moment[...] + total
    new_weight[...] = jnp.where(high, ours, got)


def norm_out(ours, got, moment, place, shard, lines, n_shard):
    return pl.pallas_call(
        functools.partial(norm_out_kernel, n_shard),
        in_specs=[IN_SMEM] * 2 + [IN_VMEM] * 3,
        out_specs=[IN_VMEM] * 2,
        out_shape=[jax.ShapeDtypeStruct(moment.shape, f32), jax.ShapeDtypeStruct((lines, LANES), f32)],
        compiler_params=SMALL,
        cost_estimate=QUICK,
        name="norm_out",
    )(place, shard, ours, got, moment)


def first_kernel(n_shard, place_ref, shard_ref, *refs):
    sources, norms, (corr, give_corr, keep, give) = refs[:6], refs[6:9], refs[9:13]
    buffer, bases, norm_buffers, sems, small_sems = refs[13], refs[14], refs[15:18], refs[18], refs[19]
    rank, size = bases.shape[1], corr.shape[2]
    high = is_high(shard_ref, 1)
    small = zip(sources[4:] + norms, [bases.at[0], bases.at[1], *norm_buffers])
    small_copies = [pltpu.make_async_copy(source, target, small_sems.at[k]) for k, (source, target) in enumerate(small)]
    copies = [pltpu.make_async_copy(source, buffer.at[j], sems.at[j]) for j, source in enumerate(sources[:4])]
    for copy in small_copies + copies:
        copy.start()
    for copy in small_copies:
        copy.wait()
    sums, shares = norm_terms(n_shard, rank, place_ref, shard_ref, *norm_buffers)
    keep[:, size:] = jnp.where(high, shares, sums)
    give[:, size:] = jnp.where(high, sums, shares)
    totals, parts = [], []
    for p in range(2):
        copies[p].wait()
        copies[2 + p].wait()
        totals.append(buffer[p] + buffer[2 + p])
        corr[p] = totals[p]
        parts.append(stacked(bases[p], totals[p], NN))
    give_corr[...] = jnp.where(high, totals[0], totals[1])
    keep[:, :size] = jnp.where(high, parts[1], parts[0])
    give[:, :size] = jnp.where(high, parts[0], parts[1])


def first(grads, errors, bases, norms, place, shard, n_shard):
    width, size = grads[0].shape
    rank = bases[0].shape[0]
    part = pltpu.VMEM((rank, size + LANES), f32)
    return pl.pallas_call(
        functools.partial(first_kernel, n_shard),
        in_specs=[IN_SMEM] * 2 + [IN_HBM] * 9,
        out_specs=[IN_VMEM] * 4,
        out_shape=[pltpu.VMEM((2, width, size), f32), pltpu.VMEM((width, size), f32), part, part],
        scratch_shapes=[
            pltpu.VMEM((4, width, size), f32),
            pltpu.VMEM((2, rank, width), f32),
            *(pltpu.VMEM(array.shape, f32) for array in norms),
            pltpu.SemaphoreType.DMA((4,)),
            pltpu.SemaphoreType.DMA((5,)),
        ],
        compiler_params=LARGE,
        name="first",
    )(place, shard, *hold(pltpu.HBM, *grads, *errors, *bases, *norms))


def both_shares(shard_ref, corr, other):
    return jnp.concatenate([corr[shard_ref[0] & 1], other[...]], axis=0)


def right_kernel(count, waits, shard_ref, whole, corr, other, *refs):
    size = corr.shape[2]
    right, left, *extra = refs[count + waits :]
    left[:, :size] = whole[:, :size]
    if count:
        left[:, size:] = refs[0][...]
    if extra:
        extra[0][...] = whole[:, size:]
    right[...] = stacked(whole[:, :size], both_shares(shard_ref, corr, other), NT)


def right_of(whole, shard, corr, other, more, waits):
    rank = whole.shape[0]
    width, size = other.shape
    beside = whole.shape[1] - size
    shapes = [(rank, 2 * width), (rank, size + sum(array.shape[1] for array in more))] + ([(rank, beside)] if beside else [])
    return pl.pallas_call(
        functools.partial(right_kernel, len(more), len(waits)),
        in_specs=[IN_SMEM] + [IN_VMEM] * (3 + len(more) + len(waits)),
        out_specs=[IN_VMEM] * len(shapes),
        out_shape=[pltpu.VMEM(shape, f32) for shape in shapes],
        compiler_params=SMALL,
        cost_estimate=QUICK,
        name="right",
    )(shard, whole, *hold(pltpu.VMEM, corr, other), *more, *waits)


def left_kernel(mask, shard_ref, right, inverse, corr, other, *refs):
    keep, give = refs[-2:]
    basis = exact(inverse[0], right[...], NN)
    part = stacked(basis, both_shares(shard_ref, corr, other), NN)
    half = part.shape[0] // 2
    high = is_high(shard_ref, mask)
    keep[...] = jnp.where(high, part[half:], part[:half])
    give[...] = jnp.where(high, part[:half], part[half:])


def left_of(right, inverse, shard, mask, corr, other, waits):
    half = pltpu.VMEM((right.shape[0] // 2, other.shape[1]), f32)
    return pl.pallas_call(
        functools.partial(left_kernel, mask),
        in_specs=[IN_SMEM] + [IN_VMEM] * (4 + len(waits)),
        out_specs=[IN_VMEM] * 2,
        out_shape=[half, half],
        compiler_params=SMALL,
        cost_estimate=QUICK,
        name="left",
    )(shard, right, inverse, *hold(pltpu.VMEM, corr, other), *waits)


def eliminate(gram_q, gram_o, rank):
    width = 4 * rank
    lane = lax.broadcasted_iota(jnp.int32, (rank, width), 1)
    row = lax.broadcasted_iota(jnp.int32, (rank, width), 0)
    square = (rank, rank)
    eye = (lax.broadcasted_iota(jnp.int32, square, 0) == lax.broadcasted_iota(jnp.int32, square, 1)).astype(f32)
    work = jnp.concatenate([gram_q, eye, gram_o, eye], axis=1)
    first_half = lane < 2 * rank
    scale = jnp.ones((rank, width), f32)
    for base in range(0, rank, GROUP):
        columns = []
        for k in range(base, base + GROUP):
            of_q = jnp.broadcast_to(work[:, k : k + 1], (rank, width))
            of_o = jnp.broadcast_to(work[:, 2 * rank + k : 2 * rank + k + 1], (rank, width))
            columns.append(jnp.where(first_half, of_q, of_o))
        for j in range(GROUP):
            k = base + j
            pivot = columns[j][k : k + 1]
            factor = jnp.where(row > k, columns[j] * (1.0 / pivot), 0.0)
            scale = jnp.where(row == k, pivot, scale)
            for i in range(j + 1, GROUP):
                columns[i] = columns[i] - factor * columns[i][k : k + 1]
            work = work - factor * work[k : k + 1]
    work = work * lax.rsqrt(scale)
    return work[:, rank : 2 * rank], work[:, 3 * rank :]


def inverse_kernel(size, ours, theirs, out):
    rank = out.shape[1]
    left, other = ours[:, :size], theirs[:, :size]
    out[0], out[1] = eliminate(exact(left, left, NT), exact(other, other, NT), rank)


def inverse_of(ours, theirs, size):
    rank = ours.shape[0]
    return pl.pallas_call(
        functools.partial(inverse_kernel, size),
        out_shape=pltpu.VMEM((2, rank, rank), f32),
        compiler_params=SMALL,
        cost_estimate=SLOW,
        name="inverse",
    )(ours, theirs)


def stack_kernel(place_ref, ours, theirs, stack, own):
    count = own.shape[2]
    index = place_ref[0]
    for p, left in enumerate((ours, theirs)):
        high, middle, low = three(left[:, : stack.shape[2]])
        stack[p] = jnp.concatenate([high, middle, low, high, middle, high], axis=0)
        window = left[:, pl.ds(pl.multiple_of(index * LANES, LANES), 2 * LANES)]
        own[p] = pltpu.roll(window, 2 * LANES - index * (count - LANES), 1)[:, :count]


def stack_of(ours, theirs, place, size, count):
    rank = ours.shape[0]
    return pl.pallas_call(
        stack_kernel,
        in_specs=[IN_SMEM, IN_VMEM, IN_VMEM],
        out_specs=[IN_VMEM] * 2,
        out_shape=[pltpu.VMEM((2, 6 * rank, size), bf16), pltpu.VMEM((2, rank, count), f32)],
        compiler_params=SMALL,
        cost_estimate=SLOW,
        name="stack",
    )(place, ours, theirs)


def finish_kernel(chunks, shard_ref, corr, rows, stack, inverse, right, their_right, own, moment_q, moment_o, *refs):
    outs, (buffer, new_moments, sems) = refs[:6], refs[6:]
    width = moment_q.shape[1]
    height = width // chunks
    copies = []

    def send(index, source, to_q, to_o, sem):
        for p, target in enumerate((to_q, to_o)):

            @pl.when(index == p)
            def _(target=target):
                pltpu.make_async_copy(source, target, sem).start()

        copies.append(pltpu.make_async_copy(source, to_q, sem))

    for theirs, factor in enumerate((right, their_right)):
        index = (shard_ref[0] & 1) ^ theirs
        factor = factor[:, width * theirs : width * (theirs + 1)]
        scaled = exact(inverse[theirs], exact(inverse[theirs], factor, NN), TN)
        high, middle, low = three(scaled.T)
        lefts = jnp.concatenate([high, high, high, middle, middle, low], axis=1)
        for c in range(chunks):
            at = pl.ds(c * height, height)
            decoded = lax.dot_general(lefts[c * height : (c + 1) * height], stack[theirs], NN, preferred_element_type=f32)
            buffer[theirs, 0, at, :] = rows[pl.ds(pl.multiple_of(index * width + c * height, 8), height), :] - step_size * decoded
            buffer[theirs, 1, at, :] = corr[index, at, :] - decoded
            for k in range(2):
                send(index, buffer.at[theirs, k, at, :], outs[2 * k].at[at, :], outs[2 * k + 1].at[at, :], sems.at[theirs, k, c])
        moment = jnp.where(index == 0, moment_q[...], moment_o[...])
        new_moments[theirs] = decay_rate * moment + exact(own[theirs], scaled, TN)
        send(index, new_moments.at[theirs], outs[4], outs[5], sems.at[theirs, 2, 0])
    for copy in copies:
        copy.wait()


def finish(shard, corr, rows, stack, inverse, right, their_right, own, moment_q, moment_o):
    width, size = corr.shape[1:]
    chunks = 3
    return pl.pallas_call(
        functools.partial(finish_kernel, chunks),
        in_specs=[IN_SMEM] + [IN_VMEM] * 9,
        out_specs=[IN_HBM] * 6,
        out_shape=[pltpu.HBM((width, size), f32)] * 4 + [pltpu.HBM(moment_q.shape, f32)] * 2,
        scratch_shapes=[
            pltpu.VMEM((2, 2, width, size), f32),
            pltpu.VMEM((2,) + moment_q.shape, f32),
            pltpu.SemaphoreType.DMA((2, 3, chunks)),
        ],
        compiler_params=LARGE,
        name="finish",
    )(shard, *hold(pltpu.VMEM, corr, rows), stack, inverse, right, their_right, own, moment_q, moment_o)


def finish_plain(high, corr, base, lefts, inverse, rights, moments):
    rows, width = moments[0].shape
    start = lax.axis_index("rep") * rows
    bases = lax.all_gather(base, "rep", axis=0, tiled=True)
    decodeds = []
    for p in range(2):
        factor = rights[p][:, p * width : (p + 1) * width]
        scaled = exact(inverse[p], exact(inverse[p], factor, NN), TN)
        decodeds.append(exact(scaled, lefts[p], TN))
    ours, theirs = decodeds
    weights, new_moments, errors = [], [], []
    for p, decoded in enumerate((jnp.where(high, theirs, ours), jnp.where(high, ours, theirs))):
        weights.append(bases[:, p * width : (p + 1) * width].T - step_size * decoded)
        new_moments.append(decay_rate * moments[p] + lax.dynamic_slice_in_dim(decoded, start, rows, 1).T)
        errors.append(corr[p] - decoded)
    return weights + errors + new_moments


def per_device(n_rep, n_shard, q_grad, o_grad, q_error, o_error, q_basis, o_basis, q_moment, o_moment, q_weight, o_weight, norm_grads, norm_moment, norm_weight):
    rank = q_basis.shape[1]
    size = q_grad.shape[1]
    flat = norm_grads.shape[-1]
    row_count = q_moment.shape[0]
    place = lax.axis_index("rep").astype(jnp.int32).reshape(1)
    shard = lax.axis_index("shard").astype(jnp.int32).reshape(1)

    gather = Gather(*base_of(q_weight, q_moment, o_weight, o_moment), place, n_rep, n_shard)
    norm_moment, norm_weight = norm_moment.reshape(1, -1), norm_weight.reshape(1, -1)
    norms = (norm_grads[0], norm_moment, norm_weight)
    corr, give_corr, keep, give = first((q_grad[0].T, o_grad[0].T), (q_error[0].T, o_error[0].T), (q_basis.T, o_basis.T), norms, place, shard, n_shard)
    masks = halves(n_shard)

    def ending(left, theirs):
        gains = norm_out(left, theirs, norm_moment, place, shard, flat // LANES, n_shard)
        return (gains, *stack_of(left, theirs, place, size, row_count)) if gather.paired else (gains,)

    for sweep in range(ROUNDS):
        last = sweep == ROUNDS - 1
        if sweep == 0:
            whole, other_corr = sum_over_all(keep, give, shard, masks, n_rep, n_shard, gather, 0, give_corr)
        else:
            whole, _ = sum_over_all(keep, give, shard, masks[1:], n_rep, n_shard, gather, 2 * sweep)
        right, left, *beside = right_of(whole, shard, corr, other_corr, [norms] if last else [], gather.met(2 * sweep))
        if sweep == 0:
            (norms,) = beside
        theirs = swap(left, "shard", masks[0], n_shard)
        gather.tasks[2 * sweep + 1, 4 if last else 2] = (functools.partial(inverse_of, size=size), left, theirs)
        if last:
            gather.tasks[3, 2] = (ending, left, theirs)
        if 2 * sweep + 1 in MEETINGS:
            gather.meet(2 * sweep + 1, keep)
        right = sum_over(right, n_rep, gather, 2 * sweep + 1)
        inverse = gather.results[2 * sweep + 1, 4 if last else 2]
        if not last:
            keep, give = left_of(right, inverse, shard, masks[1], corr, other_corr, gather.met(1))
    their_right = swap(right, "shard", masks[0], n_shard)
    (norm_moment_new, norm_weight_new), *terms = gather.results[3, 2]
    if gather.paired:
        stack, own = terms
        their_right, turned = lax.optimization_barrier((their_right, gather.blocks["turned_last_b"]))
        gather.insert([turned], ["turned_last_b"])
        outs = finish(shard, corr, gather.rows, stack, inverse, right, their_right, own, q_moment, o_moment)
    else:
        outs = finish_plain((shard[0] & 1) != 0, corr, gather.blocks["own"], (left[:, :size], theirs[:, :size]), inverse, (right, their_right), (q_moment, o_moment))
    weight_q, weight_o, error_q, error_o, q_moment_new, o_moment_new = outs
    return (
        weight_q.T,
        weight_o.T,
        q_moment_new,
        o_moment_new,
        error_q.T[None],
        error_o.T[None],
        norm_weight_new.reshape(flat),
        norm_moment_new.reshape(-1),
    )


def solution(mesh):
    n_rep, n_shard = mesh.shape["rep"], mesh.shape["shard"]

    def whole(*arrays):
        return per_device(n_rep, n_shard, *arrays)

    return jax.shard_map(
        whole,
        mesh=mesh,
        in_specs=(
            P("rep", None, "shard"),
            P("rep", None, "shard"),
            P("rep", None, "shard"),
            P("rep", None, "shard"),
            P("shard", None),
            P("shard", None),
            P("rep", "shard"),
            P("rep", "shard"),
            P("rep", "shard"),
            P("rep", "shard"),
            P("rep", "shard", None),
            P(("rep", "shard")),
            P(("rep", "shard")),
        ),
        out_specs=(
            P(None, "shard"),
            P(None, "shard"),
            P("rep", "shard"),
            P("rep", "shard"),
            P("rep", None, "shard"),
            P("rep", None, "shard"),
            P(),
            P(("rep", "shard")),
        ),
        check_vma=False,
    )
```

```python
import functools

import jax
import jax.numpy as jnp
from jax import lax
from jax.experimental import pallas as pl
from jax.experimental.pallas import tpu as pltpu
from jax.sharding import PartitionSpec as P

ROUNDS = 2
GROUP = 8
LANES = 128
MEETINGS = (1, 2)

highest = lax.Precision.HIGHEST
decay_rate = 0.9
step_size = 0.1
f32 = jnp.float32
bf16 = jnp.bfloat16
NN = (((1,), (0,)), ((), ()))
NT = (((1,), (1,)), ((), ()))
TN = (((0,), (0,)), ((), ()))

IN_HBM = pl.BlockSpec(memory_space=pltpu.HBM)
IN_VMEM = pl.BlockSpec(memory_space=pltpu.VMEM)
IN_SMEM = pl.BlockSpec(memory_space=pltpu.SMEM)
SMALL = pltpu.CompilerParams(vmem_limit_bytes=6 * 2**20)
LARGE = pltpu.CompilerParams(vmem_limit_bytes=12 * 2**20)
QUICK = pl.CostEstimate(flops=1000, bytes_accessed=1000, transcendentals=0)
SLOW = pl.CostEstimate(flops=1000, bytes_accessed=6_000_000, transcendentals=0)


def hold(space, *arrays):
    return [pltpu.with_memory_space_constraint(array, space) for array in arrays]


def exact(left, right, dims):
    return lax.dot_general(left, right, dims, precision=highest, preferred_element_type=f32)


def three(x):
    high = x.astype(bf16)
    rest = x - high.astype(f32)
    middle = rest.astype(bf16)
    low = (rest - middle.astype(f32)).astype(bf16)
    return high, middle, low


def stacked(left, right, dims):
    rows = left.shape[0]
    left_high, left_middle, left_low = three(left)
    right_high, right_middle, right_low = three(right)
    lefts = jnp.concatenate([left_high, left_middle, left_low], axis=0)
    of_high = lax.dot_general(lefts, right_high, dims, preferred_element_type=f32)
    of_middle = lax.dot_general(lefts[: 2 * rows], right_middle, dims, preferred_element_type=f32)
    of_low = lax.dot_general(left_high, right_low, dims, preferred_element_type=f32)
    small = (of_high[2 * rows :] + of_middle[rows:]) + of_low
    return of_high[:rows] + ((of_high[rows : 2 * rows] + of_middle[:rows]) + small)


def halves(count):
    masks = []
    mask = 1
    while mask < count:
        masks.append(mask)
        mask *= 2
    return masks


def swap(block, axis, mask, count):
    pairs = [(i, i ^ mask) for i in range(count)]
    return lax.ppermute(block, axis, pairs)


def sum_over(block, count, gather, stage):
    for mask in halves(count):
        block = gather.before(block, stage, mask)
        block = gather.start_tasks(block, stage, mask)
        block = block + gather.end_tasks(swap(block, "rep", mask, count), stage, mask)
        block = gather.after(block, stage, mask)
    return gather.after(gather.before(block, stage, 0), stage, 0)


def sum_over_all(keep, give, shard, masks, n_rep, n_shard, gather, stage, along=None):
    keep = gather.after(keep, stage, "begin")
    partner = None
    for mask, after in zip(masks, masks[1:] + [None]):
        got = swap(give, "shard", mask, n_shard)
        if after is not None:
            keep, give = split(keep, got, shard, after)
            if along is not None and partner is None:
                give, along = lax.optimization_barrier((give, along))
                partner = swap(along, "shard", mask, n_shard)
            keep = gather.after(gather.before(keep, stage, "core"), stage, "core")
    if stage in MEETINGS:
        gather.meet(stage, keep)
    part = sum_over(keep + got, n_rep, gather, stage)
    for mask in reversed(halves(n_shard)[1:]):
        part = gather.start_tasks(part, stage, "x")
        got = gather.end_tasks(swap(part, "shard", mask, n_shard), stage, "x")
        part = gather.before(join(part, got, shard, mask), stage, "joined")
    return part, partner


def is_high(place_ref, mask):
    return (place_ref[0] & mask) != 0


def split_kernel(mask, shard_ref, ours, got, keep, give):
    total = ours[...] + got[...]
    half = total.shape[0] // 2
    high = is_high(shard_ref, mask)
    keep[...] = jnp.where(high, total[half:], total[:half])
    give[...] = jnp.where(high, total[:half], total[half:])


def split(ours, got, shard, mask):
    half = pltpu.VMEM((ours.shape[0] // 2, ours.shape[1]), f32)
    return pl.pallas_call(
        functools.partial(split_kernel, mask),
        in_specs=[IN_SMEM, IN_VMEM, IN_VMEM],
        out_specs=[IN_VMEM] * 2,
        out_shape=[half, half],
        compiler_params=SMALL,
        cost_estimate=QUICK,
        name="split",
    )(shard, ours, got)


def joined(shard_ref, mask, ours, got):
    high = is_high(shard_ref, mask)
    return jnp.concatenate([jnp.where(high, got, ours), jnp.where(high, ours, got)], axis=0)


def join_kernel(mask, shard_ref, ours, got, whole):
    whole[...] = joined(shard_ref, mask, ours[...], got[...])


def join(ours, got, shard, mask):
    return pl.pallas_call(
        functools.partial(join_kernel, mask),
        in_specs=[IN_SMEM, IN_VMEM, IN_VMEM],
        out_specs=IN_VMEM,
        out_shape=pltpu.VMEM((2 * ours.shape[0], ours.shape[1]), f32),
        compiler_params=SMALL,
        cost_estimate=QUICK,
        name="join",
    )(shard, ours, got)


class Gather:
    PLAN = (
        ("near", "own", 2, (0, "core"), (0, "joined")),
        ("turned", "own", 1, (0, 1), (1, 4)),
        ("far_a", "own_a", 4, (0, 4), (1, 2)),
        ("turned_near", "near", 1, (1, 1), (2, 4)),
        ("last_a", "far_a", 2, (1, 2), (2, 2)),
        ("turned_far_a", "far_a", 1, (1, 2), (2, 2)),
        ("far_b", "own_b", 4, (2, "begin"), (2, 4)),
        ("turned_last_a", "last_a", 1, (2, 1), (2, "joined")),
        ("last_b", "far_b", 2, (2, 2), (3, 2)),
        ("turned_far_b", "far_b", 1, (2, 2), (3, 2)),
        ("turned_last_b", "last_b", 1, (3, 1), None),
    )
    INSERTS = {
        (1, 1): ("own",),
        (2, 1): ("near", "turned"),
        (2, 2): ("far_a", "last_a"),
        (2, 4): ("turned_near",),
        (2, "x"): ("turned_far_a",),
        (3, 1): ("far_b",),
        (3, 4): ("turned_far_b", "last_b", "turned_last_a"),
    }
    PLACES = {"own": 0, "turned": 1, "near": 2, "far": 4, "last": 6, "turned_near": 3, "turned_far": 5, "turned_last": 7}

    def place_of(self, name):
        whole = name.removesuffix("_a").removesuffix("_b")
        skipped = self.blocks["own"].shape[0] - self.blocks[name].shape[0]
        return self.PLACES[whole], skipped if name.endswith("_b") else 0

    def __init__(self, own, own_a, own_b, place, count, n_shard):
        self.count = count
        self.n_shard = n_shard
        self.place = place
        self.blocks = {"own": own, "own_a": own_a, "own_b": own_b}
        self.paired = count == 8 and own.shape[0] % 16 == 0
        self.rows = None
        self.tasks = {}
        self.results = {}
        self.send(None)

    def send(self, point):
        if self.paired:
            for name, source, mask, after, _ in self.PLAN:
                if after == point:
                    self.blocks[name] = swap(self.blocks[source], "rep", mask, self.count)

    def meet(self, stage, array):
        self.tasks[stage, 4] = (functools.partial(swap, axis="shard", mask=1, count=self.n_shard), array)

    def met(self, stage):
        return [self.results[stage, 4]] if stage in MEETINGS else []

    def start_tasks(self, value, stage, mask):
        point = (stage, mask)
        if point in self.tasks:
            task, *inputs = self.tasks[point]
            value, *inputs = lax.optimization_barrier((value, *inputs))
            self.results[point] = task(*inputs)
        if self.paired and point in self.INSERTS:
            value, *blocks = lax.optimization_barrier((value, *(self.blocks[name] for name in self.INSERTS[point])))
            self.insert(blocks, self.INSERTS[point])
        if self.paired:
            for name, source, _, after, _ in self.PLAN:
                if after == ("beside",) + point:
                    if point in self.INSERTS:
                        self.rows, self.blocks[source] = lax.optimization_barrier((self.rows, self.blocks[source]))
                    else:
                        self.results[point], self.blocks[source] = lax.optimization_barrier((self.results[point], self.blocks[source]))
            self.send(("beside",) + point)
        return value

    def end_tasks(self, value, stage, mask):
        point = (stage, mask)
        if point in self.tasks:
            value, self.results[point] = lax.optimization_barrier((value, self.results[point]))
        if self.paired and point in self.INSERTS:
            value, self.rows = lax.optimization_barrier((value, self.rows))
        return value

    def insert(self, blocks, names):
        self.rows = insert(self.place, self.rows, blocks, [self.place_of(name) for name in names], self.blocks["own"].shape[0], self.count)

    def before(self, value, stage, mask):
        if self.paired:
            for name, _, _, _, by in self.PLAN:
                if by == (stage, mask):
                    value, self.blocks[name] = lax.optimization_barrier((value, self.blocks[name]))
        return value

    def after(self, value, stage, mask):
        if self.paired:
            for name, source, _, after, _ in self.PLAN:
                if after == (stage, mask) and source in self.blocks:
                    value, self.blocks[source] = lax.optimization_barrier((value, self.blocks[source]))
            self.send((stage, mask))
        return value


def insert_kernel(masks, rows_each, place_ref, *refs):
    blocks, rows, out = refs[: len(masks)], refs[len(masks) : -1], refs[-1]
    if not rows:
        out[...] = jnp.zeros_like(out)
    height = out.shape[0]
    window = 2 * LANES
    lane = lax.broadcasted_iota(jnp.int32, (height, window), 1)
    for block, (mask, skipped) in zip(blocks, masks):
        count = block.shape[0]
        index = place_ref[0] ^ mask
        shift = index * (rows_each - LANES) + skipped
        turned = jnp.concatenate([block[...].T, jnp.zeros((height, window - count), f32)], axis=1)
        turned = pltpu.roll(turned, shift, 1)
        at = pl.ds(pl.multiple_of(index * LANES, LANES), window)
        out[:, at] = jnp.where((lane >= shift) & (lane < shift + count), turned, out[:, at])


def insert(place, rows, blocks, masks, rows_each, count):
    height, width = blocks[0].shape[1], rows_each * count
    old = [] if rows is None else hold(pltpu.VMEM, rows)
    return pl.pallas_call(
        functools.partial(insert_kernel, masks, rows_each),
        in_specs=[IN_SMEM] + [IN_VMEM] * (len(blocks) + len(old)),
        out_specs=IN_VMEM,
        out_shape=pltpu.VMEM((height, width), f32),
        input_output_aliases={1 + len(blocks): 0} if old else {},
        compiler_params=SMALL,
        cost_estimate=SLOW,
        name="insert",
    )(place, *blocks, *old)


def base_kernel(weight_q, moment_q, weight_o, moment_o, own, *parts):
    drop = step_size * decay_rate
    base = jnp.concatenate([weight_q[...] - drop * moment_q[...], weight_o[...] - drop * moment_o[...]], axis=1)
    own[...] = base
    rows = base.shape[0]
    first_part, second_part = parts
    first_part[...] = base[: first_part.shape[0]]
    second_part[...] = base[rows - second_part.shape[0] :]


def base_of(weight_q, moment_q, weight_o, moment_o):
    rows, width = weight_q.shape[0], 2 * weight_q.shape[1]
    half = rows // 2
    shapes = [(rows, width), (half, width), (rows - half, width)]
    return pl.pallas_call(
        base_kernel,
        in_specs=[IN_VMEM] * 4,
        out_specs=[IN_VMEM] * 3,
        out_shape=[pltpu.VMEM(shape, f32) for shape in shapes],
        compiler_params=SMALL,
        cost_estimate=QUICK,
        name="base",
    )(weight_q, moment_q, weight_o, moment_o)


def window_of(n_shard, share, place_ref, shard_ref, lines):
    start = (place_ref[0] * n_shard + shard_ref[0]) * share
    row = lax.broadcasted_iota(jnp.int32, (lines, LANES), 0)
    lane = lax.broadcasted_iota(jnp.int32, (lines, LANES), 1)
    flat = row * LANES + lane
    return lax.rem(start, LANES), (flat >= start) & (flat < start + share)


def norm_terms(n_shard, rows, place_ref, shard_ref, grads, moment, weight):
    lines, share = grads.shape[1] // LANES, moment.shape[1]
    shift, inside = window_of(n_shard, share, place_ref, shard_ref, lines)
    kept = weight[...] - step_size * decay_rate * moment[...]
    kept = jnp.concatenate([kept, jnp.zeros((1, LANES - share), f32)], axis=1)
    kept = pltpu.roll(jnp.broadcast_to(kept, (8, LANES)), shift, 1)[:1]
    square = jnp.concatenate([grads[:, line * LANES : (line + 1) * LANES] for line in range(lines)], axis=0)
    rest = jnp.zeros((rows - lines, LANES), f32)
    shares = jnp.where(inside, kept, 0.0) - step_size * square
    return jnp.concatenate([square, rest], axis=0), jnp.concatenate([shares, rest], axis=0)


def norm_out_kernel(n_shard, place_ref, shard_ref, ours, got, moment, new_moment, new_weight):
    lines, share = new_weight.shape[0], moment.shape[1]
    high = is_high(shard_ref, 1)
    size = ours.shape[1] - LANES
    ours, got = ours[:lines, size:], got[:lines, size:]
    sums = jnp.where(high, got, ours)
    shift, inside = window_of(n_shard, share, place_ref, shard_ref, lines)
    total = jnp.sum(jnp.where(inside, sums, 0.0), axis=0, keepdims=True)
    total = pltpu.roll(jnp.broadcast_to(total, (8, LANES)), LANES - shift, 1)[:1, :share]
    new_moment[...] = decay_rate * moment[...] + total
    new_weight[...] = jnp.where(high, ours, got)


def norm_out(ours, got, moment, place, shard, lines, n_shard):
    return pl.pallas_call(
        functools.partial(norm_out_kernel, n_shard),
        in_specs=[IN_SMEM] * 2 + [IN_VMEM] * 3,
        out_specs=[IN_VMEM] * 2,
        out_shape=[jax.ShapeDtypeStruct(moment.shape, f32), jax.ShapeDtypeStruct((lines, LANES), f32)],
        compiler_params=SMALL,
        cost_estimate=QUICK,
        name="norm_out",
    )(place, shard, ours, got, moment)


def first_kernel(n_shard, place_ref, shard_ref, *refs):
    sources, norms, (corr, give_corr, keep, give) = refs[:6], refs[6:9], refs[9:13]
    buffer, bases, norm_buffers, sems, small_sems = refs[13], refs[14], refs[15:18], refs[18], refs[19]
    rank, size = bases.shape[1], corr.shape[2]
    high = is_high(shard_ref, 1)
    small = zip(sources[4:] + norms, [bases.at[0], bases.at[1], *norm_buffers])
    small_copies = [pltpu.make_async_copy(source, target, small_sems.at[k]) for k, (source, target) in enumerate(small)]
    copies = [pltpu.make_async_copy(source, buffer.at[j], sems.at[j]) for j, source in enumerate(sources[:4])]
    for copy in small_copies + copies:
        copy.start()
    for copy in small_copies:
        copy.wait()
    sums, shares = norm_terms(n_shard, rank, place_ref, shard_ref, *norm_buffers)
    keep[:, size:] = jnp.where(high, shares, sums)
    give[:, size:] = jnp.where(high, sums, shares)
    totals, parts = [], []
    for p in range(2):
        copies[p].wait()
        copies[2 + p].wait()
        totals.append(buffer[p] + buffer[2 + p])
        corr[p] = totals[p]
        parts.append(stacked(bases[p], totals[p], NN))
    give_corr[...] = jnp.where(high, totals[0], totals[1])
    keep[:, :size] = jnp.where(high, parts[1], parts[0])
    give[:, :size] = jnp.where(high, parts[0], parts[1])


def first(grads, errors, bases, norms, place, shard, n_shard):
    width, size = grads[0].shape
    rank = bases[0].shape[0]
    part = pltpu.VMEM((rank, size + LANES), f32)
    return pl.pallas_call(
        functools.partial(first_kernel, n_shard),
        in_specs=[IN_SMEM] * 2 + [IN_HBM] * 9,
        out_specs=[IN_VMEM] * 4,
        out_shape=[pltpu.VMEM((2, width, size), f32), pltpu.VMEM((width, size), f32), part, part],
        scratch_shapes=[
            pltpu.VMEM((4, width, size), f32),
            pltpu.VMEM((2, rank, width), f32),
            *(pltpu.VMEM(array.shape, f32) for array in norms),
            pltpu.SemaphoreType.DMA((4,)),
            pltpu.SemaphoreType.DMA((5,)),
        ],
        compiler_params=LARGE,
        name="first",
    )(place, shard, *hold(pltpu.HBM, *grads, *errors, *bases, *norms))


def both_shares(shard_ref, corr, other):
    return jnp.concatenate([corr[shard_ref[0] & 1], other[...]], axis=0)


def right_kernel(count, waits, shard_ref, whole, corr, other, *refs):
    size = corr.shape[2]
    right, left, *extra = refs[count + waits :]
    left[:, :size] = whole[:, :size]
    if count:
        left[:, size:] = refs[0][...]
    if extra:
        extra[0][...] = whole[:, size:]
    right[...] = stacked(whole[:, :size], both_shares(shard_ref, corr, other), NT)


def right_of(whole, shard, corr, other, more, waits):
    rank = whole.shape[0]
    width, size = other.shape
    beside = whole.shape[1] - size
    shapes = [(rank, 2 * width), (rank, size + sum(array.shape[1] for array in more))] + ([(rank, beside)] if beside else [])
    return pl.pallas_call(
        functools.partial(right_kernel, len(more), len(waits)),
        in_specs=[IN_SMEM] + [IN_VMEM] * (3 + len(more) + len(waits)),
        out_specs=[IN_VMEM] * len(shapes),
        out_shape=[pltpu.VMEM(shape, f32) for shape in shapes],
        compiler_params=SMALL,
        cost_estimate=QUICK,
        name="right",
    )(shard, whole, *hold(pltpu.VMEM, corr, other), *more, *waits)


def left_kernel(mask, shard_ref, right, inverse, corr, other, *refs):
    keep, give = refs[-2:]
    basis = exact(inverse[0], right[...], NN)
    part = stacked(basis, both_shares(shard_ref, corr, other), NN)
    half = part.shape[0] // 2
    high = is_high(shard_ref, mask)
    keep[...] = jnp.where(high, part[half:], part[:half])
    give[...] = jnp.where(high, part[:half], part[half:])


def left_of(right, inverse, shard, mask, corr, other, waits):
    half = pltpu.VMEM((right.shape[0] // 2, other.shape[1]), f32)
    return pl.pallas_call(
        functools.partial(left_kernel, mask),
        in_specs=[IN_SMEM] + [IN_VMEM] * (4 + len(waits)),
        out_specs=[IN_VMEM] * 2,
        out_shape=[half, half],
        compiler_params=SMALL,
        cost_estimate=QUICK,
        name="left",
    )(shard, right, inverse, *hold(pltpu.VMEM, corr, other), *waits)


def eliminate(gram_q, gram_o, rank):
    width = 4 * rank
    lane = lax.broadcasted_iota(jnp.int32, (rank, width), 1)
    row = lax.broadcasted_iota(jnp.int32, (rank, width), 0)
    square = (rank, rank)
    eye = (lax.broadcasted_iota(jnp.int32, square, 0) == lax.broadcasted_iota(jnp.int32, square, 1)).astype(f32)
    work = jnp.concatenate([gram_q, eye, gram_o, eye], axis=1)
    first_half = lane < 2 * rank
    scale = jnp.ones((rank, width), f32)
    for base in range(0, rank, GROUP):
        columns = []
        for k in range(base, base + GROUP):
            of_q = jnp.broadcast_to(work[:, k : k + 1], (rank, width))
            of_o = jnp.broadcast_to(work[:, 2 * rank + k : 2 * rank + k + 1], (rank, width))
            columns.append(jnp.where(first_half, of_q, of_o))
        for j in range(GROUP):
            k = base + j
            pivot = columns[j][k : k + 1]
            factor = jnp.where(row > k, columns[j] * (1.0 / pivot), 0.0)
            scale = jnp.where(row == k, pivot, scale)
            for i in range(j + 1, GROUP):
                columns[i] = columns[i] - factor * columns[i][k : k + 1]
            work = work - factor * work[k : k + 1]
    work = work * lax.rsqrt(scale)
    return work[:, rank : 2 * rank], work[:, 3 * rank :]


def inverse_kernel(size, ours, theirs, out):
    rank = out.shape[1]
    left, other = ours[:, :size], theirs[:, :size]
    out[0], out[1] = eliminate(exact(left, left, NT), exact(other, other, NT), rank)


def inverse_of(ours, theirs, size):
    rank = ours.shape[0]
    return pl.pallas_call(
        functools.partial(inverse_kernel, size),
        out_shape=pltpu.VMEM((2, rank, rank), f32),
        compiler_params=SMALL,
        cost_estimate=SLOW,
        name="inverse",
    )(ours, theirs)


def stack_kernel(place_ref, ours, theirs, stack, own):
    count = own.shape[2]
    index = place_ref[0]
    for p, left in enumerate((ours, theirs)):
        high, middle, low = three(left[:, : stack.shape[2]])
        stack[p] = jnp.concatenate([high, middle, low, high, middle, high], axis=0)
        window = left[:, pl.ds(pl.multiple_of(index * LANES, LANES), 2 * LANES)]
        own[p] = pltpu.roll(window, 2 * LANES - index * (count - LANES), 1)[:, :count]


def stack_of(ours, theirs, place, size, count):
    rank = ours.shape[0]
    return pl.pallas_call(
        stack_kernel,
        in_specs=[IN_SMEM, IN_VMEM, IN_VMEM],
        out_specs=[IN_VMEM] * 2,
        out_shape=[pltpu.VMEM((2, 6 * rank, size), bf16), pltpu.VMEM((2, rank, count), f32)],
        compiler_params=SMALL,
        cost_estimate=SLOW,
        name="stack",
    )(place, ours, theirs)


def finish_kernel(chunks, shard_ref, corr, rows, stack, inverse, right, their_right, own, moment_q, moment_o, *refs):
    outs, (buffer, new_moments, sems) = refs[:6], refs[6:]
    width = moment_q.shape[1]
    height = width // chunks
    copies = []

    def send(index, source, to_q, to_o, sem):
        for p, target in enumerate((to_q, to_o)):

            @pl.when(index == p)
            def _(target=target):
                pltpu.make_async_copy(source, target, sem).start()

        copies.append(pltpu.make_async_copy(source, to_q, sem))

    for theirs, factor in enumerate((right, their_right)):
        index = (shard_ref[0] & 1) ^ theirs
        factor = factor[:, width * theirs : width * (theirs + 1)]
        scaled = exact(inverse[theirs], exact(inverse[theirs], factor, NN), TN)
        high, middle, low = three(scaled.T)
        lefts = jnp.concatenate([high, high, high, middle, middle, low], axis=1)
        for c in range(chunks):
            at = pl.ds(c * height, height)
            decoded = lax.dot_general(lefts[c * height : (c + 1) * height], stack[theirs], NN, preferred_element_type=f32)
            buffer[theirs, 0, at, :] = rows[pl.ds(pl.multiple_of(index * width + c * height, 8), height), :] - step_size * decoded
            buffer[theirs, 1, at, :] = corr[index, at, :] - decoded
            for k in range(2):
                send(index, buffer.at[theirs, k, at, :], outs[2 * k].at[at, :], outs[2 * k + 1].at[at, :], sems.at[theirs, k, c])
        moment = jnp.where(index == 0, moment_q[...], moment_o[...])
        new_moments[theirs] = decay_rate * moment + exact(own[theirs], scaled, TN)
        send(index, new_moments.at[theirs], outs[4], outs[5], sems.at[theirs, 2, 0])
    for copy in copies:
        copy.wait()


def finish(shard, corr, rows, stack, inverse, right, their_right, own, moment_q, moment_o):
    width, size = corr.shape[1:]
    chunks = 3
    return pl.pallas_call(
        functools.partial(finish_kernel, chunks),
        in_specs=[IN_SMEM] + [IN_VMEM] * 9,
        out_specs=[IN_HBM] * 6,
        out_shape=[pltpu.HBM((width, size), f32)] * 4 + [pltpu.HBM(moment_q.shape, f32)] * 2,
        scratch_shapes=[
            pltpu.VMEM((2, 2, width, size), f32),
            pltpu.VMEM((2,) + moment_q.shape, f32),
            pltpu.SemaphoreType.DMA((2, 3, chunks)),
        ],
        compiler_params=LARGE,
        name="finish",
    )(shard, *hold(pltpu.VMEM, corr, rows), stack, inverse, right, their_right, own, moment_q, moment_o)


def finish_plain(high, corr, base, lefts, inverse, rights, moments):
    rows, width = moments[0].shape
    start = lax.axis_index("rep") * rows
    bases = lax.all_gather(base, "rep", axis=0, tiled=True)
    decodeds = []
    for p in range(2):
        factor = rights[p][:, p * width : (p + 1) * width]
        scaled = exact(inverse[p], exact(inverse[p], factor, NN), TN)
        decodeds.append(exact(scaled, lefts[p], TN))
    ours, theirs = decodeds
    weights, new_moments, errors = [], [], []
    for p, decoded in enumerate((jnp.where(high, theirs, ours), jnp.where(high, ours, theirs))):
        weights.append(bases[:, p * width : (p + 1) * width].T - step_size * decoded)
        new_moments.append(decay_rate * moments[p] + lax.dynamic_slice_in_dim(decoded, start, rows, 1).T)
        errors.append(corr[p] - decoded)
    return weights + errors + new_moments


def per_device(n_rep, n_shard, q_grad, o_grad, q_error, o_error, q_basis, o_basis, q_moment, o_moment, q_weight, o_weight, norm_grads, norm_moment, norm_weight):
    rank = q_basis.shape[1]
    size = q_grad.shape[1]
    flat = norm_grads.shape[-1]
    row_count = q_moment.shape[0]
    place = lax.axis_index("rep").astype(jnp.int32).reshape(1)
    shard = lax.axis_index("shard").astype(jnp.int32).reshape(1)

    gather = Gather(*base_of(q_weight, q_moment, o_weight, o_moment), place, n_rep, n_shard)
    norm_moment, norm_weight = norm_moment.reshape(1, -1), norm_weight.reshape(1, -1)
    norms = (norm_grads[0], norm_moment, norm_weight)
    corr, give_corr, keep, give = first((q_grad[0].T, o_grad[0].T), (q_error[0].T, o_error[0].T), (q_basis.T, o_basis.T), norms, place, shard, n_shard)
    masks = halves(n_shard)

    def ending(left, theirs):
        gains = norm_out(left, theirs, norm_moment, place, shard, flat // LANES, n_shard)
        return (gains, *stack_of(left, theirs, place, size, row_count)) if gather.paired else (gains,)

    for sweep in range(ROUNDS):
        last = sweep == ROUNDS - 1
        if sweep == 0:
            whole, other_corr = sum_over_all(keep, give, shard, masks, n_rep, n_shard, gather, 0, give_corr)
        else:
            whole, _ = sum_over_all(keep, give, shard, masks[1:], n_rep, n_shard, gather, 2 * sweep)
        right, left, *beside = right_of(whole, shard, corr, other_corr, [norms] if last else [], gather.met(2 * sweep))
        if sweep == 0:
            (norms,) = beside
        theirs = swap(left, "shard", masks[0], n_shard)
        gather.tasks[2 * sweep + 1, 4 if last else 2] = (functools.partial(inverse_of, size=size), left, theirs)
        if last:
            gather.tasks[3, 2] = (ending, left, theirs)
        if 2 * sweep + 1 in MEETINGS:
            gather.meet(2 * sweep + 1, keep)
        right = sum_over(right, n_rep, gather, 2 * sweep + 1)
        inverse = gather.results[2 * sweep + 1, 4 if last else 2]
        if not last:
            keep, give = left_of(right, inverse, shard, masks[1], corr, other_corr, gather.met(1))
    their_right = swap(right, "shard", masks[0], n_shard)
    (norm_moment_new, norm_weight_new), *terms = gather.results[3, 2]
    if gather.paired:
        stack, own = terms
        right, turned = lax.optimization_barrier((right, gather.blocks["turned_last_b"]))
        gather.insert([turned], ["turned_last_b"])
        outs = finish(shard, corr, gather.rows, stack, inverse, right, their_right, own, q_moment, o_moment)
    else:
        outs = finish_plain((shard[0] & 1) != 0, corr, gather.blocks["own"], (left[:, :size], theirs[:, :size]), inverse, (right, their_right), (q_moment, o_moment))
    weight_q, weight_o, error_q, error_o, q_moment_new, o_moment_new = outs
    return (
        weight_q.T,
        weight_o.T,
        q_moment_new,
        o_moment_new,
        error_q.T[None],
        error_o.T[None],
        norm_weight_new.reshape(flat),
        norm_moment_new.reshape(-1),
    )


def solution(mesh):
    n_rep, n_shard = mesh.shape["rep"], mesh.shape["shard"]

    def whole(*arrays):
        return per_device(n_rep, n_shard, *arrays)

    return jax.shard_map(
        whole,
        mesh=mesh,
        in_specs=(
            P("rep", None, "shard"),
            P("rep", None, "shard"),
            P("rep", None, "shard"),
            P("rep", None, "shard"),
            P("shard", None),
            P("shard", None),
            P("rep", "shard"),
            P("rep", "shard"),
            P("rep", "shard"),
            P("rep", "shard"),
            P("rep", "shard", None),
            P(("rep", "shard")),
            P(("rep", "shard")),
        ),
        out_specs=(
            P(None, "shard"),
            P(None, "shard"),
            P("rep", "shard"),
            P("rep", "shard"),
            P("rep", None, "shard"),
            P("rep", None, "shard"),
            P(),
            P(("rep", "shard")),
        ),
        check_vma=False,
    )
```
